32 devices in a mesh: row: 2 (over y), col: 16 (over z, x, core).
Axes of the slice: x: 2, y: 2, z: 4, core: 2. Of those that a mesh axis runs over, the one named last changes fastest.
Arguments:
- phase_codes: int32 [64, 32768], P('row', 'col'), may hold values from 0 to 4095
- aperture: int32 [64, 32768], P('row', 'col'), may hold values from 0 to 1
- tile_offsets: int32 [4, 64], P('row', 'col'), may hold values from 0 to 4095
Outputs:
- psf_field: float32 [2, 64, 131072], P(None, 'row', 'col')
The draws below stay inside these ranges and needn't reach their ends.
All inputs are finite; a program needn't handle non-finite values.
Results may differ from the reference program's by a relative error of at most 0.00013.
Values sent between devices are 32-bit elements; how exact they have to be, the bound alone decides.
No kernel may reach another device: no remote copies, remote signals or barrier semaphores. Data moves between devices by JAX's collectives and lax.ppermute only.
A program may use at most 64 MiB of HBM per device.

```python
import jax
import jax.numpy as jnp

NPUP = 32768
NPAD = 131072
ROWS = 64
LEVELS = 4096
TILE_R = 16
TILE_C = 512


def draw_aperture(key, part):
    column_pos = jnp.arange(NPUP, dtype=jnp.int32)
    row_pos = jnp.arange(ROWS, dtype=jnp.int32)
    column_part = 850 * column_pos // NPUP
    threshold = 150 + row_pos[:, None] * column_part[None, :] // ROWS
    uniform_draw = jax.random.randint(key, (ROWS, NPUP), 0, 1000, dtype=jnp.int32)
    return (uniform_draw < threshold).astype(jnp.int32)


def touch_ends(drawn, key, low, high):
    longest = drawn.shape.index(max(drawn.shape))
    spots = []
    for shift in (0, 1):
        where = [jax.random.randint(jax.random.fold_in(key, axis), (), 0, length) for axis, length in enumerate(drawn.shape)]
        where[longest] = (where[longest] + shift) % drawn.shape[longest]
        spots.append(tuple(where))
    return drawn.at[spots[0]].set(low).at[spots[1]].set(high)


def setup_inputs(seed: int = 0) -> dict:
    seeds = jax.random.split(jax.random.key(seed), 4)
    phase_codes = touch_ends(jax.random.randint(seeds[0], (ROWS, NPUP), 0, LEVELS), jax.random.fold_in(seeds[0], 1), 0, LEVELS - 1).astype(jnp.int32)
    aperture = draw_aperture(jax.random.fold_in(seeds[3], 71), 0)
    tile_offsets = touch_ends(jax.random.randint(seeds[2], (ROWS // TILE_R, NPUP // TILE_C), 0, LEVELS), jax.random.fold_in(seeds[2], 1), 0, LEVELS - 1).astype(jnp.int32)
    return {"phase_codes": phase_codes, "aperture": aperture, "tile_offsets": tile_offsets}


def reference(phase_codes, aperture, tile_offsets):
    tile_rows, tile_cols = tile_offsets.shape
    piston = jnp.cumsum(tile_offsets, axis=0) % LEVELS
    codes = phase_codes.reshape(tile_rows, TILE_R, tile_cols, TILE_C) + piston[:, None, :, None]
    codes = (codes % LEVELS).reshape(ROWS, NPUP)
    theta = codes.astype(jnp.float32) * (2.0 * jnp.pi / LEVELS)
    amplitude = aperture.astype(jnp.float32)
    field = amplitude * jnp.cos(theta) + 1j * (amplitude * jnp.sin(theta))
    spectrum = jnp.fft.fft(field, n=NPAD, axis=1)
    open_count = jnp.sum(aperture)
    scale = jnp.sqrt(jnp.float32(ROWS) / open_count.astype(jnp.float32))
    psf_field = jnp.stack([jnp.real(spectrum), jnp.imag(spectrum)]) * scale
    return psf_field.astype(jnp.float32)
```

```python
import math
from functools import partial

import jax
import jax.numpy as jnp
import ml_dtypes
import numpy as np
from jax import lax
from jax.experimental import pallas as pl
from jax.experimental.pallas import tpu as pltpu
from jax.sharding import PartitionSpec as P

LEVELS = 4096
TILE_R = 16
TILE_C = 512
LANES = 128
SUBS = 8
INNER = 256
PAD = 4
GROUP = 8


class Plan:
    def __init__(self, row_dev, pupil_dev, n_col, n_row):
        self.row_dev = row_dev
        self.pupil_dev = pupil_dev
        self.n_col = n_col
        self.n_row = n_row
        self.rows_all = row_dev * n_row
        self.group = min(GROUP, n_col)
        self.n_groups = n_col // self.group
        self.rows = row_dev // self.group
        self.n_pupil = pupil_dev * n_col
        self.n_pad = PAD * self.n_pupil
        self.n1 = self.n_pupil // INNER
        self.k1 = PAD * self.n1
        self.n1_dev = pupil_dev // INNER
        self.k2_group = INNER // self.n_groups
        self.k2_dev = INNER // n_col
        self.freq_tiles = PAD * pupil_dev // LANES
        self.k1_tiles = self.k1 // LANES
        self.lane_parts = INNER // LANES
        self.chunk = self.rows * 2 * self.lane_parts * self.n1_dev


def split_bf16(table):
    high = table.astype(ml_dtypes.bfloat16)
    low = (table - high.astype(np.float64)).astype(ml_dtypes.bfloat16)
    return high, low


def outer_tables(plan):
    angle = np.arange(plan.n1)[:, None] * np.arange(plan.k1)[None, :] % plan.k1
    angle = angle * (2.0 * np.pi / plan.k1)
    cos, sin = np.cos(angle), np.sin(angle)
    return split_bf16(np.block([[cos, -sin], [sin, cos]]))


def inner_tables(plan):
    angle = np.arange(INNER)[:, None] * np.arange(INNER)[None, :] % INNER
    angle = angle * (2.0 * np.pi / INNER)
    cos, sin = np.cos(angle), np.sin(angle)
    by_group = []
    for g in range(plan.n_groups):
        part = slice(g * plan.k2_group, (g + 1) * plan.k2_group)
        by_group.append(np.block([[cos[part], sin[part]], [-sin[part], cos[part]]]))
    return split_bf16(np.stack(by_group))


def twist_tables(plan):
    angle = np.arange(INNER)[:, None] * np.arange(plan.k1)[None, :] * (2.0 * np.pi / plan.n_pad)
    return np.cos(angle).astype(np.float32), np.sin(angle).astype(np.float32)


def field_kernel(plan, piston_ref, count_ref, codes_ref, mask_ref, out_ref):
    for t in range(plan.row_dev // SUBS):
        for j in range(plan.pupil_dev // LANES):
            rows = slice(t * SUBS, (t + 1) * SUBS)
            lanes = slice(j * LANES, (j + 1) * LANES)
            piston = piston_ref[t * SUBS // TILE_R, j * LANES // TILE_C]
            code = (codes_ref[rows, lanes] + piston) & (LEVELS - 1)
            quadrant = (code + LEVELS // 8) >> 10
            rest = (code - (quadrant << 10)).astype(jnp.float32) * (2.0 * math.pi / LEVELS)
            sq = rest * rest
            cos = 1.0 + sq * (-1.0 / 2 + sq * (1.0 / 24 + sq * (-1.0 / 720 + sq * (1.0 / 40320))))
            sin = rest * (1.0 + sq * (-1.0 / 6 + sq * (1.0 / 120 + sq * (-1.0 / 5040 + sq * (1.0 / 362880)))))
            amplitude = mask_ref[rows, lanes].astype(jnp.float32)
            swap = (quadrant & 1) == 1
            real = jnp.where(swap, sin, cos) * jnp.where(((quadrant + 1) & 2) == 2, -amplitude, amplitude)
            imag = jnp.where(swap, cos, sin) * jnp.where((quadrant & 2) == 2, -amplitude, amplitude)
            for part, value in enumerate((real, imag)):
                start = (part * plan.lane_parts + j % plan.lane_parts) * plan.n1_dev + j // plan.lane_parts
                step = 2 * plan.lane_parts * plan.n1_dev
                take = min(plan.rows, SUBS)
                for d in range(SUBS // take):
                    row = t * SUBS + d * take
                    dest, first = row // plan.rows, row % plan.rows
                    for g in range(plan.n_groups):
                        out_ref[g * plan.group + dest, pl.ds(first * step + start, take, stride=step), :] = value[
                            d * take : (d + 1) * take
                        ]
    count = count_ref[0, 0].astype(jnp.float32)
    for dest in range(plan.n_col):
        out_ref[dest, plan.chunk :, :] = jnp.full((SUBS, LANES), count, jnp.float32)


def transform_kernel(plan, group_ref, x_ref, tail_ref, w1h_ref, w1l_ref, tc_ref, ts_ref, w2h_ref, w2l_ref, out_ref):
    del group_ref
    r = pl.program_id(0)
    halves = []
    for part in range(2):
        pieces = []
        for lt in range(plan.lane_parts):
            at = (part * plan.lane_parts + lt) * plan.n1_dev
            pieces.append(x_ref[:, at : at + plan.n1_dev, :].reshape(plan.n1, LANES))
        halves.append(jnp.concatenate(pieces, axis=1))
    x = jnp.concatenate(halves, axis=0)
    xh = x.astype(jnp.bfloat16)
    xl = (x - xh.astype(jnp.float32)).astype(jnp.bfloat16)

    def outer(a, b):
        return lax.dot_general(a, b, (((0,), (0,)), ((), ())), preferred_element_type=jnp.float32)

    y = outer(xh, w1h_ref[...]) + outer(xl, w1h_ref[...]) + outer(xh, w1l_ref[...])
    yr, yi = y[:, : plan.k1], y[:, plan.k1 :]
    tc, ts = tc_ref[...], ts_ref[...]
    b = jnp.concatenate([yr * tc + yi * ts, yi * tc - yr * ts], axis=0)
    bh = b.astype(jnp.bfloat16)
    bl = (b - bh.astype(jnp.float32)).astype(jnp.bfloat16)

    def inner(a, b):
        return jnp.dot(a, b, preferred_element_type=jnp.float32)

    z = inner(w2h_ref[0], bh) + inner(w2l_ref[0], bh) + inner(w2h_ref[0], bl)
    count = jnp.sum(tail_ref[:, 0, :], axis=0, keepdims=True)
    scale = jnp.sqrt(float(plan.rows_all) / count)
    take = min(plan.k2_dev, SUBS)
    step = plan.k1_tiles * plan.rows
    for part in range(2):
        for k2 in range(0, plan.k2_group, take):
            dest, k2_in = k2 // plan.k2_dev, k2 % plan.k2_dev
            for j in range(plan.k1_tiles):
                at = (part * plan.freq_tiles + k2_in * plan.k1_tiles + j) * plan.rows
                row = part * plan.k2_group + k2
                value = z[row : row + take, j * LANES : (j + 1) * LANES] * scale
                out_ref[dest, pl.ds(at + r, take, stride=step), :] = value


def merge_kernel(plan, in_ref, out_ref):
    per = SUBS // plan.rows
    for f in range(plan.freq_tiles):
        for d in range(per):
            out_ref[0, d * plan.rows : (d + 1) * plan.rows, f * LANES : (f + 1) * LANES] = in_ref[
                d, f * plan.rows : (f + 1) * plan.rows, :
            ]


def per_device(phase_codes, aperture, tile_offsets):
    n_col = lax.axis_size("col")
    n_row = lax.axis_size("row")
    row_index = lax.axis_index("row")
    plan = Plan(*phase_codes.shape, n_col, n_row)
    tile_rows, tile_cols = tile_offsets.shape

    running = [tile_offsets[0]]
    for i in range(1, tile_rows):
        running.append(running[-1] + tile_offsets[i])
    count = jnp.sum(aperture)
    info = jnp.concatenate([running[-1], count[None]])[None, :]
    before = jnp.zeros((tile_cols,), jnp.int32)
    for d in range(1, n_row):
        other = lax.ppermute(info, "row", [(i, (i + d) % n_row) for i in range(n_row)])
        before = before + jnp.where(row_index >= d, other[0, :tile_cols], 0)
        count = count + other[0, tile_cols]
    piston = jnp.stack(running) + before[None, :]

    smem = pl.BlockSpec(memory_space=pltpu.SMEM)
    vmem = pl.BlockSpec(memory_space=pltpu.VMEM)
    packed = pl.pallas_call(
        partial(field_kernel, plan),
        out_shape=jax.ShapeDtypeStruct((n_col, plan.chunk + SUBS, LANES), jnp.float32),
        in_specs=[smem, smem, vmem, vmem],
        out_specs=vmem,
        compiler_params=pltpu.CompilerParams(vmem_limit_bytes=40 * 2**20),
        name="field",
    )(piston, count.reshape(1, 1), phase_codes, aperture)
    received = lax.all_to_all(packed, "col", split_axis=0, concat_axis=0, tiled=True)

    w1h, w1l = outer_tables(plan)
    w2h, w2l = inner_tables(plan)
    tc, ts = twist_tables(plan)
    group = (lax.axis_index("col") // plan.group).reshape(1).astype(jnp.int32)
    chunk_row = plan.chunk // plan.rows
    whole = lambda a: pl.BlockSpec(a.shape, lambda r, g: (0,) * a.ndim)
    mine = lambda a: pl.BlockSpec((1,) + a.shape[1:], lambda r, g: (g[0], 0, 0))
    out_rows = 2 * plan.freq_tiles * plan.rows
    spectrum = pl.pallas_call(
        partial(transform_kernel, plan),
        out_shape=jax.ShapeDtypeStruct((plan.group, out_rows, LANES), jnp.float32),
        grid_spec=pltpu.PrefetchScalarGridSpec(
            num_scalar_prefetch=1,
            grid=(plan.rows,),
            in_specs=[
                pl.BlockSpec((n_col, chunk_row, LANES), lambda r, g: (0, r, 0)),
                pl.BlockSpec((n_col, SUBS, LANES), lambda r, g: (0, plan.chunk // SUBS, 0)),
                whole(w1h),
                whole(w1l),
                whole(tc),
                whole(ts),
                mine(w2h),
                mine(w2l),
            ],
            out_specs=pl.BlockSpec((plan.group, out_rows, LANES), lambda r, g: (0, 0, 0)),
        ),
        compiler_params=pltpu.CompilerParams(vmem_limit_bytes=48 * 2**20),
        name="transform",
    )(group, received, received, w1h, w1l, tc, ts, w2h, w2l)

    groups = [[g * plan.group + i for i in range(plan.group)] for g in range(plan.n_groups)]
    blocks = lax.all_to_all(
        spectrum, "col", split_axis=0, concat_axis=0, tiled=True, axis_index_groups=groups
    )
    per = SUBS // plan.rows
    half = plan.freq_tiles * plan.rows
    return pl.pallas_call(
        partial(merge_kernel, plan),
        out_shape=jax.ShapeDtypeStruct((2, plan.row_dev, plan.freq_tiles * LANES), jnp.float32),
        grid=(2, plan.row_dev // SUBS),
        in_specs=[pl.BlockSpec((per, half, LANES), lambda c, t: (t, c, 0))],
        out_specs=pl.BlockSpec((1, SUBS, plan.freq_tiles * LANES), lambda c, t: (c, t, 0)),
        name="merge",
    )(blocks)


def solution(mesh):
    placed = (P("row", "col"), P("row", "col"), P("row", "col"))
    return jax.shard_map(
        per_device, mesh=mesh, in_specs=placed, out_specs=P(None, "row", "col"), check_vma=False
    )
```

```python
import math
from functools import partial

import jax
import jax.numpy as jnp
import ml_dtypes
import numpy as np
from jax import lax
from jax.experimental import pallas as pl
from jax.experimental.pallas import tpu as pltpu
from jax.sharding import PartitionSpec as P

LEVELS = 4096
TILE_R = 16
TILE_C = 512
LANES = 128
SUBS = 8
INNER = 256
PAD = 4
SPLITS = (2, 2)
GROUP = 8


class Plan:
    def __init__(self, row_dev, pupil_dev, n_col, n_row):
        self.row_dev = row_dev
        self.pupil_dev = pupil_dev
        self.n_col = n_col
        self.n_row = n_row
        self.rows_all = row_dev * n_row
        self.group = min(GROUP, n_col)
        self.n_groups = n_col // self.group
        self.rows = row_dev // self.group
        self.n_pupil = pupil_dev * n_col
        self.n_pad = PAD * self.n_pupil
        self.n1 = self.n_pupil // INNER
        self.k1 = PAD * self.n1
        self.n1_dev = pupil_dev // INNER
        self.k2_group = INNER // self.n_groups
        self.k2_dev = INNER // n_col
        self.freq_tiles = PAD * pupil_dev // LANES
        self.k1_tiles = self.k1 // LANES
        self.lane_parts = INNER // LANES
        self.chunk = self.rows * 2 * self.lane_parts * self.n1_dev


def split_bf16(table):
    high = table.astype(ml_dtypes.bfloat16)
    low = (table - high.astype(np.float64)).astype(ml_dtypes.bfloat16)
    return np.stack([high, low])


def outer_tables(plan):
    angle = np.arange(plan.n1)[:, None] * np.arange(plan.k1)[None, :] % plan.k1
    angle = angle * (2.0 * np.pi / plan.k1)
    cos, sin = np.cos(angle), np.sin(angle)
    return split_bf16(np.block([[cos, -sin], [sin, cos]]))


def inner_tables(plan):
    angle = np.arange(INNER)[:, None] * np.arange(INNER)[None, :] % INNER
    angle = angle * (2.0 * np.pi / INNER)
    cos, sin = np.cos(angle), np.sin(angle)
    by_dest = []
    for q in range(plan.n_col):
        part = slice(q * plan.k2_dev, (q + 1) * plan.k2_dev)
        by_dest.append(np.block([[cos[part], sin[part]], [-sin[part], cos[part]]]))
    return split_bf16(np.stack(by_dest))


def twist_tables(plan):
    angle = np.arange(INNER)[:, None] * np.arange(plan.k1)[None, :] * (2.0 * np.pi / plan.n_pad)
    return np.stack([np.cos(angle), np.sin(angle)]).astype(np.float32)


def field_kernel(plan, row_ref, tiles_ref, *refs):
    others, (codes_ref, mask_ref, all_mask_ref, out_ref, open_ref) = refs[: plan.n_row - 1], refs[plan.n_row - 1 :]
    step_id = pl.program_id(0)
    tile_cols = plan.pupil_dev // TILE_C

    @pl.when(step_id == 0)
    def _():
        total = jnp.zeros((SUBS, LANES), jnp.int32)
        for t in range(plan.row_dev // SUBS):
            for j in range(plan.pupil_dev // LANES):
                total = total + all_mask_ref[t * SUBS : (t + 1) * SUBS, j * LANES : (j + 1) * LANES]
        open_ref[...] = total.astype(jnp.float32)

    pistons = []
    for i in range(tile_cols):
        piston = jnp.int32(0)
        for d, other in enumerate(others):
            column = other[0, i]
            for k in range(1, plan.row_dev // TILE_R):
                column = column + other[k, i]
            piston = piston + jnp.where(row_ref[0] > d, column, 0)
        for k in range(plan.row_dev // TILE_R):
            piston = piston + jnp.where(step_id >= k, tiles_ref[k, i], 0)
        pistons.append(piston)
    take = min(plan.rows, SUBS)
    stride = 2 * plan.lane_parts * plan.n1_dev
    for t in range(TILE_R // SUBS):
        for j in range(plan.pupil_dev // LANES):
            rows = slice(t * SUBS, (t + 1) * SUBS)
            lanes = slice(j * LANES, (j + 1) * LANES)
            code = (codes_ref[rows, lanes] + pistons[j * LANES // TILE_C]) & (LEVELS - 1)
            quadrant = (code + LEVELS // 8) >> 10
            rest = (code - (quadrant << 10)).astype(jnp.float32) * (2.0 * math.pi / LEVELS)
            sq = rest * rest
            cos = 1.0 + sq * (-1.0 / 2 + sq * (1.0 / 24 + sq * (-1.0 / 720 + sq * (1.0 / 40320))))
            sin = rest * (1.0 + sq * (-1.0 / 6 + sq * (1.0 / 120 + sq * (-1.0 / 5040 + sq * (1.0 / 362880)))))
            amplitude = mask_ref[rows, lanes].astype(jnp.float32)
            swap = (quadrant & 1) == 1
            real = jnp.where(swap, sin, cos) * jnp.where(((quadrant + 1) & 2) == 2, -amplitude, amplitude)
            imag = jnp.where(swap, cos, sin) * jnp.where((quadrant & 2) == 2, -amplitude, amplitude)
            for part, value in enumerate((real, imag)):
                start = (part * plan.lane_parts + j % plan.lane_parts) * plan.n1_dev + j // plan.lane_parts
                for d in range(SUBS // take):
                    row = t * SUBS + d * take
                    dest, first = row // plan.rows, row % plan.rows
                    for g in range(plan.n_groups):
                        out_ref[g, dest, pl.ds(first * stride + start, take, stride=stride), :] = value[
                            d * take : (d + 1) * take
                        ]
    for g in range(plan.n_groups):
        for dest in range(TILE_R // plan.rows):
            out_ref[g, dest, plan.chunk :, :] = open_ref[...]


def transform_kernel(plan, first, rows, with_count, me_ref, x_ref, w1_ref, twist_ref, w2_ref, *refs):
    chunk_row = plan.chunk // plan.rows
    me = me_ref[0]

    def outer(a, b):
        return lax.dot_general(a, b, (((0,), (0,)), ((), ())), preferred_element_type=jnp.float32)

    def inner(a, b):
        return jnp.dot(a, b, preferred_element_type=jnp.float32)

    if with_count:
        refs[plan.group][...] = jnp.sum(x_ref[:, plan.chunk :, :], axis=0)
    w2 = [jnp.concatenate([w2_ref[s, me ^ b] for b in range(plan.group)], axis=0) for s in range(2)]
    tc, ts = twist_ref[0], twist_ref[1]
    for r in range(rows):
        halves = []
        for part in range(2):
            pieces = []
            for lt in range(plan.lane_parts):
                at = (first + r) * chunk_row + (part * plan.lane_parts + lt) * plan.n1_dev
                pieces.append(x_ref[:, at : at + plan.n1_dev, :].reshape(plan.n1, LANES))
            halves.append(jnp.concatenate(pieces, axis=1))
        x = jnp.concatenate(halves, axis=0)
        xh = x.astype(jnp.bfloat16)
        xl = (x - xh.astype(jnp.float32)).astype(jnp.bfloat16)
        y = outer(xh, w1_ref[0]) + outer(xl, w1_ref[0]) + outer(xh, w1_ref[1])
        yr, yi = y[:, : plan.k1], y[:, plan.k1 :]
        f = jnp.concatenate([yr * tc + yi * ts, yi * tc - yr * ts], axis=0)
        fh = f.astype(jnp.bfloat16)
        fl = (f - fh.astype(jnp.float32)).astype(jnp.bfloat16)
        z = inner(w2[0], fh) + inner(w2[1], fh) + inner(w2[0], fl)
        size = 2 * plan.k2_dev
        for b in range(plan.group):
            refs[b][r] = z[b * size : (b + 1) * size].reshape(2, plan.k2_dev, plan.k1)


def merge_kernel(plan, splits, at_ref, *refs):
    del at_ref
    n = len(splits)
    even, odd, parity_ref, counts = refs[:n], refs[n : 2 * n], refs[2 * n], refs[2 * n + 1 : 2 * n + 1 + plan.n_row]
    out_ref, tile_ref = refs[-2], refs[-1]
    total = counts[0][...]
    for other in counts[1:]:
        total = total + other[...]
    total = jnp.sum(jnp.sum(total, axis=0, keepdims=True), axis=1, keepdims=True)
    scale = jnp.sqrt(float(plan.rows_all) / total)
    swapped = parity_ref[0] == 1
    take = min(plan.k2_dev, SUBS)
    for i, rows in enumerate(splits):
        for r in range(rows):
            for k2 in range(0, plan.k2_dev, take):
                for j in range(plan.k1_tiles):
                    lanes = slice(j * LANES, (j + 1) * LANES)
                    a = even[i][r, 0, k2 : k2 + take, lanes] * scale
                    b = odd[i][r, 0, k2 : k2 + take, lanes] * scale
                    at = (k2 * plan.k1_tiles + j) * SUBS + sum(splits[:i]) + r
                    stride = plan.k1_tiles * SUBS
                    tile_ref[pl.ds(at, take, stride=stride), :] = jnp.where(swapped, b, a)
                    tile_ref[pl.ds(at + plan.rows, take, stride=stride), :] = jnp.where(swapped, a, b)
    for f in range(plan.freq_tiles):
        out_ref[0, :, f * LANES : (f + 1) * LANES] = tile_ref[f * SUBS : (f + 1) * SUBS, :]


def per_device(phase_codes, aperture, tile_offsets):
    n_col = lax.axis_size("col")
    n_row = lax.axis_size("row")
    plan = Plan(*phase_codes.shape, n_col, n_row)
    row_index = lax.axis_index("row").astype(jnp.int32).reshape(1)
    col_index = lax.axis_index("col").astype(jnp.int32).reshape(1)
    me = col_index

    def along_rows(value):
        return [lax.ppermute(value, "row", [(i, (i + d) % n_row) for i in range(n_row)]) for d in range(1, n_row)]

    smem = pl.BlockSpec(memory_space=pltpu.SMEM)
    vmem = pl.BlockSpec(memory_space=pltpu.VMEM)
    others = along_rows(tile_offsets)
    steps = plan.row_dev // TILE_R
    block = (plan.n_groups, plan.group // steps, plan.chunk + SUBS, LANES)
    packed = pl.pallas_call(
        partial(field_kernel, plan),
        out_shape=jax.ShapeDtypeStruct((plan.n_groups, plan.group, plan.chunk + SUBS, LANES), jnp.float32),
        grid=(steps,),
        in_specs=[smem, smem]
        + [smem] * (n_row - 1)
        + [
            pl.BlockSpec((TILE_R, plan.pupil_dev), lambda t: (t, 0)),
            pl.BlockSpec((TILE_R, plan.pupil_dev), lambda t: (t, 0)),
            pl.BlockSpec((plan.row_dev, plan.pupil_dev), lambda t: (0, 0)),
        ],
        out_specs=pl.BlockSpec(block, lambda t: (0, t, 0, 0)),
        scratch_shapes=[pltpu.VMEM((SUBS, LANES), jnp.float32)],
        name="field",
    )(row_index, tile_offsets, *others, phase_codes, aperture, aperture)
    packed = packed.reshape(n_col, plan.chunk + SUBS, LANES)
    received = lax.all_to_all(packed, "col", split_axis=0, concat_axis=0, tiled=True)

    w1, w2, twist = outer_tables(plan), inner_tables(plan), twist_tables(plan)
    splits = SPLITS if sum(SPLITS) == plan.rows else (plan.rows,)
    chunks = []
    for i, rows in enumerate(splits):
        shapes = [jax.ShapeDtypeStruct((rows, 2, plan.k2_dev, plan.k1), jnp.float32)] * plan.group
        if i == 0:
            shapes = shapes + [jax.ShapeDtypeStruct((SUBS, LANES), jnp.float32)]
        made = pl.pallas_call(
            partial(transform_kernel, plan, sum(splits[:i]), rows, i == 0),
            out_shape=shapes,
            in_specs=[smem, vmem, vmem, vmem, vmem],
            out_specs=[vmem] * len(shapes),
            compiler_params=pltpu.CompilerParams(vmem_limit_bytes=24 * 2**20),
            name="transform",
        )(me, received, w1, twist, w2)
        if i == 0:
            counts = [made[-1]] + along_rows(made[-1])
        chunks.append(
            [made[0]]
            + [lax.ppermute(made[b], "col", [(q, q ^ b) for q in range(n_col)]) for b in range(1, plan.group)]
        )

    inside = col_index % plan.group
    parity = inside % 2
    out = None
    for b in range(plan.group - 2, -1, -2):
        tile = (inside // 2) ^ (b // 2)
        pair = [c[b] for c in chunks] + [c[b + 1] for c in chunks]
        in_specs = [pl.BlockSpec((rows, 1, plan.k2_dev, plan.k1), lambda c, t: (0, c, 0, 0)) for rows in splits] * 2
        in_specs = in_specs + [smem] + [pl.BlockSpec((SUBS, LANES), lambda c, t: (0, 0))] * n_row
        args = [tile, *pair, parity, *counts]
        aliases = {}
        kernel = partial(merge_kernel, plan, splits)
        if out is not None:
            in_specs = in_specs + [pl.BlockSpec(memory_space=pl.ANY)]
            args = args + [out]
            aliases = {len(args) - 1: 0}
        out = pl.pallas_call(
            kernel,
            out_shape=jax.ShapeDtypeStruct((2, plan.row_dev, plan.freq_tiles * LANES), jnp.float32),
            grid_spec=pltpu.PrefetchScalarGridSpec(
                num_scalar_prefetch=1,
                grid=(2,),
                in_specs=in_specs,
                out_specs=pl.BlockSpec((1, SUBS, plan.freq_tiles * LANES), lambda c, t: (c, t[0], 0)),
                scratch_shapes=[pltpu.VMEM((plan.freq_tiles * SUBS, LANES), jnp.float32)],
            ),
            input_output_aliases=aliases,
            name="merge",
        )(*args)
    return out


def solution(mesh):
    placed = (P("row", "col"), P("row", "col"), P("row", "col"))
    return jax.shard_map(
        per_device, mesh=mesh, in_specs=placed, out_specs=P(None, "row", "col"), check_vma=False
    )
```

```python
import math
from functools import partial

import jax
import jax.numpy as jnp
import ml_dtypes
import numpy as np
from jax import lax
from jax.experimental import pallas as pl
from jax.experimental.pallas import tpu as pltpu
from jax.sharding import PartitionSpec as P

LEVELS = 4096
TILE_R = 16
TILE_C = 512
LANES = 128
SUBS = 8
INNER = 256
PAD = 4
SPLITS = (2, 2)
GROUP = 8


class Plan:
    def __init__(self, row_dev, pupil_dev, n_col, n_row):
        self.row_dev = row_dev
        self.pupil_dev = pupil_dev
        self.n_col = n_col
        self.n_row = n_row
        self.rows_all = row_dev * n_row
        self.group = min(GROUP, n_col)
        self.n_groups = n_col // self.group
        self.rows = row_dev // self.group
        self.n_pupil = pupil_dev * n_col
        self.n_pad = PAD * self.n_pupil
        self.n1 = self.n_pupil // INNER
        self.k1 = PAD * self.n1
        self.n1_dev = pupil_dev // INNER
        self.k2_group = INNER // self.n_groups
        self.k2_dev = INNER // n_col
        self.freq_tiles = PAD * pupil_dev // LANES
        self.k1_tiles = self.k1 // LANES
        self.lane_parts = INNER // LANES
        self.chunk = self.rows * 2 * self.lane_parts * self.n1_dev


def split_bf16(table):
    high = table.astype(ml_dtypes.bfloat16)
    low = (table - high.astype(np.float64)).astype(ml_dtypes.bfloat16)
    return np.stack([high, low])


def matmul_tables(plan):
    angle = np.arange(plan.n1)[:, None] * np.arange(plan.k1)[None, :] % plan.k1
    angle = angle * (2.0 * np.pi / plan.k1)
    cos, sin = np.cos(angle), np.sin(angle)
    parts = [cos, sin, -sin, cos]
    angle = np.arange(INNER)[:, None] * np.arange(INNER)[None, :] % INNER
    angle = angle * (2.0 * np.pi / INNER)
    cos, sin = np.cos(angle), np.sin(angle)
    for q in range(plan.n_col):
        part = slice(q * plan.k2_dev, (q + 1) * plan.k2_dev)
        parts.append(np.block([[cos[part], sin[part]], [-sin[part], cos[part]]]))
    return split_bf16(np.concatenate(parts))


def twist_tables(plan):
    angle = np.arange(INNER)[:, None] * np.arange(plan.k1)[None, :] * (2.0 * np.pi / plan.n_pad)
    return np.stack([np.cos(angle), np.sin(angle)]).astype(np.float32)


def field_kernel(plan, row_ref, tiles_ref, *refs):
    others, (codes_ref, mask_ref, all_mask_ref, out_ref, open_ref) = refs[: plan.n_row - 1], refs[plan.n_row - 1 :]
    step_id = pl.program_id(0)
    tile_cols = plan.pupil_dev // TILE_C

    @pl.when(step_id == 0)
    def _():
        total = jnp.zeros((SUBS, LANES), jnp.int32)
        for t in range(plan.row_dev // SUBS):
            for j in range(plan.pupil_dev // LANES):
                total = total + all_mask_ref[t * SUBS : (t + 1) * SUBS, j * LANES : (j + 1) * LANES]
        open_ref[...] = total.astype(jnp.float32)

    pistons = []
    for i in range(tile_cols):
        piston = jnp.int32(0)
        for d, other in enumerate(others):
            column = other[0, i]
            for k in range(1, plan.row_dev // TILE_R):
                column = column + other[k, i]
            piston = piston + jnp.where(row_ref[0] > d, column, 0)
        for k in range(plan.row_dev // TILE_R):
            piston = piston + jnp.where(step_id >= k, tiles_ref[k, i], 0)
        pistons.append(piston)
    take = min(plan.rows, SUBS)
    stride = 2 * plan.lane_parts * plan.n1_dev
    for t in range(TILE_R // SUBS):
        for j in range(plan.pupil_dev // LANES):
            rows = slice(t * SUBS, (t + 1) * SUBS)
            lanes = slice(j * LANES, (j + 1) * LANES)
            code = (codes_ref[rows, lanes] + pistons[j * LANES // TILE_C]) & (LEVELS - 1)
            quadrant = (code + LEVELS // 8) >> 10
            rest = (code - (quadrant << 10)).astype(jnp.float32) * (2.0 * math.pi / LEVELS)
            sq = rest * rest
            cos = 1.0 + sq * (-1.0 / 2 + sq * (1.0 / 24 + sq * (-1.0 / 720 + sq * (1.0 / 40320))))
            sin = rest * (1.0 + sq * (-1.0 / 6 + sq * (1.0 / 120 + sq * (-1.0 / 5040 + sq * (1.0 / 362880)))))
            amplitude = mask_ref[rows, lanes].astype(jnp.float32)
            swap = (quadrant & 1) == 1
            real = jnp.where(swap, sin, cos) * jnp.where(((quadrant + 1) & 2) == 2, -amplitude, amplitude)
            imag = jnp.where(swap, cos, sin) * jnp.where((quadrant & 2) == 2, -amplitude, amplitude)
            for part, value in enumerate((real, imag)):
                start = (part * plan.lane_parts + j % plan.lane_parts) * plan.n1_dev + j // plan.lane_parts
                for d in range(SUBS // take):
                    row = t * SUBS + d * take
                    dest, first = row // plan.rows, row % plan.rows
                    for g in range(plan.n_groups):
                        out_ref[g, dest, pl.ds(first * stride + start, take, stride=stride), :] = value[
                            d * take : (d + 1) * take
                        ]
    for g in range(plan.n_groups):
        for dest in range(TILE_R // plan.rows):
            out_ref[g, dest, plan.chunk :, :] = open_ref[...]


def transform_kernel(plan, first, rows, with_count, me_ref, x_ref, table_ref, twist_ref, *refs):
    chunk_row = plan.chunk // plan.rows
    me = me_ref[0]

    def outer(a, b):
        return lax.dot_general(a, b, (((0,), (0,)), ((), ())), preferred_element_type=jnp.float32)

    def inner(a, b):
        return jnp.dot(a, b, preferred_element_type=jnp.float32)

    if with_count:
        refs[plan.group][...] = jnp.sum(x_ref[:, plan.chunk :, :], axis=0)
    side = 2 * plan.n1
    size = 2 * plan.k2_dev
    w1 = [jnp.concatenate([table_ref[s, :side], table_ref[s, side : 2 * side]], axis=1) for s in range(2)]
    w2 = []
    for s in range(2):
        starts = [pl.multiple_of(2 * side + (me ^ b) * size, size) for b in range(plan.group)]
        w2.append(jnp.concatenate([table_ref[s, pl.ds(start, size)] for start in starts], axis=0))
    tc, ts = twist_ref[0], twist_ref[1]
    for r in range(rows):
        halves = []
        for part in range(2):
            pieces = []
            for lt in range(plan.lane_parts):
                at = (first + r) * chunk_row + (part * plan.lane_parts + lt) * plan.n1_dev
                pieces.append(x_ref[:, at : at + plan.n1_dev, :].reshape(plan.n1, LANES))
            halves.append(jnp.concatenate(pieces, axis=1))
        x = jnp.concatenate(halves, axis=0)
        xh = x.astype(jnp.bfloat16)
        xl = (x - xh.astype(jnp.float32)).astype(jnp.bfloat16)
        y = outer(xh, w1[0]) + outer(xl, w1[0]) + outer(xh, w1[1])
        yr, yi = y[:, : plan.k1], y[:, plan.k1 :]
        f = jnp.concatenate([yr * tc + yi * ts, yi * tc - yr * ts], axis=0)
        fh = f.astype(jnp.bfloat16)
        fl = (f - fh.astype(jnp.float32)).astype(jnp.bfloat16)
        z = inner(w2[0], fh) + inner(w2[1], fh) + inner(w2[0], fl)
        for b in range(plan.group):
            refs[b][r] = z[b * size : (b + 1) * size].reshape(2, plan.k2_dev, plan.k1)


def merge_kernel(plan, splits, me_ref, *refs):
    n = len(splits)
    chunks = [refs[i * plan.group : (i + 1) * plan.group] for i in range(n)]
    counts = refs[n * plan.group : n * plan.group + plan.n_row]
    out_ref, tile_ref, row_ref, sems = refs[n * plan.group + plan.n_row :]
    total = counts[0][...]
    for other in counts[1:]:
        total = total + other[...]
    total = jnp.sum(jnp.sum(total, axis=0, keepdims=True), axis=1, keepdims=True)
    scale = jnp.sqrt(float(plan.rows_all) / total)
    inside = lax.rem(me_ref[0], plan.group)
    swapped = lax.rem(inside, 2) == 1
    take = min(plan.k2_dev, SUBS)
    stride = plan.k1_tiles * SUBS
    copies = []
    for pair in range(plan.group // 2):
        for part in range(2):
            slot = pair * 2 + part
            for i, rows in enumerate(splits):
                for r in range(rows):
                    for k2 in range(0, plan.k2_dev, take):
                        for j in range(plan.k1_tiles):
                            lanes = slice(j * LANES, (j + 1) * LANES)
                            a = chunks[i][2 * pair][r, part, k2 : k2 + take, lanes] * scale
                            b = chunks[i][2 * pair + 1][r, part, k2 : k2 + take, lanes] * scale
                            at = (k2 * plan.k1_tiles + j) * SUBS + sum(splits[:i]) + r
                            tile_ref[slot, pl.ds(at, take, stride=stride), :] = jnp.where(swapped, b, a)
                            tile_ref[slot, pl.ds(at + plan.rows, take, stride=stride), :] = jnp.where(swapped, a, b)
            for f in range(plan.freq_tiles):
                row_ref[slot, :, f * LANES : (f + 1) * LANES] = tile_ref[slot, f * SUBS : (f + 1) * SUBS, :]
            tile = lax.div(inside, 2) ^ pair
            target = out_ref.at[part, pl.ds(pl.multiple_of(tile * SUBS, SUBS), SUBS), :]
            copy = pltpu.make_async_copy(row_ref.at[slot], target, sems.at[slot])
            copy.start()
            copies.append(copy)
    for copy in copies:
        copy.wait()


def per_device(phase_codes, aperture, tile_offsets):
    n_col = lax.axis_size("col")
    n_row = lax.axis_size("row")
    plan = Plan(*phase_codes.shape, n_col, n_row)
    row_index = lax.axis_index("row").astype(jnp.int32).reshape(1)
    col_index = lax.axis_index("col").astype(jnp.int32).reshape(1)
    me = col_index

    def along_rows(value):
        return [lax.ppermute(value, "row", [(i, (i + d) % n_row) for i in range(n_row)]) for d in range(1, n_row)]

    smem = pl.BlockSpec(memory_space=pltpu.SMEM)
    vmem = pl.BlockSpec(memory_space=pltpu.VMEM)
    others = along_rows(tile_offsets)
    steps = plan.row_dev // TILE_R
    block = (plan.n_groups, plan.group // steps, plan.chunk + SUBS, LANES)
    packed = pl.pallas_call(
        partial(field_kernel, plan),
        out_shape=jax.ShapeDtypeStruct((plan.n_groups, plan.group, plan.chunk + SUBS, LANES), jnp.float32),
        grid=(steps,),
        in_specs=[smem, smem]
        + [smem] * (n_row - 1)
        + [
            pl.BlockSpec((TILE_R, plan.pupil_dev), lambda t: (t, 0)),
            pl.BlockSpec((TILE_R, plan.pupil_dev), lambda t: (t, 0)),
            pl.BlockSpec((plan.row_dev, plan.pupil_dev), lambda t: (0, 0)),
        ],
        out_specs=pl.BlockSpec(block, lambda t: (0, t, 0, 0)),
        scratch_shapes=[pltpu.VMEM((SUBS, LANES), jnp.float32)],
        name="field",
    )(row_index, tile_offsets, *others, phase_codes, aperture, aperture)
    packed = packed.reshape(n_col, plan.chunk + SUBS, LANES)
    received = lax.all_to_all(packed, "col", split_axis=0, concat_axis=0, tiled=True)

    table, twist = matmul_tables(plan), twist_tables(plan)
    splits = SPLITS if sum(SPLITS) == plan.rows else (plan.rows,)
    chunks = []
    for i, rows in enumerate(splits):
        shapes = [jax.ShapeDtypeStruct((rows, 2, plan.k2_dev, plan.k1), jnp.float32)] * plan.group
        if i == 0:
            shapes = shapes + [jax.ShapeDtypeStruct((SUBS, LANES), jnp.float32)]
        made = pl.pallas_call(
            partial(transform_kernel, plan, sum(splits[:i]), rows, i == 0),
            out_shape=shapes,
            in_specs=[smem, vmem, vmem, vmem],
            out_specs=[vmem] * len(shapes),
            compiler_params=pltpu.CompilerParams(vmem_limit_bytes=24 * 2**20),
            name="transform",
        )(me, received, table, twist)
        if i == 0:
            counts = [made[-1]] + along_rows(made[-1])
        chunks.append(
            [made[0]]
            + [lax.ppermute(made[b], "col", [(q, q ^ b) for q in range(n_col)]) for b in range(1, plan.group)]
        )

    slots = plan.group
    return pl.pallas_call(
        partial(merge_kernel, plan, splits),
        out_shape=jax.ShapeDtypeStruct((2, plan.row_dev, plan.freq_tiles * LANES), jnp.float32),
        in_specs=[smem] + [vmem] * (len(splits) * plan.group + n_row),
        out_specs=pl.BlockSpec(memory_space=pl.ANY),
        scratch_shapes=[
            pltpu.VMEM((slots, plan.freq_tiles * SUBS, LANES), jnp.float32),
            pltpu.VMEM((slots, SUBS, plan.freq_tiles * LANES), jnp.float32),
            pltpu.SemaphoreType.DMA((slots,)),
        ],
        compiler_params=pltpu.CompilerParams(vmem_limit_bytes=24 * 2**20),
        name="merge",
    )(me, *[chunk for part in chunks for chunk in part], *counts)


def solution(mesh):
    placed = (P("row", "col"), P("row", "col"), P("row", "col"))
    return jax.shard_map(
        per_device, mesh=mesh, in_specs=placed, out_specs=P(None, "row", "col"), check_vma=False
    )
```

```python
import math
from functools import partial

import jax
import jax.numpy as jnp
import ml_dtypes
import numpy as np
from jax import lax
from jax.experimental import pallas as pl
from jax.experimental.pallas import tpu as pltpu
from jax.sharding import PartitionSpec as P

LEVELS = 4096
TILE_R = 16
TILE_C = 512
LANES = 128
SUBS = 8
INNER = 256
PAD = 4
FINE = 16
ORDER = (7, 6, 5, 4, 3, 2, 1)
SPLITS = (4,)
GROUP = 8


class Plan:
    def __init__(self, row_dev, pupil_dev, n_col, n_row):
        self.row_dev = row_dev
        self.pupil_dev = pupil_dev
        self.n_col = n_col
        self.n_row = n_row
        self.rows_all = row_dev * n_row
        self.group = min(GROUP, n_col)
        self.n_groups = n_col // self.group
        self.rows = row_dev // self.group
        self.n_pupil = pupil_dev * n_col
        self.n_pad = PAD * self.n_pupil
        self.n1 = self.n_pupil // INNER
        self.k1 = PAD * self.n1
        self.n1_dev = pupil_dev // INNER
        self.k2_group = INNER // self.n_groups
        self.k2_dev = INNER // n_col
        self.freq_tiles = PAD * pupil_dev // LANES
        self.k1_tiles = self.k1 // LANES
        self.lane_parts = INNER // LANES
        self.chunk = self.rows * 2 * self.lane_parts * self.n1_dev


def split_bf16(table):
    high = table.astype(ml_dtypes.bfloat16)
    low = (table - high.astype(np.float64)).astype(ml_dtypes.bfloat16)
    return np.stack([high, low])


def outer_tables(plan):
    angle = np.arange(plan.n1)[:, None] * np.arange(plan.k1)[None, :] % plan.k1
    angle = angle * (2.0 * np.pi / plan.k1)
    return split_bf16(np.concatenate([np.cos(angle), np.sin(angle)]))


def inner_tables(plan):
    angle = np.arange(INNER)[:, None] * np.arange(INNER)[None, :] % INNER
    angle = angle * (2.0 * np.pi / INNER)
    table = np.concatenate([np.cos(angle), np.sin(angle)], axis=1)
    return split_bf16(table.reshape(plan.n_col, plan.k2_dev, 2 * INNER))


def twist_tables(plan):
    made = []
    for cells in (np.arange(0, INNER, FINE), np.arange(FINE)):
        angle = cells[:, None] * np.arange(plan.k1)[None, :] * (2.0 * np.pi / plan.n_pad)
        made.extend([np.cos(angle), np.sin(angle)])
    return np.concatenate(made).astype(np.float32)


def field_kernel(plan, row_ref, tiles_ref, *refs):
    others, (codes_ref, mask_ref, all_mask_ref, out_ref, open_ref) = refs[: plan.n_row - 1], refs[plan.n_row - 1 :]
    step_id = pl.program_id(0)
    tile_cols = plan.pupil_dev // TILE_C

    @pl.when(step_id == 0)
    def _():
        total = jnp.zeros((SUBS, LANES), jnp.int32)
        for t in range(plan.row_dev // SUBS):
            for j in range(plan.pupil_dev // LANES):
                total = total + all_mask_ref[t * SUBS : (t + 1) * SUBS, j * LANES : (j + 1) * LANES]
        open_ref[...] = total.astype(jnp.float32)

    pistons = []
    for i in range(tile_cols):
        piston = jnp.int32(0)
        for d, other in enumerate(others):
            column = other[0, i]
            for k in range(1, plan.row_dev // TILE_R):
                column = column + other[k, i]
            piston = piston + jnp.where(row_ref[0] > d, column, 0)
        for k in range(plan.row_dev // TILE_R):
            piston = piston + jnp.where(step_id >= k, tiles_ref[k, i], 0)
        pistons.append(piston)
    take = min(plan.rows, SUBS)
    stride = 2 * plan.lane_parts * plan.n1_dev
    for t in range(TILE_R // SUBS):
        for j in range(plan.pupil_dev // LANES):
            rows = slice(t * SUBS, (t + 1) * SUBS)
            lanes = slice(j * LANES, (j + 1) * LANES)
            code = (codes_ref[rows, lanes] + pistons[j * LANES // TILE_C]) & (LEVELS - 1)
            quadrant = (code + LEVELS // 8) >> 10
            rest = (code - (quadrant << 10)).astype(jnp.float32) * (2.0 * math.pi / LEVELS)
            sq = rest * rest
            cos = 1.0 + sq * (-1.0 / 2 + sq * (1.0 / 24 + sq * (-1.0 / 720 + sq * (1.0 / 40320))))
            sin = rest * (1.0 + sq * (-1.0 / 6 + sq * (1.0 / 120 + sq * (-1.0 / 5040 + sq * (1.0 / 362880)))))
            amplitude = mask_ref[rows, lanes].astype(jnp.float32)
            swap = (quadrant & 1) == 1
            real = jnp.where(swap, sin, cos) * jnp.where(((quadrant + 1) & 2) == 2, -amplitude, amplitude)
            imag = jnp.where(swap, cos, sin) * jnp.where((quadrant & 2) == 2, -amplitude, amplitude)
            for part, value in enumerate((real, imag)):
                start = (part * plan.lane_parts + j % plan.lane_parts) * plan.n1_dev + j // plan.lane_parts
                for d in range(SUBS // take):
                    row = t * SUBS + d * take
                    dest, first = row // plan.rows, row % plan.rows
                    for g in range(plan.n_groups):
                        out_ref[g, dest, pl.ds(first * stride + start, take, stride=stride), :] = value[
                            d * take : (d + 1) * take
                        ]
    for g in range(plan.n_groups):
        for dest in range(TILE_R // plan.rows):
            out_ref[g, dest, plan.chunk :, :] = open_ref[...]


def transform_kernel(plan, first, rows, with_count, me_ref, x_ref, outer_ref, inner_ref, twist_ref, *refs):
    chunk_row = plan.chunk // plan.rows
    me = me_ref[0]

    def outer(a, b):
        return lax.dot_general(a, b, (((0,), (0,)), ((), ())), preferred_element_type=jnp.float32)

    def inner(a, b):
        return jnp.dot(a, b, preferred_element_type=jnp.float32)

    if with_count:
        refs[plan.group][...] = jnp.sum(x_ref[:, plan.chunk :, :], axis=0)
    n1, k2_dev = plan.n1, plan.k2_dev
    w1, w2 = [], []
    for s in range(2):
        cos, sin = outer_ref[s, :n1], outer_ref[s, n1:]
        w1.append(jnp.concatenate([jnp.concatenate([cos, sin]), jnp.concatenate([-sin, cos])], axis=1))
        blocks = []
        for b in range(plan.group):
            both = inner_ref[s, me ^ b]
            cos, sin = both[:, :INNER], both[:, INNER:]
            blocks.append(both)
            blocks.append(jnp.concatenate([-sin, cos], axis=1))
        w2.append(jnp.concatenate(blocks))
    size = 2 * k2_dev
    count = INNER // FINE
    fine_cos, fine_sin = twist_ref[2 * count : 2 * count + FINE], twist_ref[2 * count + FINE :]
    tc, ts = [], []
    for a in range(count):
        cos, sin = twist_ref[a : a + 1], twist_ref[count + a : count + a + 1]
        tc.append(cos * fine_cos - sin * fine_sin)
        ts.append(sin * fine_cos + cos * fine_sin)
    tc, ts = jnp.concatenate(tc), jnp.concatenate(ts)
    for r in range(rows):
        halves = []
        for part in range(2):
            pieces = []
            for lt in range(plan.lane_parts):
                at = (first + r) * chunk_row + (part * plan.lane_parts + lt) * plan.n1_dev
                pieces.append(x_ref[:, at : at + plan.n1_dev, :].reshape(plan.n1, LANES))
            halves.append(jnp.concatenate(pieces, axis=1))
        x = jnp.concatenate(halves, axis=0)
        xh = x.astype(jnp.bfloat16)
        xl = (x - xh.astype(jnp.float32)).astype(jnp.bfloat16)
        y = outer(xh, w1[0]) + outer(xl, w1[0]) + outer(xh, w1[1])
        yr, yi = y[:, : plan.k1], y[:, plan.k1 :]
        f = jnp.concatenate([yr * tc + yi * ts, yi * tc - yr * ts], axis=0)
        fh = f.astype(jnp.bfloat16)
        fl = (f - fh.astype(jnp.float32)).astype(jnp.bfloat16)
        z = inner(w2[0], fh) + inner(w2[1], fh) + inner(w2[0], fl)
        for b in range(plan.group):
            refs[b][r] = z[b * size : (b + 1) * size].reshape(2, plan.k2_dev, plan.k1)


def merge_kernel(plan, splits, me_ref, *refs):
    n = len(splits)
    chunks = []
    for i in range(n):
        given = refs[i * plan.group : (i + 1) * plan.group]
        chunks.append([given[(ORDER + (0,)).index(b)] for b in range(plan.group)])
    counts = refs[n * plan.group : n * plan.group + plan.n_row]
    out_ref, tile_ref, row_ref, sems = refs[n * plan.group + plan.n_row :]
    total = counts[0][...]
    for other in counts[1:]:
        total = total + other[...]
    total = jnp.sum(jnp.sum(total, axis=0, keepdims=True), axis=1, keepdims=True)
    scale = jnp.sqrt(float(plan.rows_all) / total)
    inside = lax.rem(me_ref[0], plan.group)
    swapped = lax.rem(inside, 2) == 1
    take = min(plan.k2_dev, SUBS)
    stride = plan.k1_tiles * SUBS
    copies = []
    for pair in range(plan.group // 2):
        for part in range(2):
            slot = pair * 2 + part
            for i, rows in enumerate(splits):
                for r in range(rows):
                    for k2 in range(0, plan.k2_dev, take):
                        for j in range(plan.k1_tiles):
                            lanes = slice(j * LANES, (j + 1) * LANES)
                            a = chunks[i][2 * pair][r, part, k2 : k2 + take, lanes] * scale
                            b = chunks[i][2 * pair + 1][r, part, k2 : k2 + take, lanes] * scale
                            at = (k2 * plan.k1_tiles + j) * SUBS + sum(splits[:i]) + r
                            tile_ref[slot, pl.ds(at, take, stride=stride), :] = jnp.where(swapped, b, a)
                            tile_ref[slot, pl.ds(at + plan.rows, take, stride=stride), :] = jnp.where(swapped, a, b)
            for f in range(plan.freq_tiles):
                row_ref[slot, :, f * LANES : (f + 1) * LANES] = tile_ref[slot, f * SUBS : (f + 1) * SUBS, :]
            tile = lax.div(inside, 2) ^ pair
            target = out_ref.at[part, pl.ds(pl.multiple_of(tile * SUBS, SUBS), SUBS), :]
            copy = pltpu.make_async_copy(row_ref.at[slot], target, sems.at[slot])
            copy.start()
            copies.append(copy)
    for copy in copies:
        copy.wait()


def per_device(phase_codes, aperture, tile_offsets):
    n_col = lax.axis_size("col")
    n_row = lax.axis_size("row")
    plan = Plan(*phase_codes.shape, n_col, n_row)
    row_index = lax.axis_index("row").astype(jnp.int32).reshape(1)
    col_index = lax.axis_index("col").astype(jnp.int32).reshape(1)
    me = col_index

    def along_rows(value):
        return [lax.ppermute(value, "row", [(i, (i + d) % n_row) for i in range(n_row)]) for d in range(1, n_row)]

    smem = pl.BlockSpec(memory_space=pltpu.SMEM)
    vmem = pl.BlockSpec(memory_space=pltpu.VMEM)
    others = along_rows(tile_offsets)
    steps = plan.row_dev // TILE_R
    block = (plan.n_groups, plan.group // steps, plan.chunk + SUBS, LANES)
    packed = pl.pallas_call(
        partial(field_kernel, plan),
        out_shape=jax.ShapeDtypeStruct((plan.n_groups, plan.group, plan.chunk + SUBS, LANES), jnp.float32),
        grid=(steps,),
        in_specs=[smem, smem]
        + [smem] * (n_row - 1)
        + [
            pl.BlockSpec((TILE_R, plan.pupil_dev), lambda t: (t, 0)),
            pl.BlockSpec((TILE_R, plan.pupil_dev), lambda t: (t, 0)),
            pl.BlockSpec((plan.row_dev, plan.pupil_dev), lambda t: (0, 0)),
        ],
        out_specs=pl.BlockSpec(block, lambda t: (0, t, 0, 0)),
        scratch_shapes=[pltpu.VMEM((SUBS, LANES), jnp.float32)],
        name="field",
    )(row_index, tile_offsets, *others, phase_codes, aperture, aperture)
    packed = packed.reshape(n_col, plan.chunk + SUBS, LANES)
    received = lax.all_to_all(packed, "col", split_axis=0, concat_axis=0, tiled=True)

    tables = [outer_tables(plan), inner_tables(plan), twist_tables(plan)]
    splits = SPLITS if sum(SPLITS) == plan.rows else (plan.rows,)
    chunks = []
    for i, rows in enumerate(splits):
        shapes = [jax.ShapeDtypeStruct((rows, 2, plan.k2_dev, plan.k1), jnp.float32)] * plan.group
        if i == 0:
            shapes = shapes + [jax.ShapeDtypeStruct((SUBS, LANES), jnp.float32)]
        made = pl.pallas_call(
            partial(transform_kernel, plan, sum(splits[:i]), rows, i == 0),
            out_shape=shapes,
            in_specs=[smem, vmem, vmem, vmem, vmem],
            out_specs=[vmem] * len(shapes),
            compiler_params=pltpu.CompilerParams(vmem_limit_bytes=24 * 2**20),
            name="transform",
        )(me, received, *tables)
        sent = {b: lax.ppermute(made[b], "col", [(q, q ^ b) for q in range(n_col)]) for b in ORDER}
        if i == 0:
            counts = [made[-1]] + along_rows(made[-1])
        chunks.append([sent[b] for b in ORDER] + [made[0]])

    slots = plan.group
    return pl.pallas_call(
        partial(merge_kernel, plan, splits),
        out_shape=jax.ShapeDtypeStruct((2, plan.row_dev, plan.freq_tiles * LANES), jnp.float32),
        in_specs=[smem] + [vmem] * (len(splits) * plan.group + n_row),
        out_specs=pl.BlockSpec(memory_space=pl.ANY),
        scratch_shapes=[
            pltpu.VMEM((slots, plan.freq_tiles * SUBS, LANES), jnp.float32),
            pltpu.VMEM((slots, SUBS, plan.freq_tiles * LANES), jnp.float32),
            pltpu.SemaphoreType.DMA((slots,)),
        ],
        compiler_params=pltpu.CompilerParams(vmem_limit_bytes=24 * 2**20),
        name="merge",
    )(me, *[chunk for part in chunks for chunk in part], *counts)


def solution(mesh):
    placed = (P("row", "col"), P("row", "col"), P("row", "col"))
    return jax.shard_map(
        per_device, mesh=mesh, in_specs=placed, out_specs=P(None, "row", "col"), check_vma=False
    )
```

```python
import math
from functools import partial

import jax
import jax.numpy as jnp
import ml_dtypes
import numpy as np
from jax import lax
from jax.experimental import pallas as pl
from jax.experimental.pallas import tpu as pltpu
from jax.sharding import PartitionSpec as P

LEVELS = 4096
TILE_R = 16
TILE_C = 512
LANES = 128
SUBS = 8
INNER = 256
PAD = 4
FINE = 16
ORDER = (7, 6, 5, 4, 3, 2, 1)
SPLITS = (4,)
GROUP = 8


class Plan:
    def __init__(self, row_dev, pupil_dev, n_col, n_row):
        self.row_dev = row_dev
        self.pupil_dev = pupil_dev
        self.n_col = n_col
        self.n_row = n_row
        self.rows_all = row_dev * n_row
        self.group = min(GROUP, n_col)
        self.n_groups = n_col // self.group
        self.rows = row_dev // self.group
        self.n_pupil = pupil_dev * n_col
        self.n_pad = PAD * self.n_pupil
        self.n1 = self.n_pupil // INNER
        self.k1 = PAD * self.n1
        self.n1_dev = pupil_dev // INNER
        self.k2_group = INNER // self.n_groups
        self.k2_dev = INNER // n_col
        self.freq_tiles = PAD * pupil_dev // LANES
        self.k1_tiles = self.k1 // LANES
        self.lane_parts = INNER // LANES
        self.chunk = self.rows * 2 * self.lane_parts * self.n1_dev


def split_bf16(table):
    high = table.astype(ml_dtypes.bfloat16)
    low = (table - high.astype(np.float64)).astype(ml_dtypes.bfloat16)
    return np.stack([high, low])


def outer_tables(plan):
    angle = np.arange(plan.n1)[:, None] * np.arange(plan.k1)[None, :] % plan.k1
    angle = angle * (2.0 * np.pi / plan.k1)
    return split_bf16(np.concatenate([np.cos(angle), np.sin(angle)]))


def inner_tables(plan):
    angle = np.arange(INNER)[:, None] * np.arange(INNER)[None, :] % INNER
    angle = angle * (2.0 * np.pi / INNER)
    table = np.concatenate([np.cos(angle), np.sin(angle)], axis=1)
    return split_bf16(table.reshape(plan.n_col, plan.k2_dev, 2 * INNER))


def twist_tables(plan):
    made = []
    for cells in (np.arange(0, INNER, FINE), np.arange(FINE)):
        angle = cells[:, None] * np.arange(plan.k1)[None, :] * (2.0 * np.pi / plan.n_pad)
        made.extend([np.cos(angle), np.sin(angle)])
    return np.concatenate(made).astype(np.float32)


def unit_phase(code):
    quadrant = (code + LEVELS // 8) >> 10
    rest = (code - (quadrant << 10)).astype(jnp.float32) * (2.0 * math.pi / LEVELS)
    sq = rest * rest
    cos = 1.0 + sq * (-1.0 / 2 + sq * (1.0 / 24 + sq * (-1.0 / 720 + sq * (1.0 / 40320))))
    sin = rest * (1.0 + sq * (-1.0 / 6 + sq * (1.0 / 120 + sq * (-1.0 / 5040 + sq * (1.0 / 362880)))))
    swap = (quadrant & 1) == 1
    minus_cos = ((quadrant + 1) & 2) == 2
    minus_sin = (quadrant & 2) == 2
    return jnp.where(swap, sin, cos), jnp.where(swap, cos, sin), minus_cos, minus_sin


def field_kernel(plan, tiles_ref, codes_ref, mask_ref, out_ref, open_ref):
    step_id = pl.program_id(0)
    pistons = []
    for i in range(plan.pupil_dev // TILE_C):
        piston = jnp.int32(0)
        for k in range(plan.row_dev // TILE_R):
            piston = piston + jnp.where(step_id >= k, tiles_ref[k, i], 0)
        pistons.append(piston)
    stride = 2 * plan.lane_parts * plan.n1_dev
    total = jnp.zeros((SUBS, LANES), jnp.float32)
    for t in range(TILE_R // SUBS):
        for j in range(plan.pupil_dev // LANES):
            rows = slice(t * SUBS, (t + 1) * SUBS)
            lanes = slice(j * LANES, (j + 1) * LANES)
            code = (codes_ref[rows, lanes] + pistons[j * LANES // TILE_C]) & (LEVELS - 1)
            cos, sin, minus_cos, minus_sin = unit_phase(code)
            amplitude = mask_ref[rows, lanes].astype(jnp.float32)
            total = total + amplitude
            real = cos * jnp.where(minus_cos, -amplitude, amplitude)
            imag = sin * jnp.where(minus_sin, -amplitude, amplitude)
            for part, value in enumerate((real, imag)):
                start = (part * plan.lane_parts + j % plan.lane_parts) * plan.n1_dev + j // plan.lane_parts
                for g in range(plan.n_groups):
                    out_ref[g, pl.ds(t * SUBS * stride + start, SUBS, stride=stride), :] = value

    @pl.when(step_id == 0)
    def _():
        open_ref[...] = total

    @pl.when(step_id > 0)
    def _():
        open_ref[...] = open_ref[...] + total


def transform_kernel(plan, first, rows, me_ref, info_ref, x_ref, outer_ref, inner_ref, twist_ref, *refs):
    chunk_row = plan.chunk // plan.rows
    me = me_ref[0]

    def outer(a, b):
        return lax.dot_general(a, b, (((0,), (0,)), ((), ())), preferred_element_type=jnp.float32)

    def inner(a, b):
        return jnp.dot(a, b, preferred_element_type=jnp.float32)

    info = info_ref[: plan.n_col]
    info = jnp.broadcast_to(info[:, None, :], (plan.n_col, plan.n1_dev, LANES)).reshape(plan.n1, LANES)
    tile = lax.broadcasted_iota(jnp.int32, info.shape, 0) % plan.n1_dev * INNER // TILE_C
    own = lax.broadcasted_iota(jnp.int32, info.shape, 1) == tile
    before = jnp.sum(jnp.where(own, info, 0.0), axis=1, keepdims=True).astype(jnp.int32)
    turn_cos, turn_sin, minus_cos, minus_sin = unit_phase(before)
    turn_cos = jnp.where(minus_cos, -turn_cos, turn_cos)
    turn_sin = jnp.where(minus_sin, -turn_sin, turn_sin)
    n1, k2_dev = plan.n1, plan.k2_dev
    w1, w2 = [], []
    for s in range(2):
        cos, sin = outer_ref[s, :n1], outer_ref[s, n1:]
        w1.append(jnp.concatenate([jnp.concatenate([cos, sin]), jnp.concatenate([-sin, cos])], axis=1))
        blocks = []
        for b in range(plan.group):
            both = inner_ref[s, me ^ b]
            cos, sin = both[:, :INNER], both[:, INNER:]
            blocks.append(both)
            blocks.append(jnp.concatenate([-sin, cos], axis=1))
        w2.append(jnp.concatenate(blocks))
    size = 2 * k2_dev
    count = INNER // FINE
    fine_cos, fine_sin = twist_ref[2 * count : 2 * count + FINE], twist_ref[2 * count + FINE :]
    tc, ts = [], []
    for a in range(count):
        cos, sin = twist_ref[a : a + 1], twist_ref[count + a : count + a + 1]
        tc.append(cos * fine_cos - sin * fine_sin)
        ts.append(sin * fine_cos + cos * fine_sin)
    tc, ts = jnp.concatenate(tc), jnp.concatenate(ts)
    for r in range(rows):
        halves = []
        for part in range(2):
            pieces = []
            for lt in range(plan.lane_parts):
                at = (first + r) * chunk_row + (part * plan.lane_parts + lt) * plan.n1_dev
                pieces.append(x_ref[:, at : at + plan.n1_dev, :].reshape(plan.n1, LANES))
            halves.append(jnp.concatenate(pieces, axis=1))
        real, imag = halves
        x = jnp.concatenate([real * turn_cos - imag * turn_sin, real * turn_sin + imag * turn_cos], axis=0)
        xh = x.astype(jnp.bfloat16)
        xl = (x - xh.astype(jnp.float32)).astype(jnp.bfloat16)
        y = outer(xh, w1[0]) + outer(xl, w1[0]) + outer(xh, w1[1])
        yr, yi = y[:, : plan.k1], y[:, plan.k1 :]
        f = jnp.concatenate([yr * tc + yi * ts, yi * tc - yr * ts], axis=0)
        fh = f.astype(jnp.bfloat16)
        fl = (f - fh.astype(jnp.float32)).astype(jnp.bfloat16)
        z = inner(w2[0], fh) + inner(w2[1], fh) + inner(w2[0], fl)
        for b in range(plan.group):
            refs[b][r] = z[b * size : (b + 1) * size].reshape(2, plan.k2_dev, plan.k1)


def merge_kernel(plan, splits, me_ref, *refs):
    n = len(splits)
    chunks = []
    for i in range(n):
        given = refs[i * plan.group : (i + 1) * plan.group]
        chunks.append([given[(ORDER + (0,)).index(b)] for b in range(plan.group)])
    counts = refs[n * plan.group : n * plan.group + plan.n_row]
    out_ref, tile_ref, row_ref, sems = refs[n * plan.group + plan.n_row :]
    total = counts[0][...]
    for other in counts[1:]:
        total = total + other[...]
    total = jnp.sum(jnp.sum(total, axis=0, keepdims=True), axis=1, keepdims=True)
    scale = jnp.sqrt(float(plan.rows_all) / total)
    inside = lax.rem(me_ref[0], plan.group)
    swapped = lax.rem(inside, 2) == 1
    take = min(plan.k2_dev, SUBS)
    stride = plan.k1_tiles * SUBS
    copies = []
    for pair in range(plan.group // 2):
        for part in range(2):
            slot = pair * 2 + part
            for i, rows in enumerate(splits):
                for r in range(rows):
                    for k2 in range(0, plan.k2_dev, take):
                        for j in range(plan.k1_tiles):
                            lanes = slice(j * LANES, (j + 1) * LANES)
                            a = chunks[i][2 * pair][r, part, k2 : k2 + take, lanes] * scale
                            b = chunks[i][2 * pair + 1][r, part, k2 : k2 + take, lanes] * scale
                            at = (k2 * plan.k1_tiles + j) * SUBS + sum(splits[:i]) + r
                            tile_ref[slot, pl.ds(at, take, stride=stride), :] = jnp.where(swapped, b, a)
                            tile_ref[slot, pl.ds(at + plan.rows, take, stride=stride), :] = jnp.where(swapped, a, b)
            for f in range(plan.freq_tiles):
                row_ref[slot, :, f * LANES : (f + 1) * LANES] = tile_ref[slot, f * SUBS : (f + 1) * SUBS, :]
            tile = lax.div(inside, 2) ^ pair
            target = out_ref.at[part, pl.ds(pl.multiple_of(tile * SUBS, SUBS), SUBS), :]
            copy = pltpu.make_async_copy(row_ref.at[slot], target, sems.at[slot])
            copy.start()
            copies.append(copy)
    for copy in copies:
        copy.wait()


def per_device(phase_codes, aperture, tile_offsets):
    n_col = lax.axis_size("col")
    n_row = lax.axis_size("row")
    plan = Plan(*phase_codes.shape, n_col, n_row)
    row_index = lax.axis_index("row")
    col_index = lax.axis_index("col")
    me = col_index.astype(jnp.int32).reshape(1)

    def along_rows(value):
        return [lax.ppermute(value, "row", [(i, (i + d) % n_row) for i in range(n_row)]) for d in range(1, n_row)]

    smem = pl.BlockSpec(memory_space=pltpu.SMEM)
    vmem = pl.BlockSpec(memory_space=pltpu.VMEM)
    before = jnp.zeros((1, plan.pupil_dev // TILE_C), jnp.int32)
    for d, other in enumerate(along_rows(tile_offsets)):
        before = before + jnp.where(row_index > d, jnp.sum(other, axis=0, keepdims=True), 0)
    before = jnp.pad((before & (LEVELS - 1)).astype(jnp.float32), ((0, 0), (0, LANES - before.shape[1])))
    mine = jnp.arange(n_col, dtype=jnp.int32)[:, None] == col_index

    field_rows = plan.row_dev * 2 * plan.lane_parts * plan.n1_dev
    steps = plan.row_dev // TILE_R
    packed, opened = pl.pallas_call(
        partial(field_kernel, plan),
        out_shape=[
            jax.ShapeDtypeStruct((plan.n_groups, field_rows, LANES), jnp.float32),
            jax.ShapeDtypeStruct((SUBS, LANES), jnp.float32),
        ],
        grid=(steps,),
        in_specs=[
            smem,
            pl.BlockSpec((TILE_R, plan.pupil_dev), lambda t: (t, 0)),
            pl.BlockSpec((TILE_R, plan.pupil_dev), lambda t: (t, 0)),
        ],
        out_specs=[
            pl.BlockSpec((plan.n_groups, field_rows // steps, LANES), lambda t: (0, t, 0)),
            pl.BlockSpec((SUBS, LANES), lambda t: (0, 0)),
        ],
        name="field",
    )(tile_offsets, phase_codes, aperture)
    packed = packed.reshape(n_col, plan.chunk, LANES)
    received = lax.all_to_all(packed, "col", split_axis=0, concat_axis=0, tiled=True)

    info = jnp.concatenate([jnp.where(mine, before, 0.0), opened])
    for bit in range(n_col.bit_length() - 1):
        info = info + lax.ppermute(info, "col", [(q, q ^ 1 << bit) for q in range(n_col)])
    opened = info[n_col:]
    counts = [opened] + along_rows(opened)

    tables = [outer_tables(plan), inner_tables(plan), twist_tables(plan)]
    splits = SPLITS if sum(SPLITS) == plan.rows else (plan.rows,)
    chunks = []
    for i, rows in enumerate(splits):
        shapes = [jax.ShapeDtypeStruct((rows, 2, plan.k2_dev, plan.k1), jnp.float32)] * plan.group
        made = pl.pallas_call(
            partial(transform_kernel, plan, sum(splits[:i]), rows),
            out_shape=shapes,
            in_specs=[smem] + [vmem] * 5,
            out_specs=[vmem] * len(shapes),
            compiler_params=pltpu.CompilerParams(vmem_limit_bytes=24 * 2**20),
            name="transform",
        )(me, info, received, *tables)
        sent = {b: lax.ppermute(made[b], "col", [(q, q ^ b) for q in range(n_col)]) for b in ORDER}
        chunks.append([sent[b] for b in ORDER] + [made[0]])

    slots = plan.group
    return pl.pallas_call(
        partial(merge_kernel, plan, splits),
        out_shape=jax.ShapeDtypeStruct((2, plan.row_dev, plan.freq_tiles * LANES), jnp.float32),
        in_specs=[smem] + [vmem] * (len(splits) * plan.group + n_row),
        out_specs=pl.BlockSpec(memory_space=pl.ANY),
        scratch_shapes=[
            pltpu.VMEM((slots, plan.freq_tiles * SUBS, LANES), jnp.float32),
            pltpu.VMEM((slots, SUBS, plan.freq_tiles * LANES), jnp.float32),
            pltpu.SemaphoreType.DMA((slots,)),
        ],
        compiler_params=pltpu.CompilerParams(vmem_limit_bytes=24 * 2**20),
        name="merge",
    )(me, *[chunk for part in chunks for chunk in part], *counts)


def solution(mesh):
    placed = (P("row", "col"), P("row", "col"), P("row", "col"))
    return jax.shard_map(
        per_device, mesh=mesh, in_specs=placed, out_specs=P(None, "row", "col"), check_vma=False
    )
```

```python
import math
from functools import partial

import jax
import jax.numpy as jnp
import ml_dtypes
import numpy as np
from jax import lax
from jax.experimental import pallas as pl
from jax.experimental.pallas import tpu as pltpu
from jax.sharding import PartitionSpec as P

LEVELS = 4096
TILE_R = 16
TILE_C = 512
LANES = 128
SUBS = 8
INNER = 256
PAD = 4
FINE = 16
CHIP_ORDER = (4, 1, 5, 2, 6, 3, 7)
ORDER = (7, 6, 5, 4, 3, 2, 1)
GROUP = 8


class Plan:
    def __init__(self, row_dev, pupil_dev, n_col, n_row):
        self.row_dev = row_dev
        self.pupil_dev = pupil_dev
        self.n_col = n_col
        self.n_row = n_row
        self.rows_all = row_dev * n_row
        self.group = min(GROUP, n_col)
        self.n_groups = n_col // self.group
        self.rows = row_dev // self.group
        self.n_pupil = pupil_dev * n_col
        self.n_pad = PAD * self.n_pupil
        self.n1 = self.n_pupil // INNER
        self.k1 = PAD * self.n1
        self.n1_dev = pupil_dev // INNER
        self.k2_group = INNER // self.n_groups
        self.k2_dev = INNER // n_col
        self.freq_tiles = PAD * pupil_dev // LANES
        self.k1_tiles = self.k1 // LANES
        self.lane_parts = INNER // LANES
        self.chunk = self.rows * 2 * self.lane_parts * self.n1_dev


def split_bf16(table):
    high = table.astype(ml_dtypes.bfloat16)
    low = (table - high.astype(np.float64)).astype(ml_dtypes.bfloat16)
    return np.stack([high, low])


def outer_tables(plan, blocks):
    angle = np.arange(plan.n1)[:, None] * np.arange(plan.k1)[None, :] % plan.k1
    angle = angle * (2.0 * np.pi / plan.k1)
    table = np.stack([np.cos(angle), np.sin(angle)]).reshape(2, blocks, plan.n1 // blocks, plan.k1)
    return split_bf16(table.transpose(1, 0, 2, 3))


def inner_tables(plan):
    angle = np.arange(INNER)[:, None] * np.arange(INNER)[None, :] % INNER
    angle = angle * (2.0 * np.pi / INNER)
    table = np.concatenate([np.cos(angle), np.sin(angle)], axis=1)
    return split_bf16(table.reshape(plan.n_col, plan.k2_dev, 2 * INNER))


def twist_tables(plan):
    made = []
    for cells in (np.arange(0, INNER, FINE), np.arange(FINE)):
        angle = cells[:, None] * np.arange(plan.k1)[None, :] * (2.0 * np.pi / plan.n_pad)
        made.extend([np.cos(angle), np.sin(angle)])
    return np.concatenate(made).astype(np.float32)


def unit_phase(code):
    quadrant = (code + LEVELS // 8) >> 10
    rest = (code - (quadrant << 10)).astype(jnp.float32) * (2.0 * math.pi / LEVELS)
    sq = rest * rest
    cos = 1.0 + sq * (-1.0 / 2 + sq * (1.0 / 24 + sq * (-1.0 / 720 + sq * (1.0 / 40320))))
    sin = rest * (1.0 + sq * (-1.0 / 6 + sq * (1.0 / 120 + sq * (-1.0 / 5040 + sq * (1.0 / 362880)))))
    swap = (quadrant & 1) == 1
    minus_cos = ((quadrant + 1) & 2) == 2
    minus_sin = (quadrant & 2) == 2
    return jnp.where(swap, sin, cos), jnp.where(swap, cos, sin), minus_cos, minus_sin


def field_kernel(plan, tiles_ref, codes_ref, mask_ref, out_ref, open_ref):
    step_id = pl.program_id(0)
    pistons = []
    for i in range(plan.pupil_dev // TILE_C):
        piston = jnp.int32(0)
        for k in range(plan.row_dev // TILE_R):
            piston = piston + jnp.where(step_id >= k, tiles_ref[k, i], 0)
        pistons.append(piston)
    stride = 2 * plan.lane_parts * plan.n1_dev
    total = jnp.zeros((SUBS, LANES), jnp.float32)
    for t in range(TILE_R // SUBS):
        for j in range(plan.pupil_dev // LANES):
            rows = slice(t * SUBS, (t + 1) * SUBS)
            lanes = slice(j * LANES, (j + 1) * LANES)
            code = (codes_ref[rows, lanes] + pistons[j * LANES // TILE_C]) & (LEVELS - 1)
            cos, sin, minus_cos, minus_sin = unit_phase(code)
            amplitude = mask_ref[rows, lanes].astype(jnp.float32)
            total = total + amplitude
            real = cos * jnp.where(minus_cos, -amplitude, amplitude)
            imag = sin * jnp.where(minus_sin, -amplitude, amplitude)
            for part, value in enumerate((real, imag)):
                start = (part * plan.lane_parts + j % plan.lane_parts) * plan.n1_dev + j // plan.lane_parts
                for g in range(plan.n_groups):
                    out_ref[g, pl.ds(t * SUBS * stride + start, SUBS, stride=stride), :] = value

    @pl.when(step_id == 0)
    def _():
        open_ref[...] = total

    @pl.when(step_id > 0)
    def _():
        open_ref[...] = open_ref[...] + total


def chip_field_kernel(plan, me_ref, *refs):
    n_other = plan.n_row - 1
    tiles, others, refs = refs[:2], (refs[2 : 2 + n_other], refs[2 + n_other : 2 + 2 * n_other]), refs[2 + 2 * n_other :]
    codes_hbm, mask_hbm, near_codes_ref, near_mask_ref = refs[:4]
    outs, (codes_ref, mask_ref, made_ref, sems) = refs[4:-4], refs[-4:]
    core, chip, row = me_ref[0], me_ref[1], me_ref[2]
    half = plan.row_dev // 2
    first = pl.multiple_of(core * half, half)
    copies = [
        pltpu.make_async_copy(codes_hbm, codes_ref, sems.at[0]),
        pltpu.make_async_copy(mask_hbm, mask_ref, sems.at[1]),
    ]
    for copy in copies:
        copy.start()
    total = jnp.zeros((SUBS, LANES), jnp.int32)
    stride = 2 * plan.lane_parts * plan.n1_dev
    for owner in (1, 0):
        if owner == 0:
            for copy in copies:
                copy.wait()
        codes, mask = ((codes_ref, mask_ref), (near_codes_ref, near_mask_ref))[owner]
        before = jnp.zeros((1, plan.pupil_dev // TILE_C), jnp.int32)
        for d, other in enumerate(others[owner]):
            before = before + jnp.where(row > d, jnp.sum(other[...], axis=0, keepdims=True), 0)
        for k in range(plan.row_dev // TILE_R):
            before = before + jnp.where(first >= k * TILE_R, tiles[owner][k : k + 1], 0)
        for t in range(plan.row_dev // SUBS):
            for j in range(plan.pupil_dev // LANES):
                total = total + mask[t * SUBS : (t + 1) * SUBS, j * LANES : (j + 1) * LANES]
        for t in range(half // SUBS):
            at = pl.multiple_of(first + t * SUBS, SUBS)
            for j in range(plan.pupil_dev // LANES):
                lanes = slice(j * LANES, (j + 1) * LANES)
                column = j * LANES // TILE_C
                piston = jnp.broadcast_to(before[:, column : column + 1], (SUBS, LANES))
                code = (codes[pl.ds(at, SUBS), lanes] + piston) & (LEVELS - 1)
                cos, sin, minus_cos, minus_sin = unit_phase(code)
                amplitude = mask[pl.ds(at, SUBS), lanes].astype(jnp.float32)
                real = cos * jnp.where(minus_cos, -amplitude, amplitude)
                imag = sin * jnp.where(minus_sin, -amplitude, amplitude)
                for part, value in enumerate((real, imag)):
                    start = (part * plan.lane_parts + j % plan.lane_parts) * plan.n1_dev + j // plan.lane_parts
                    made_ref[owner, pl.ds(t * SUBS * stride + start, SUBS, stride=stride), :] = value
    own_rows = lax.rem(chip, len(outs))
    for b, out in enumerate(outs):
        source = pl.multiple_of((own_rows ^ b) * plan.chunk, plan.chunk)
        for i in range(plan.chunk // plan.n1_dev):
            for side in range(2):
                block = made_ref[side ^ core, pl.ds(pl.multiple_of(source + i * plan.n1_dev, plan.n1_dev), plan.n1_dev), :]
                out[(2 * i + side) * plan.n1_dev : (2 * i + side + 1) * plan.n1_dev, :] = block
        out[2 * plan.chunk :, :] = total.astype(jnp.float32)


def chip_transform_kernel(plan, order, me_ref, *refs):
    n_chips = plan.n_col // 2
    given = refs[:n_chips]
    outer_ref, inner_ref, twist_ref = refs[n_chips : n_chips + 3]
    outs, count_ref = refs[n_chips + 3 : -1], refs[-1]
    chunks = [given[order.index(b)] for b in range(n_chips)]
    me = me_ref[0]
    chip = me >> 1
    count = chunks[0][2 * plan.chunk :, :]
    for chunk in chunks[1:]:
        count = count + chunk[2 * plan.chunk :, :]
    count_ref[...] = count
    w1 = []
    for s in range(2):
        rows = [outer_ref[s, chip ^ b] for b in range(n_chips)]
        w1.append([jnp.concatenate([both[i] for both in rows]) for i in range(2)])
    n1_chip = 2 * plan.n1_dev

    def part_of(r, part):
        pieces = []
        for lt in range(plan.lane_parts):
            at = ((r * 2 + part) * plan.lane_parts + lt) * n1_chip
            pieces.append(jnp.concatenate([chunk[at : at + n1_chip, :] for chunk in chunks]))
        return jnp.concatenate(pieces, axis=1)

    def field_of(r):
        return jnp.concatenate([part_of(r, 0), part_of(r, 1)])

    transform_rows(plan, me, plan.rows, field_of, w1, inner_ref, twist_ref, outs)


def transform_kernel(plan, me_ref, info_ref, x_ref, outer_ref, inner_ref, twist_ref, *refs):
    chunk_row = plan.chunk // plan.rows
    info = info_ref[: plan.n_col]
    info = jnp.broadcast_to(info[:, None, :], (plan.n_col, plan.n1_dev, LANES)).reshape(plan.n1, LANES)
    tile = lax.broadcasted_iota(jnp.int32, info.shape, 0) % plan.n1_dev * INNER // TILE_C
    own = lax.broadcasted_iota(jnp.int32, info.shape, 1) == tile
    before = jnp.sum(jnp.where(own, info, 0.0), axis=1, keepdims=True).astype(jnp.int32)
    turn_cos, turn_sin, minus_cos, minus_sin = unit_phase(before)
    turn_cos = jnp.where(minus_cos, -turn_cos, turn_cos)
    turn_sin = jnp.where(minus_sin, -turn_sin, turn_sin)
    w1 = [[outer_ref[s, 0, i] for i in range(2)] for s in range(2)]

    def field_of(r):
        halves = []
        for part in range(2):
            pieces = []
            for lt in range(plan.lane_parts):
                at = r * chunk_row + (part * plan.lane_parts + lt) * plan.n1_dev
                pieces.append(x_ref[:, at : at + plan.n1_dev, :].reshape(plan.n1, LANES))
            halves.append(jnp.concatenate(pieces, axis=1))
        real, imag = halves
        return jnp.concatenate([real * turn_cos - imag * turn_sin, real * turn_sin + imag * turn_cos], axis=0)

    transform_rows(plan, me_ref[0], plan.rows, field_of, w1, inner_ref, twist_ref, refs)


def transform_rows(plan, me, rows, field_of, outer_parts, inner_ref, twist_ref, outs):
    def outer(a, b):
        return lax.dot_general(a, b, (((0,), (0,)), ((), ())), preferred_element_type=jnp.float32)

    def inner(a, b):
        return jnp.dot(a, b, preferred_element_type=jnp.float32)

    k2_dev = plan.k2_dev
    w1, w2 = [], []
    for s in range(2):
        cos, sin = outer_parts[s]
        w1.append(jnp.concatenate([jnp.concatenate([cos, sin]), jnp.concatenate([-sin, cos])], axis=1))
        blocks = []
        for b in range(plan.group):
            both = inner_ref[s, me ^ b]
            cos, sin = both[:, :INNER], both[:, INNER:]
            blocks.append(both)
            blocks.append(jnp.concatenate([-sin, cos], axis=1))
        w2.append(jnp.concatenate(blocks))
    size = 2 * k2_dev
    count = INNER // FINE
    fine_cos, fine_sin = twist_ref[2 * count : 2 * count + FINE], twist_ref[2 * count + FINE :]
    tc, ts = [], []
    for a in range(count):
        cos, sin = twist_ref[a : a + 1], twist_ref[count + a : count + a + 1]
        tc.append(cos * fine_cos - sin * fine_sin)
        ts.append(sin * fine_cos + cos * fine_sin)
    tc, ts = jnp.concatenate(tc), jnp.concatenate(ts)
    for r in range(rows):
        x = field_of(r)
        xh = x.astype(jnp.bfloat16)
        xl = (x - xh.astype(jnp.float32)).astype(jnp.bfloat16)
        y = outer(xh, w1[0]) + outer(xl, w1[0]) + outer(xh, w1[1])
        yr, yi = y[:, : plan.k1], y[:, plan.k1 :]
        f = jnp.concatenate([yr * tc + yi * ts, yi * tc - yr * ts], axis=0)
        fh = f.astype(jnp.bfloat16)
        fl = (f - fh.astype(jnp.float32)).astype(jnp.bfloat16)
        z = inner(w2[0], fh) + inner(w2[1], fh) + inner(w2[0], fl)
        for b in range(plan.group):
            outs[b][r] = z[b * size : (b + 1) * size].reshape(2, k2_dev, plan.k1)


def merge_kernel(plan, swap_bit, me_ref, *refs):
    chunks = [refs[(ORDER + (0,)).index(b)] for b in range(plan.group)]
    counts = refs[plan.group : plan.group + plan.n_row]
    out_ref, tile_ref, row_ref, sems = refs[plan.group + plan.n_row :]
    total = counts[0][...]
    for other in counts[1:]:
        total = total + other[...]
    total = jnp.sum(jnp.sum(total, axis=0, keepdims=True), axis=1, keepdims=True)
    scale = jnp.sqrt(float(plan.rows_all) / total)
    inside = lax.rem(me_ref[0], plan.group)
    swapped = lax.rem(inside // swap_bit, 2) == 1
    take = min(plan.k2_dev, SUBS)
    stride = plan.k1_tiles * SUBS
    copies = []
    for slot in range(plan.group):
        part = slot % 2
        base = [b for b in range(plan.group) if b & swap_bit == 0][slot // 2]
        for r in range(plan.rows):
            for k2 in range(0, plan.k2_dev, take):
                for j in range(plan.k1_tiles):
                    lanes = slice(j * LANES, (j + 1) * LANES)
                    a = chunks[base][r, part, k2 : k2 + take, lanes] * scale
                    b = chunks[base + swap_bit][r, part, k2 : k2 + take, lanes] * scale
                    at = (k2 * plan.k1_tiles + j) * SUBS + r
                    tile_ref[slot, pl.ds(at, take, stride=stride), :] = jnp.where(swapped, b, a)
                    tile_ref[slot, pl.ds(at + plan.rows, take, stride=stride), :] = jnp.where(swapped, a, b)
        for f in range(plan.freq_tiles):
            row_ref[slot, :, f * LANES : (f + 1) * LANES] = tile_ref[slot, f * SUBS : (f + 1) * SUBS, :]
        source = inside ^ base
        tile = source // 2 if swap_bit == 1 else source % 2 * 2 + source // 4
        target = out_ref.at[part, pl.ds(pl.multiple_of(tile * SUBS, SUBS), SUBS), :]
        copy = pltpu.make_async_copy(row_ref.at[slot], target, sems.at[slot])
        copy.start()
        copies.append(copy)
    for copy in copies:
        copy.wait()


def along_rows(n_row, value):
    return [lax.ppermute(value, "row", [(i, (i + d) % n_row) for i in range(n_row)]) for d in range(1, n_row)]


def spectra_shapes(plan):
    return [jax.ShapeDtypeStruct((plan.rows, 2, plan.k2_dev, plan.k1), jnp.float32)] * plan.group


def spectra_by_chip(plan, phase_codes, aperture, tile_offsets):
    n_col, n_row = plan.n_col, plan.n_row
    n_chips = n_col // 2
    row_index = lax.axis_index("row").astype(jnp.int32)
    col_index = lax.axis_index("col").astype(jnp.int32)
    smem, vmem, hbm = (pl.BlockSpec(memory_space=m) for m in (pltpu.SMEM, pltpu.VMEM, pl.ANY))
    swap = [(q, q ^ 1) for q in range(n_col)]
    others = along_rows(n_row, tile_offsets)
    near_others = []
    for d in range(1, n_row):
        pairs = [(r * n_col + q, (r + d) % n_row * n_col + (q ^ 1)) for r in range(n_row) for q in range(n_col)]
        near_others.append(lax.ppermute(tile_offsets, ("row", "col"), pairs))
    near = [lax.ppermute(value, "col", swap) for value in (tile_offsets, phase_codes, aperture)]
    alike = min(n_chips, plan.group // 2)
    block = jax.ShapeDtypeStruct((2 * plan.chunk + SUBS, LANES), jnp.float32)
    rows = pl.pallas_call(
        partial(chip_field_kernel, plan),
        out_shape=[block] * alike,
        in_specs=[smem] + [vmem] * (2 * n_row) + [hbm, hbm, vmem, vmem],
        out_specs=[vmem] * alike,
        scratch_shapes=[
            pltpu.VMEM(phase_codes.shape, jnp.int32),
            pltpu.VMEM(aperture.shape, jnp.int32),
            pltpu.VMEM((2, alike * plan.chunk, LANES), jnp.float32),
            pltpu.SemaphoreType.DMA((2,)),
        ],
        compiler_params=pltpu.CompilerParams(vmem_limit_bytes=16 * 2**20),
        name="field",
    )(
        jnp.stack([col_index % 2, col_index // 2, row_index]),
        tile_offsets,
        near[0],
        *others,
        *near_others,
        phase_codes,
        aperture,
        near[1],
        near[2],
    )
    order = CHIP_ORDER + (0,)
    received = [rows[0] if b == 0 else lax.ppermute(rows[b % alike], "col", [(q, q ^ 2 * b) for q in range(n_col)]) for b in order]
    tables = [outer_tables(plan, n_chips), inner_tables(plan), twist_tables(plan)]
    *made, opened = pl.pallas_call(
        partial(chip_transform_kernel, plan, order),
        out_shape=spectra_shapes(plan) + [jax.ShapeDtypeStruct((SUBS, LANES), jnp.float32)],
        in_specs=[smem] + [vmem] * (n_chips + 3),
        out_specs=[vmem] * (plan.group + 1),
        compiler_params=pltpu.CompilerParams(vmem_limit_bytes=24 * 2**20),
        name="transform",
    )(col_index.reshape(1), *received, *tables)
    return made, opened


def spectra_by_device(plan, phase_codes, aperture, tile_offsets):
    n_col, n_row = plan.n_col, plan.n_row
    row_index = lax.axis_index("row")
    col_index = lax.axis_index("col")
    me = col_index.astype(jnp.int32).reshape(1)
    smem = pl.BlockSpec(memory_space=pltpu.SMEM)
    vmem = pl.BlockSpec(memory_space=pltpu.VMEM)
    before = jnp.zeros((1, plan.pupil_dev // TILE_C), jnp.int32)
    for d, other in enumerate(along_rows(n_row, tile_offsets)):
        before = before + jnp.where(row_index > d, jnp.sum(other, axis=0, keepdims=True), 0)
    before = jnp.pad((before & (LEVELS - 1)).astype(jnp.float32), ((0, 0), (0, LANES - before.shape[1])))
    mine = jnp.arange(n_col, dtype=jnp.int32)[:, None] == col_index

    field_rows = plan.row_dev * 2 * plan.lane_parts * plan.n1_dev
    steps = plan.row_dev // TILE_R
    packed, opened = pl.pallas_call(
        partial(field_kernel, plan),
        out_shape=[
            jax.ShapeDtypeStruct((plan.n_groups, field_rows, LANES), jnp.float32),
            jax.ShapeDtypeStruct((SUBS, LANES), jnp.float32),
        ],
        grid=(steps,),
        in_specs=[
            smem,
            pl.BlockSpec((TILE_R, plan.pupil_dev), lambda t: (t, 0)),
            pl.BlockSpec((TILE_R, plan.pupil_dev), lambda t: (t, 0)),
        ],
        out_specs=[
            pl.BlockSpec((plan.n_groups, field_rows // steps, LANES), lambda t: (0, t, 0)),
            pl.BlockSpec((SUBS, LANES), lambda t: (0, 0)),
        ],
        name="field",
    )(tile_offsets, phase_codes, aperture)
    packed = packed.reshape(n_col, plan.chunk, LANES)
    received = lax.all_to_all(packed, "col", split_axis=0, concat_axis=0, tiled=True)

    info = jnp.concatenate([jnp.where(mine, before, 0.0), opened])
    for bit in range(n_col.bit_length() - 1):
        info = info + lax.ppermute(info, "col", [(q, q ^ 1 << bit) for q in range(n_col)])
    tables = [outer_tables(plan, 1), inner_tables(plan), twist_tables(plan)]
    made = pl.pallas_call(
        partial(transform_kernel, plan),
        out_shape=spectra_shapes(plan),
        in_specs=[smem] + [vmem] * 5,
        out_specs=[vmem] * plan.group,
        compiler_params=pltpu.CompilerParams(vmem_limit_bytes=24 * 2**20),
        name="transform",
    )(me, info, received, *tables)
    return made, info[n_col:]


def per_device(phase_codes, aperture, tile_offsets):
    n_col = lax.axis_size("col")
    n_row = lax.axis_size("row")
    plan = Plan(*phase_codes.shape, n_col, n_row)
    by_chip = plan.n1_dev % SUBS == 0 and len(CHIP_ORDER) == n_col // 2 - 1
    spectra = spectra_by_chip if by_chip else spectra_by_device
    made, opened = spectra(plan, phase_codes, aperture, tile_offsets)
    chunks = [lax.ppermute(made[b], "col", [(q, q ^ b) for q in range(n_col)]) for b in ORDER] + [made[0]]
    counts = [opened] + along_rows(n_row, opened)
    smem = pl.BlockSpec(memory_space=pltpu.SMEM)
    vmem = pl.BlockSpec(memory_space=pltpu.VMEM)
    return pl.pallas_call(
        partial(merge_kernel, plan, 2 if by_chip else 1),
        out_shape=jax.ShapeDtypeStruct((2, plan.row_dev, plan.freq_tiles * LANES), jnp.float32),
        in_specs=[smem] + [vmem] * (plan.group + n_row),
        out_specs=pl.BlockSpec(memory_space=pl.ANY),
        scratch_shapes=[
            pltpu.VMEM((plan.group, plan.freq_tiles * SUBS, LANES), jnp.float32),
            pltpu.VMEM((plan.group, SUBS, plan.freq_tiles * LANES), jnp.float32),
            pltpu.SemaphoreType.DMA((plan.group,)),
        ],
        compiler_params=pltpu.CompilerParams(vmem_limit_bytes=24 * 2**20),
        name="merge",
    )(lax.axis_index("col").astype(jnp.int32).reshape(1), *chunks, *counts)


def solution(mesh):
    placed = (P("row", "col"), P("row", "col"), P("row", "col"))
    return jax.shard_map(
        per_device, mesh=mesh, in_specs=placed, out_specs=P(None, "row", "col"), check_vma=False
    )
```

```python
import math
from functools import partial

import jax
import jax.numpy as jnp
import ml_dtypes
import numpy as np
from jax import lax
from jax.experimental import pallas as pl
from jax.experimental.pallas import tpu as pltpu
from jax.sharding import PartitionSpec as P

LEVELS = 4096
TILE_R = 16
TILE_C = 512
LANES = 128
SUBS = 8
INNER = 256
PAD = 4
FINE = 16
ORDER = (6, 4, 2, 7, 5, 3, 1)
SPLITS = (4,)
GROUP = 8


class Plan:
    def __init__(self, row_dev, pupil_dev, n_col, n_row):
        self.row_dev = row_dev
        self.pupil_dev = pupil_dev
        self.n_col = n_col
        self.n_row = n_row
        self.rows_all = row_dev * n_row
        self.group = min(GROUP, n_col)
        self.n_groups = n_col // self.group
        self.rows = row_dev // self.group
        self.n_pupil = pupil_dev * n_col
        self.n_pad = PAD * self.n_pupil
        self.n1 = self.n_pupil // INNER
        self.k1 = PAD * self.n1
        self.n1_dev = pupil_dev // INNER
        self.k2_group = INNER // self.n_groups
        self.k2_dev = INNER // n_col
        self.freq_tiles = PAD * pupil_dev // LANES
        self.k1_tiles = self.k1 // LANES
        self.lane_parts = INNER // LANES
        self.chunk = self.rows * 2 * self.lane_parts * self.n1_dev


def split_bf16(table):
    high = table.astype(ml_dtypes.bfloat16)
    low = (table - high.astype(np.float64)).astype(ml_dtypes.bfloat16)
    return np.stack([high, low])


def outer_tables(plan):
    angle = np.arange(plan.n1)[:, None] * np.arange(plan.k1)[None, :] % plan.k1
    angle = angle * (2.0 * np.pi / plan.k1)
    return split_bf16(np.concatenate([np.cos(angle), np.sin(angle)]))


def inner_tables(plan):
    angle = np.arange(INNER)[:, None] * np.arange(INNER)[None, :] % INNER
    angle = angle * (2.0 * np.pi / INNER)
    table = np.concatenate([np.cos(angle), np.sin(angle)], axis=1)
    return split_bf16(table.reshape(plan.n_col, plan.k2_dev, 2 * INNER))


def twist_tables(plan):
    made = []
    for cells in (np.arange(0, INNER, FINE), np.arange(FINE)):
        angle = cells[:, None] * np.arange(plan.k1)[None, :] * (2.0 * np.pi / plan.n_pad)
        made.extend([np.cos(angle), np.sin(angle)])
    return np.concatenate(made).astype(np.float32)


def unit_phase(code):
    quadrant = (code + LEVELS // 8) >> 10
    rest = (code - (quadrant << 10)).astype(jnp.float32) * (2.0 * math.pi / LEVELS)
    sq = rest * rest
    cos = 1.0 + sq * (-1.0 / 2 + sq * (1.0 / 24 + sq * (-1.0 / 720 + sq * (1.0 / 40320))))
    sin = rest * (1.0 + sq * (-1.0 / 6 + sq * (1.0 / 120 + sq * (-1.0 / 5040 + sq * (1.0 / 362880)))))
    swap = (quadrant & 1) == 1
    minus_cos = ((quadrant + 1) & 2) == 2
    minus_sin = (quadrant & 2) == 2
    return jnp.where(swap, sin, cos), jnp.where(swap, cos, sin), minus_cos, minus_sin


def field_kernel(plan, tiles_ref, codes_ref, mask_ref, out_ref, open_ref):
    step_id = pl.program_id(0)
    pistons = []
    for i in range(plan.pupil_dev // TILE_C):
        piston = jnp.int32(0)
        for k in range(plan.row_dev // TILE_R):
            piston = piston + jnp.where(step_id >= k, tiles_ref[k, i], 0)
        pistons.append(piston)
    stride = 2 * plan.lane_parts * plan.n1_dev
    total = jnp.zeros((SUBS, LANES), jnp.float32)
    for t in range(TILE_R // SUBS):
        for j in range(plan.pupil_dev // LANES):
            rows = slice(t * SUBS, (t + 1) * SUBS)
            lanes = slice(j * LANES, (j + 1) * LANES)
            code = (codes_ref[rows, lanes] + pistons[j * LANES // TILE_C]) & (LEVELS - 1)
            cos, sin, minus_cos, minus_sin = unit_phase(code)
            amplitude = mask_ref[rows, lanes].astype(jnp.float32)
            total = total + amplitude
            real = cos * jnp.where(minus_cos, -amplitude, amplitude)
            imag = sin * jnp.where(minus_sin, -amplitude, amplitude)
            for part, value in enumerate((real, imag)):
                start = (part * plan.lane_parts + j % plan.lane_parts) * plan.n1_dev + j // plan.lane_parts
                for g in range(plan.n_groups):
                    out_ref[g, pl.ds(t * SUBS * stride + start, SUBS, stride=stride), :] = value

    @pl.when(step_id == 0)
    def _():
        open_ref[...] = total

    @pl.when(step_id > 0)
    def _():
        open_ref[...] = open_ref[...] + total


def transform_kernel(plan, first, rows, me_ref, info_ref, x_ref, outer_ref, inner_ref, twist_ref, *refs):
    chunk_row = plan.chunk // plan.rows
    me = me_ref[0]

    def outer(a, b):
        return lax.dot_general(a, b, (((0,), (0,)), ((), ())), preferred_element_type=jnp.float32)

    def inner(a, b):
        return jnp.dot(a, b, preferred_element_type=jnp.float32)

    info = info_ref[: plan.n_col]
    info = jnp.broadcast_to(info[:, None, :], (plan.n_col, plan.n1_dev, LANES)).reshape(plan.n1, LANES)
    tile = lax.broadcasted_iota(jnp.int32, info.shape, 0) % plan.n1_dev * INNER // TILE_C
    own = lax.broadcasted_iota(jnp.int32, info.shape, 1) == tile
    before = jnp.sum(jnp.where(own, info, 0.0), axis=1, keepdims=True).astype(jnp.int32)
    turn_cos, turn_sin, minus_cos, minus_sin = unit_phase(before)
    turn_cos = jnp.where(minus_cos, -turn_cos, turn_cos)
    turn_sin = jnp.where(minus_sin, -turn_sin, turn_sin)
    n1, k2_dev = plan.n1, plan.k2_dev
    w1, w2 = [], []
    for s in range(2):
        cos, sin = outer_ref[s, :n1], outer_ref[s, n1:]
        w1.append(jnp.concatenate([jnp.concatenate([cos, sin]), jnp.concatenate([-sin, cos])], axis=1))
        blocks = []
        for b in range(plan.group):
            both = inner_ref[s, me ^ b]
            cos, sin = both[:, :INNER], both[:, INNER:]
            blocks.append(both)
            blocks.append(jnp.concatenate([-sin, cos], axis=1))
        w2.append(jnp.concatenate(blocks))
    size = 2 * k2_dev
    count = INNER // FINE
    fine_cos, fine_sin = twist_ref[2 * count : 2 * count + FINE], twist_ref[2 * count + FINE :]
    tc, ts = [], []
    for a in range(count):
        cos, sin = twist_ref[a : a + 1], twist_ref[count + a : count + a + 1]
        tc.append(cos * fine_cos - sin * fine_sin)
        ts.append(sin * fine_cos + cos * fine_sin)
    tc, ts = jnp.concatenate(tc), jnp.concatenate(ts)
    xs = []
    for r in range(rows):
        halves = []
        for part in range(2):
            pieces = []
            for lt in range(plan.lane_parts):
                at = (first + r) * chunk_row + (part * plan.lane_parts + lt) * plan.n1_dev
                pieces.append(x_ref[:, at : at + plan.n1_dev, :].reshape(plan.n1, LANES))
            halves.append(jnp.concatenate(pieces, axis=1))
        real, imag = halves
        xs.append(jnp.concatenate([real * turn_cos - imag * turn_sin, real * turn_sin + imag * turn_cos], axis=0))
    x = jnp.concatenate(xs, axis=1)
    xh = x.astype(jnp.bfloat16)
    xl = (x - xh.astype(jnp.float32)).astype(jnp.bfloat16)
    y = outer(jnp.concatenate([xh, xl, xh]), jnp.concatenate([w1[0], w1[0], w1[1]]))
    fs = []
    for r in range(rows):
        yr, yi = y[r * INNER : (r + 1) * INNER, : plan.k1], y[r * INNER : (r + 1) * INNER, plan.k1 :]
        fs.append(jnp.concatenate([yr * tc + yi * ts, yi * tc - yr * ts], axis=0))
    f = jnp.concatenate(fs, axis=1)
    fh = f.astype(jnp.bfloat16)
    fl = (f - fh.astype(jnp.float32)).astype(jnp.bfloat16)
    z = inner(jnp.concatenate([w2[0], w2[1], w2[0]], axis=1), jnp.concatenate([fh, fh, fl]))
    for r in range(rows):
        for b in range(plan.group):
            refs[b][r] = z[b * size : (b + 1) * size, r * plan.k1 : (r + 1) * plan.k1].reshape(2, plan.k2_dev, plan.k1)


def merge_kernel(plan, splits, me_ref, *refs):
    n = len(splits)
    chunks = []
    for i in range(n):
        given = refs[i * plan.group : (i + 1) * plan.group]
        chunks.append([given[(ORDER + (0,)).index(b)] for b in range(plan.group)])
    counts = refs[n * plan.group : n * plan.group + plan.n_row]
    out_ref, tile_ref, row_ref, sems = refs[n * plan.group + plan.n_row :]
    total = counts[0][...]
    for other in counts[1:]:
        total = total + other[...]
    total = jnp.sum(jnp.sum(total, axis=0, keepdims=True), axis=1, keepdims=True)
    scale = jnp.sqrt(float(plan.rows_all) / total)
    inside = lax.rem(me_ref[0], plan.group)
    swapped = lax.rem(inside, 2) == 1
    take = min(plan.k2_dev, SUBS)
    stride = plan.k1_tiles * SUBS
    copies = []
    for pair in range(plan.group // 2):
        for part in range(2):
            slot = pair * 2 + part
            for i, rows in enumerate(splits):
                for r in range(rows):
                    for k2 in range(0, plan.k2_dev, take):
                        for j in range(plan.k1_tiles):
                            lanes = slice(j * LANES, (j + 1) * LANES)
                            a = chunks[i][2 * pair][r, part, k2 : k2 + take, lanes] * scale
                            b = chunks[i][2 * pair + 1][r, part, k2 : k2 + take, lanes] * scale
                            at = (k2 * plan.k1_tiles + j) * SUBS + sum(splits[:i]) + r
                            tile_ref[slot, pl.ds(at, take, stride=stride), :] = jnp.where(swapped, b, a)
                            tile_ref[slot, pl.ds(at + plan.rows, take, stride=stride), :] = jnp.where(swapped, a, b)
            for f in range(plan.freq_tiles):
                row_ref[slot, :, f * LANES : (f + 1) * LANES] = tile_ref[slot, f * SUBS : (f + 1) * SUBS, :]
            tile = lax.div(inside, 2) ^ pair
            target = out_ref.at[part, pl.ds(pl.multiple_of(tile * SUBS, SUBS), SUBS), :]
            copy = pltpu.make_async_copy(row_ref.at[slot], target, sems.at[slot])
            copy.start()
            copies.append(copy)
    for copy in copies:
        copy.wait()


def per_device(phase_codes, aperture, tile_offsets):
    n_col = lax.axis_size("col")
    n_row = lax.axis_size("row")
    plan = Plan(*phase_codes.shape, n_col, n_row)
    row_index = lax.axis_index("row")
    col_index = lax.axis_index("col")
    me = col_index.astype(jnp.int32).reshape(1)

    def along_rows(value):
        return [lax.ppermute(value, "row", [(i, (i + d) % n_row) for i in range(n_row)]) for d in range(1, n_row)]

    smem = pl.BlockSpec(memory_space=pltpu.SMEM)
    vmem = pl.BlockSpec(memory_space=pltpu.VMEM)
    before = jnp.zeros((1, plan.pupil_dev // TILE_C), jnp.int32)
    for d, other in enumerate(along_rows(tile_offsets)):
        before = before + jnp.where(row_index > d, jnp.sum(other, axis=0, keepdims=True), 0)
    before = jnp.pad((before & (LEVELS - 1)).astype(jnp.float32), ((0, 0), (0, LANES - before.shape[1])))
    mine = jnp.arange(n_col, dtype=jnp.int32)[:, None] == col_index

    field_rows = plan.row_dev * 2 * plan.lane_parts * plan.n1_dev
    steps = plan.row_dev // TILE_R
    packed, opened = pl.pallas_call(
        partial(field_kernel, plan),
        out_shape=[
            jax.ShapeDtypeStruct((plan.n_groups, field_rows, LANES), jnp.float32),
            jax.ShapeDtypeStruct((SUBS, LANES), jnp.float32),
        ],
        grid=(steps,),
        in_specs=[
            smem,
            pl.BlockSpec((TILE_R, plan.pupil_dev), lambda t: (t, 0)),
            pl.BlockSpec((TILE_R, plan.pupil_dev), lambda t: (t, 0)),
        ],
        out_specs=[
            pl.BlockSpec((plan.n_groups, field_rows // steps, LANES), lambda t: (0, t, 0)),
            pl.BlockSpec((SUBS, LANES), lambda t: (0, 0)),
        ],
        name="field",
    )(tile_offsets, phase_codes, aperture)
    packed = packed.reshape(n_col, plan.chunk, LANES)
    received = lax.all_to_all(packed, "col", split_axis=0, concat_axis=0, tiled=True)

    info = jnp.concatenate([jnp.where(mine, before, 0.0), opened])
    for bit in range(n_col.bit_length() - 1):
        info = info + lax.ppermute(info, "col", [(q, q ^ 1 << bit) for q in range(n_col)])
    opened = info[n_col:]
    counts = [opened] + along_rows(opened)

    tables = [outer_tables(plan), inner_tables(plan), twist_tables(plan)]
    splits = SPLITS if sum(SPLITS) == plan.rows else (plan.rows,)
    chunks = []
    for i, rows in enumerate(splits):
        shapes = [jax.ShapeDtypeStruct((rows, 2, plan.k2_dev, plan.k1), jnp.float32)] * plan.group
        made = pl.pallas_call(
            partial(transform_kernel, plan, sum(splits[:i]), rows),
            out_shape=shapes,
            in_specs=[smem] + [vmem] * 5,
            out_specs=[vmem] * len(shapes),
            compiler_params=pltpu.CompilerParams(vmem_limit_bytes=24 * 2**20),
            name="transform",
        )(me, info, received, *tables)
        sent = {b: lax.ppermute(made[b], "col", [(q, q ^ b) for q in range(n_col)]) for b in ORDER}
        chunks.append([sent[b] for b in ORDER] + [made[0]])

    slots = plan.group
    return pl.pallas_call(
        partial(merge_kernel, plan, splits),
        out_shape=jax.ShapeDtypeStruct((2, plan.row_dev, plan.freq_tiles * LANES), jnp.float32),
        in_specs=[smem] + [vmem] * (len(splits) * plan.group + n_row),
        out_specs=pl.BlockSpec(memory_space=pl.ANY),
        scratch_shapes=[
            pltpu.VMEM((slots, plan.freq_tiles * SUBS, LANES), jnp.float32),
            pltpu.VMEM((slots, SUBS, plan.freq_tiles * LANES), jnp.float32),
            pltpu.SemaphoreType.DMA((slots,)),
        ],
        compiler_params=pltpu.CompilerParams(vmem_limit_bytes=24 * 2**20),
        name="merge",
    )(me, *[chunk for part in chunks for chunk in part], *counts)


def solution(mesh):
    placed = (P("row", "col"), P("row", "col"), P("row", "col"))
    return jax.shard_map(
        per_device, mesh=mesh, in_specs=placed, out_specs=P(None, "row", "col"), check_vma=False
    )
```

```python
import math
from functools import partial

import jax
import jax.numpy as jnp
import ml_dtypes
import numpy as np
from jax import lax
from jax.experimental import pallas as pl
from jax.experimental.pallas import tpu as pltpu
from jax.sharding import PartitionSpec as P

LEVELS = 4096
TILE_R = 16
TILE_C = 512
LANES = 128
SUBS = 8
INNER = 256
PAD = 4
FINE = 16
CHIP_ORDER = (4, 1, 5, 2, 6, 3, 7)
ORDER = (6, 4, 2, 7, 5, 3, 1)
GROUP = 8


class Plan:
    def __init__(self, row_dev, pupil_dev, n_col, n_row):
        self.row_dev = row_dev
        self.pupil_dev = pupil_dev
        self.n_col = n_col
        self.n_row = n_row
        self.rows_all = row_dev * n_row
        self.group = min(GROUP, n_col)
        self.n_groups = n_col // self.group
        self.rows = row_dev // self.group
        self.n_pupil = pupil_dev * n_col
        self.n_pad = PAD * self.n_pupil
        self.n1 = self.n_pupil // INNER
        self.k1 = PAD * self.n1
        self.n1_dev = pupil_dev // INNER
        self.k2_group = INNER // self.n_groups
        self.k2_dev = INNER // n_col
        self.freq_tiles = PAD * pupil_dev // LANES
        self.k1_tiles = self.k1 // LANES
        self.lane_parts = INNER // LANES
        self.chunk = self.rows * 2 * self.lane_parts * self.n1_dev


def split_bf16(table):
    high = table.astype(ml_dtypes.bfloat16)
    low = (table - high.astype(np.float64)).astype(ml_dtypes.bfloat16)
    return np.stack([high, low])


def outer_tables(plan, blocks):
    angle = np.arange(plan.n1)[:, None] * np.arange(plan.k1)[None, :] % plan.k1
    angle = angle * (2.0 * np.pi / plan.k1)
    table = np.stack([np.cos(angle), np.sin(angle)]).reshape(2, blocks, plan.n1 // blocks, plan.k1)
    return split_bf16(table.transpose(1, 0, 2, 3))


def inner_tables(plan):
    angle = np.arange(INNER)[:, None] * np.arange(INNER)[None, :] % INNER
    angle = angle * (2.0 * np.pi / INNER)
    table = np.concatenate([np.cos(angle), np.sin(angle)], axis=1)
    return split_bf16(table.reshape(plan.n_col, plan.k2_dev, 2 * INNER))


def twist_tables(plan):
    made = []
    for cells in (np.arange(0, INNER, FINE), np.arange(FINE)):
        angle = cells[:, None] * np.arange(plan.k1)[None, :] * (2.0 * np.pi / plan.n_pad)
        made.extend([np.cos(angle), np.sin(angle)])
    return np.concatenate(made).astype(np.float32)


def unit_phase(code):
    quadrant = (code + LEVELS // 8) >> 10
    rest = (code - (quadrant << 10)).astype(jnp.float32) * (2.0 * math.pi / LEVELS)
    sq = rest * rest
    cos = 1.0 + sq * (-1.0 / 2 + sq * (1.0 / 24 + sq * (-1.0 / 720 + sq * (1.0 / 40320))))
    sin = rest * (1.0 + sq * (-1.0 / 6 + sq * (1.0 / 120 + sq * (-1.0 / 5040 + sq * (1.0 / 362880)))))
    swap = (quadrant & 1) == 1
    minus_cos = ((quadrant + 1) & 2) == 2
    minus_sin = (quadrant & 2) == 2
    return jnp.where(swap, sin, cos), jnp.where(swap, cos, sin), minus_cos, minus_sin


def field_kernel(plan, tiles_ref, codes_ref, mask_ref, out_ref, open_ref):
    step_id = pl.program_id(0)
    pistons = []
    for i in range(plan.pupil_dev // TILE_C):
        piston = jnp.int32(0)
        for k in range(plan.row_dev // TILE_R):
            piston = piston + jnp.where(step_id >= k, tiles_ref[k, i], 0)
        pistons.append(piston)
    stride = 2 * plan.lane_parts * plan.n1_dev
    total = jnp.zeros((SUBS, LANES), jnp.float32)
    for t in range(TILE_R // SUBS):
        for j in range(plan.pupil_dev // LANES):
            rows = slice(t * SUBS, (t + 1) * SUBS)
            lanes = slice(j * LANES, (j + 1) * LANES)
            code = (codes_ref[rows, lanes] + pistons[j * LANES // TILE_C]) & (LEVELS - 1)
            cos, sin, minus_cos, minus_sin = unit_phase(code)
            amplitude = mask_ref[rows, lanes].astype(jnp.float32)
            total = total + amplitude
            real = cos * jnp.where(minus_cos, -amplitude, amplitude)
            imag = sin * jnp.where(minus_sin, -amplitude, amplitude)
            for part, value in enumerate((real, imag)):
                start = (part * plan.lane_parts + j % plan.lane_parts) * plan.n1_dev + j // plan.lane_parts
                for g in range(plan.n_groups):
                    out_ref[g, pl.ds(t * SUBS * stride + start, SUBS, stride=stride), :] = value

    @pl.when(step_id == 0)
    def _():
        open_ref[...] = total

    @pl.when(step_id > 0)
    def _():
        open_ref[...] = open_ref[...] + total


def own_kernel(plan, me_ref, tiles_ref, codes_ref, mask_ref, code_ref, kept_ref, open_ref):
    half = plan.row_dev // 2
    first = pl.multiple_of(me_ref[0] * half, half)
    total = jnp.zeros((SUBS, LANES), jnp.int32)
    for t in range(plan.row_dev // SUBS):
        for j in range(plan.pupil_dev // LANES):
            total = total + mask_ref[t * SUBS : (t + 1) * SUBS, j * LANES : (j + 1) * LANES]
    open_ref[...] = total
    for i in range(plan.pupil_dev // TILE_C):
        lanes = slice(i * TILE_C, (i + 1) * TILE_C)
        piston = jnp.int32(0)
        for k in range(plan.row_dev // TILE_R):
            piston = piston + jnp.where(first >= k * TILE_R, tiles_ref[k, i], 0)
        code_ref[:, lanes] = codes_ref[:, lanes] + piston
    kept_ref[...] = mask_ref[pl.ds(first, half), :]


def chip_field_kernel(plan, me_ref, *refs):
    n_other = plan.n_row - 1
    others, refs = (refs[:n_other], refs[n_other : 2 * n_other]), refs[2 * n_other :]
    near_tiles_ref, own_codes_ref, own_mask_ref, open_ref, near_codes_ref, near_mask_ref = refs[:6]
    outs, made_ref = refs[6:-1], refs[-1]
    core, chip, row = me_ref[0], me_ref[1], me_ref[2]
    half = plan.row_dev // 2
    first = pl.multiple_of(core * half, half)
    total = open_ref[...]
    for t in range(plan.row_dev // SUBS):
        for j in range(plan.pupil_dev // LANES):
            total = total + near_mask_ref[t * SUBS : (t + 1) * SUBS, j * LANES : (j + 1) * LANES]
    total = total.astype(jnp.float32)
    stride = 2 * plan.lane_parts * plan.n1_dev
    for owner in range(2):
        before = jnp.zeros((1, plan.pupil_dev // TILE_C), jnp.int32)
        for d, other in enumerate(others[owner]):
            before = before + jnp.where(row > d, jnp.sum(other[...], axis=0, keepdims=True), 0)
        if owner == 1:
            for k in range(plan.row_dev // TILE_R):
                before = before + jnp.where(first >= k * TILE_R, near_tiles_ref[k : k + 1], 0)
        codes, mask = ((own_codes_ref, own_mask_ref), (near_codes_ref, near_mask_ref))[owner]
        for t in range(half // SUBS):
            rows = pl.ds(t * SUBS, SUBS) if owner == 0 else pl.ds(pl.multiple_of(first + t * SUBS, SUBS), SUBS)
            for j in range(plan.pupil_dev // LANES):
                lanes = slice(j * LANES, (j + 1) * LANES)
                column = j * LANES // TILE_C
                piston = jnp.broadcast_to(before[:, column : column + 1], (SUBS, LANES))
                cos, sin, minus_cos, minus_sin = unit_phase((codes[rows, lanes] + piston) & (LEVELS - 1))
                amplitude = mask[rows, lanes].astype(jnp.float32)
                real = cos * jnp.where(minus_cos, -amplitude, amplitude)
                imag = sin * jnp.where(minus_sin, -amplitude, amplitude)
                for part, value in enumerate((real, imag)):
                    start = (part * plan.lane_parts + j % plan.lane_parts) * plan.n1_dev + j // plan.lane_parts
                    made_ref[owner, pl.ds(t * SUBS * stride + start, SUBS, stride=stride), :] = value
    own_rows = lax.rem(chip, plan.group // 2)
    for b, out in enumerate(outs):
        source = pl.multiple_of((own_rows ^ b % (plan.group // 2)) * plan.chunk, plan.chunk)
        for i in range(plan.chunk // plan.n1_dev):
            for side in range(2):
                block = made_ref[side ^ core, pl.ds(pl.multiple_of(source + i * plan.n1_dev, plan.n1_dev), plan.n1_dev), :]
                out[(2 * i + side) * plan.n1_dev : (2 * i + side + 1) * plan.n1_dev, :] = block
        out[2 * plan.chunk :, :] = total


def tables_kernel(plan, blocks, me_ref, outer_ref, inner_ref, twist_ref, w1_ref, w2_ref, turn_ref):
    me = me_ref[0]
    w1, w2 = [], []
    for s in range(2):
        rows = [outer_ref[s, (me >> 1) ^ b if blocks > 1 else 0] for b in range(blocks)]
        cos, sin = (jnp.concatenate([both[i] for both in rows]) for i in range(2))
        w1.append(jnp.concatenate([jnp.concatenate([cos, sin]), jnp.concatenate([-sin, cos])], axis=1))
        parts = []
        for b in range(plan.group):
            both = inner_ref[s, me ^ b]
            parts.append(both)
            parts.append(jnp.concatenate([-both[:, INNER:], both[:, :INNER]], axis=1))
        w2.append(jnp.concatenate(parts))
    w1_ref[...] = jnp.concatenate([w1[0], w1[0], w1[1]])
    w2_ref[...] = jnp.concatenate([w2[0], w2[1], w2[0]], axis=1)
    turn_ref[...] = twist_ref[...]


def chip_transform_kernel(plan, order, *refs):
    n_chips = plan.n_col // 2
    chunks = [refs[order.index(b)] for b in range(n_chips)]
    tables, outs, count_ref = refs[n_chips : n_chips + 3], refs[n_chips + 3 : -1], refs[-1]
    count = chunks[0][2 * plan.chunk :, :]
    for chunk in chunks[1:]:
        count = count + chunk[2 * plan.chunk :, :]
    count_ref[...] = count
    n1_chip = 2 * plan.n1_dev

    def part_of(r, part):
        pieces = []
        for lt in range(plan.lane_parts):
            at = ((r * 2 + part) * plan.lane_parts + lt) * n1_chip
            pieces.append(jnp.concatenate([chunk[at : at + n1_chip, :] for chunk in chunks]))
        return jnp.concatenate(pieces, axis=1)

    fields = [jnp.concatenate([part_of(r, 0), part_of(r, 1)]) for r in range(plan.rows)]
    transform_rows(plan, fields, tables, outs)


def transform_kernel(plan, info_ref, x_ref, *refs):
    chunk_row = plan.chunk // plan.rows
    info = info_ref[: plan.n_col]
    info = jnp.broadcast_to(info[:, None, :], (plan.n_col, plan.n1_dev, LANES)).reshape(plan.n1, LANES)
    tile = lax.broadcasted_iota(jnp.int32, info.shape, 0) % plan.n1_dev * INNER // TILE_C
    own = lax.broadcasted_iota(jnp.int32, info.shape, 1) == tile
    before = jnp.sum(jnp.where(own, info, 0.0), axis=1, keepdims=True).astype(jnp.int32)
    turn_cos, turn_sin, minus_cos, minus_sin = unit_phase(before)
    turn_cos = jnp.where(minus_cos, -turn_cos, turn_cos)
    turn_sin = jnp.where(minus_sin, -turn_sin, turn_sin)

    def field_of(r):
        halves = []
        for part in range(2):
            pieces = []
            for lt in range(plan.lane_parts):
                at = r * chunk_row + (part * plan.lane_parts + lt) * plan.n1_dev
                pieces.append(x_ref[:, at : at + plan.n1_dev, :].reshape(plan.n1, LANES))
            halves.append(jnp.concatenate(pieces, axis=1))
        real, imag = halves
        return jnp.concatenate([real * turn_cos - imag * turn_sin, real * turn_sin + imag * turn_cos], axis=0)

    transform_rows(plan, [field_of(r) for r in range(plan.rows)], refs[:3], refs[3:])


def transform_rows(plan, fields, tables, outs):
    w1_ref, w2_ref, turn_ref = tables
    size = 2 * plan.k2_dev
    x = jnp.concatenate(fields, axis=1)
    xh = x.astype(jnp.bfloat16)
    xl = (x - xh.astype(jnp.float32)).astype(jnp.bfloat16)
    y = lax.dot_general(
        jnp.concatenate([xh, xl, xh]), w1_ref[...], (((0,), (0,)), ((), ())), preferred_element_type=jnp.float32
    )
    tc, ts = [], []
    count = INNER // FINE
    fine_cos, fine_sin = turn_ref[2 * count : 2 * count + FINE], turn_ref[2 * count + FINE :]
    for a in range(count):
        cos, sin = turn_ref[a : a + 1], turn_ref[count + a : count + a + 1]
        tc.append(cos * fine_cos - sin * fine_sin)
        ts.append(sin * fine_cos + cos * fine_sin)
    tc, ts = jnp.concatenate(tc), jnp.concatenate(ts)
    fs = []
    for r in range(plan.rows):
        yr, yi = y[r * INNER : (r + 1) * INNER, : plan.k1], y[r * INNER : (r + 1) * INNER, plan.k1 :]
        fs.append(jnp.concatenate([yr * tc + yi * ts, yi * tc - yr * ts], axis=0))
    f = jnp.concatenate(fs, axis=1)
    fh = f.astype(jnp.bfloat16)
    fl = (f - fh.astype(jnp.float32)).astype(jnp.bfloat16)
    z = jnp.dot(w2_ref[...], jnp.concatenate([fh, fh, fl]), preferred_element_type=jnp.float32)
    for r in range(plan.rows):
        for b in range(plan.group):
            outs[b][r] = z[b * size : (b + 1) * size, r * plan.k1 : (r + 1) * plan.k1].reshape(2, plan.k2_dev, plan.k1)


def merge_kernel(plan, swap_bit, me_ref, *refs):
    chunks = [refs[(ORDER + (0,)).index(b)] for b in range(plan.group)]
    counts = refs[plan.group : plan.group + plan.n_row]
    out_ref, tile_ref, sems = refs[plan.group + plan.n_row :]
    total = counts[0][...]
    for other in counts[1:]:
        total = total + other[...]
    total = jnp.sum(jnp.sum(total, axis=0, keepdims=True), axis=1, keepdims=True)
    scale = jnp.sqrt(float(plan.rows_all) / total)
    inside = lax.rem(me_ref[0], plan.group)
    swapped = lax.rem(inside // swap_bit, 2) == 1
    take = min(plan.k2_dev, SUBS)
    stride = plan.k1_tiles * SUBS
    copies = []
    for slot in range(plan.group):
        part = slot % 2
        base = [b for b in range(plan.group) if b & swap_bit == 0][slot // 2]
        for r in range(plan.rows):
            for k2 in range(0, plan.k2_dev, take):
                for j in range(plan.k1_tiles):
                    lanes = slice(j * LANES, (j + 1) * LANES)
                    a = chunks[base][r, part, k2 : k2 + take, lanes] * scale
                    b = chunks[base + swap_bit][r, part, k2 : k2 + take, lanes] * scale
                    at = (k2 * plan.k1_tiles + j) * SUBS + r
                    tile_ref[slot, pl.ds(at, take, stride=stride), :] = jnp.where(swapped, b, a)
                    tile_ref[slot, pl.ds(at + plan.rows, take, stride=stride), :] = jnp.where(swapped, a, b)
        source = inside ^ base
        tile = source // 2 if swap_bit == 1 else source % 2 * 2 + source // 4
        copy = pltpu.make_async_copy(tile_ref.at[slot], out_ref.at[part, tile], sems.at[slot])
        copy.start()
        copies.append(copy)
    for copy in copies:
        copy.wait()


def along_rows(n_row, value):
    return [lax.ppermute(value, "row", [(i, (i + d) % n_row) for i in range(n_row)]) for d in range(1, n_row)]


def spectra_shapes(plan):
    return [jax.ShapeDtypeStruct((plan.rows, 2, plan.k2_dev, plan.k1), jnp.float32)] * plan.group


def ready_tables(plan, me, blocks):
    smem, vmem = pl.BlockSpec(memory_space=pltpu.SMEM), pl.BlockSpec(memory_space=pltpu.VMEM)
    return pl.pallas_call(
        partial(tables_kernel, plan, blocks),
        out_shape=[
            jax.ShapeDtypeStruct((6 * plan.n1, 2 * plan.k1), jnp.bfloat16),
            jax.ShapeDtypeStruct((2 * plan.group * plan.k2_dev, 6 * INNER), jnp.bfloat16),
            jax.ShapeDtypeStruct((2 * (INNER // FINE + FINE), plan.k1), jnp.float32),
        ],
        in_specs=[smem] + [vmem] * 3,
        out_specs=[vmem] * 3,
        compiler_params=pltpu.CompilerParams(vmem_limit_bytes=24 * 2**20),
        name="tables",
    )(me, outer_tables(plan, blocks), inner_tables(plan), twist_tables(plan))


def spectra_by_chip(plan, phase_codes, aperture, tile_offsets):
    n_col, n_row = plan.n_col, plan.n_row
    n_chips = n_col // 2
    half = plan.row_dev // 2
    row_index = lax.axis_index("row").astype(jnp.int32)
    col_index = lax.axis_index("col").astype(jnp.int32)
    smem, vmem = pl.BlockSpec(memory_space=pltpu.SMEM), pl.BlockSpec(memory_space=pltpu.VMEM)
    swap = [(q, q ^ 1) for q in range(n_col)]
    others = along_rows(n_row, tile_offsets)
    near_others = []
    for d in range(1, n_row):
        pairs = [(r * n_col + q, (r + d) % n_row * n_col + (q ^ 1)) for r in range(n_row) for q in range(n_col)]
        near_others.append(lax.ppermute(tile_offsets, ("row", "col"), pairs))
    near = [lax.ppermute(value, "col", swap) for value in (tile_offsets, phase_codes, aperture)]
    place = jnp.stack([col_index % 2, col_index // 2, row_index])
    own = pl.pallas_call(
        partial(own_kernel, plan),
        out_shape=[jax.ShapeDtypeStruct((half, plan.pupil_dev), jnp.int32)] * 2
        + [jax.ShapeDtypeStruct((SUBS, LANES), jnp.int32)],
        grid_spec=pltpu.PrefetchScalarGridSpec(
            num_scalar_prefetch=1,
            grid=(1,),
            in_specs=[
                smem,
                pl.BlockSpec((half, plan.pupil_dev), lambda i, p: (p[0], 0)),
                pl.BlockSpec((plan.row_dev, plan.pupil_dev), lambda i, p: (0, 0)),
            ],
            out_specs=[vmem] * 3,
        ),
        compiler_params=pltpu.CompilerParams(vmem_limit_bytes=16 * 2**20),
        name="own",
    )(place, tile_offsets, phase_codes, aperture)
    block = jax.ShapeDtypeStruct((2 * plan.chunk + SUBS, LANES), jnp.float32)
    rows = pl.pallas_call(
        partial(chip_field_kernel, plan),
        out_shape=[block] * n_chips,
        in_specs=[smem] + [vmem] * (2 * n_row + 4),
        out_specs=[vmem] * n_chips,
        scratch_shapes=[pltpu.VMEM((2, half * plan.chunk // plan.rows, LANES), jnp.float32)],
        compiler_params=pltpu.CompilerParams(vmem_limit_bytes=16 * 2**20),
        name="field",
    )(place, *others, *near_others, near[0], *own, near[1], near[2])
    order = CHIP_ORDER + (0,)
    received = [rows[0] if b == 0 else lax.ppermute(rows[b], "col", [(q, q ^ 2 * b) for q in range(n_col)]) for b in order]
    *made, opened = pl.pallas_call(
        partial(chip_transform_kernel, plan, order),
        out_shape=spectra_shapes(plan) + [jax.ShapeDtypeStruct((SUBS, LANES), jnp.float32)],
        in_specs=[vmem] * (n_chips + 3),
        out_specs=[vmem] * (plan.group + 1),
        compiler_params=pltpu.CompilerParams(vmem_limit_bytes=24 * 2**20),
        name="transform",
    )(*received, *ready_tables(plan, col_index.reshape(1), n_chips))
    return made, opened


def spectra_by_device(plan, phase_codes, aperture, tile_offsets):
    n_col, n_row = plan.n_col, plan.n_row
    row_index = lax.axis_index("row")
    col_index = lax.axis_index("col")
    me = col_index.astype(jnp.int32).reshape(1)
    smem = pl.BlockSpec(memory_space=pltpu.SMEM)
    vmem = pl.BlockSpec(memory_space=pltpu.VMEM)
    before = jnp.zeros((1, plan.pupil_dev // TILE_C), jnp.int32)
    for d, other in enumerate(along_rows(n_row, tile_offsets)):
        before = before + jnp.where(row_index > d, jnp.sum(other, axis=0, keepdims=True), 0)
    before = jnp.pad((before & (LEVELS - 1)).astype(jnp.float32), ((0, 0), (0, LANES - before.shape[1])))
    mine = jnp.arange(n_col, dtype=jnp.int32)[:, None] == col_index

    field_rows = plan.row_dev * 2 * plan.lane_parts * plan.n1_dev
    steps = plan.row_dev // TILE_R
    packed, opened = pl.pallas_call(
        partial(field_kernel, plan),
        out_shape=[
            jax.ShapeDtypeStruct((plan.n_groups, field_rows, LANES), jnp.float32),
            jax.ShapeDtypeStruct((SUBS, LANES), jnp.float32),
        ],
        grid=(steps,),
        in_specs=[
            smem,
            pl.BlockSpec((TILE_R, plan.pupil_dev), lambda t: (t, 0)),
            pl.BlockSpec((TILE_R, plan.pupil_dev), lambda t: (t, 0)),
        ],
        out_specs=[
            pl.BlockSpec((plan.n_groups, field_rows // steps, LANES), lambda t: (0, t, 0)),
            pl.BlockSpec((SUBS, LANES), lambda t: (0, 0)),
        ],
        name="field",
    )(tile_offsets, phase_codes, aperture)
    packed = packed.reshape(n_col, plan.chunk, LANES)
    received = lax.all_to_all(packed, "col", split_axis=0, concat_axis=0, tiled=True)

    info = jnp.concatenate([jnp.where(mine, before, 0.0), opened])
    for bit in range(n_col.bit_length() - 1):
        info = info + lax.ppermute(info, "col", [(q, q ^ 1 << bit) for q in range(n_col)])
    made = pl.pallas_call(
        partial(transform_kernel, plan),
        out_shape=spectra_shapes(plan),
        in_specs=[vmem] * 5,
        out_specs=[vmem] * plan.group,
        compiler_params=pltpu.CompilerParams(vmem_limit_bytes=24 * 2**20),
        name="transform",
    )(info, received, *ready_tables(plan, me, 1))
    return made, info[n_col:]


def per_device(phase_codes, aperture, tile_offsets):
    n_col = lax.axis_size("col")
    n_row = lax.axis_size("row")
    plan = Plan(*phase_codes.shape, n_col, n_row)
    by_chip = plan.n1_dev % SUBS == 0 and len(CHIP_ORDER) == n_col // 2 - 1
    spectra = spectra_by_chip if by_chip else spectra_by_device
    made, opened = spectra(plan, phase_codes, aperture, tile_offsets)
    chunks = [lax.ppermute(made[b], "col", [(q, q ^ b) for q in range(n_col)]) for b in ORDER] + [made[0]]
    opened, chunks[2] = lax.optimization_barrier((opened, chunks[2]))
    counts = [opened] + along_rows(n_row, opened)
    smem = pl.BlockSpec(memory_space=pltpu.SMEM)
    vmem = pl.BlockSpec(memory_space=pltpu.VMEM)
    tiles = plan.row_dev // SUBS
    out = pl.pallas_call(
        partial(merge_kernel, plan, 2 if by_chip else 1),
        out_shape=jax.ShapeDtypeStruct((2, tiles, plan.freq_tiles * SUBS, LANES), jnp.float32),
        in_specs=[smem] + [vmem] * (plan.group + n_row),
        out_specs=pl.BlockSpec(memory_space=pl.ANY),
        scratch_shapes=[
            pltpu.VMEM((plan.group, plan.freq_tiles * SUBS, LANES), jnp.float32),
            pltpu.SemaphoreType.DMA((plan.group,)),
        ],
        compiler_params=pltpu.CompilerParams(vmem_limit_bytes=24 * 2**20),
        name="merge",
    )(lax.axis_index("col").astype(jnp.int32).reshape(1), *chunks, *counts)
    out = out.reshape(2, tiles, plan.freq_tiles, SUBS, LANES).transpose(0, 1, 3, 2, 4)
    return out.reshape(2, plan.row_dev, plan.freq_tiles * LANES)


def solution(mesh):
    placed = (P("row", "col"), P("row", "col"), P("row", "col"))
    return jax.shard_map(
        per_device, mesh=mesh, in_specs=placed, out_specs=P(None, "row", "col"), check_vma=False
    )
```

```python
import math
from functools import partial

import jax
import jax.numpy as jnp
import ml_dtypes
import numpy as np
from jax import lax
from jax.experimental import pallas as pl
from jax.experimental.pallas import tpu as pltpu
from jax.sharding import PartitionSpec as P

LEVELS = 4096
TILE_R = 16
TILE_C = 512
LANES = 128
SUBS = 8
INNER = 256
PAD = 4
FINE = 16
CHIP_ORDER = (4, 1, 5, 2, 6, 3, 7)
ORDER = (6, 4, 2, 7, 5, 3, 1)
GROUP = 8


class Plan:
    def __init__(self, row_dev, pupil_dev, n_col, n_row):
        self.row_dev = row_dev
        self.pupil_dev = pupil_dev
        self.n_col = n_col
        self.n_row = n_row
        self.rows_all = row_dev * n_row
        self.group = min(GROUP, n_col)
        self.n_groups = n_col // self.group
        self.rows = row_dev // self.group
        self.n_pupil = pupil_dev * n_col
        self.n_pad = PAD * self.n_pupil
        self.n1 = self.n_pupil // INNER
        self.k1 = PAD * self.n1
        self.n1_dev = pupil_dev // INNER
        self.k2_group = INNER // self.n_groups
        self.k2_dev = INNER // n_col
        self.freq_tiles = PAD * pupil_dev // LANES
        self.k1_tiles = self.k1 // LANES
        self.lane_parts = INNER // LANES
        self.chunk = self.rows * 2 * self.lane_parts * self.n1_dev


def split_bf16(table):
    high = table.astype(ml_dtypes.bfloat16)
    low = (table - high.astype(np.float64)).astype(ml_dtypes.bfloat16)
    return np.stack([high, low])


def outer_tables(plan, blocks):
    angle = np.arange(plan.n1)[:, None] * np.arange(plan.k1)[None, :] % plan.k1
    angle = angle * (2.0 * np.pi / plan.k1)
    table = np.stack([np.cos(angle), np.sin(angle)]).reshape(2, blocks, plan.n1 // blocks, plan.k1)
    return split_bf16(table.transpose(1, 0, 2, 3))


def inner_tables(plan):
    angle = np.arange(INNER)[:, None] * np.arange(INNER)[None, :] % INNER
    angle = angle * (2.0 * np.pi / INNER)
    table = np.concatenate([np.cos(angle), np.sin(angle)], axis=1)
    return split_bf16(table.reshape(plan.n_col, plan.k2_dev, 2 * INNER))


def twist_tables(plan):
    made = []
    for cells in (np.arange(0, INNER, FINE), np.arange(FINE)):
        angle = cells[:, None] * np.arange(plan.k1)[None, :] * (2.0 * np.pi / plan.n_pad)
        made.extend([np.cos(angle), np.sin(angle)])
    return np.concatenate(made).astype(np.float32)


def unit_phase(code):
    quadrant = (code + LEVELS // 8) >> 10
    rest = (code - (quadrant << 10)).astype(jnp.float32) * (2.0 * math.pi / LEVELS)
    sq = rest * rest
    cos = 1.0 + sq * (-1.0 / 2 + sq * (1.0 / 24 + sq * (-1.0 / 720 + sq * (1.0 / 40320))))
    sin = rest * (1.0 + sq * (-1.0 / 6 + sq * (1.0 / 120 + sq * (-1.0 / 5040 + sq * (1.0 / 362880)))))
    swap = (quadrant & 1) == 1
    minus_cos = ((quadrant + 1) & 2) == 2
    minus_sin = (quadrant & 2) == 2
    return jnp.where(swap, sin, cos), jnp.where(swap, cos, sin), minus_cos, minus_sin


def field_kernel(plan, tiles_ref, codes_ref, mask_ref, out_ref, open_ref):
    step_id = pl.program_id(0)
    pistons = []
    for i in range(plan.pupil_dev // TILE_C):
        piston = jnp.int32(0)
        for k in range(plan.row_dev // TILE_R):
            piston = piston + jnp.where(step_id >= k, tiles_ref[k, i], 0)
        pistons.append(piston)
    stride = 2 * plan.lane_parts * plan.n1_dev
    total = jnp.zeros((SUBS, LANES), jnp.float32)
    for t in range(TILE_R // SUBS):
        for j in range(plan.pupil_dev // LANES):
            rows = slice(t * SUBS, (t + 1) * SUBS)
            lanes = slice(j * LANES, (j + 1) * LANES)
            code = (codes_ref[rows, lanes] + pistons[j * LANES // TILE_C]) & (LEVELS - 1)
            cos, sin, minus_cos, minus_sin = unit_phase(code)
            amplitude = mask_ref[rows, lanes].astype(jnp.float32)
            total = total + amplitude
            real = cos * jnp.where(minus_cos, -amplitude, amplitude)
            imag = sin * jnp.where(minus_sin, -amplitude, amplitude)
            for part, value in enumerate((real, imag)):
                start = (part * plan.lane_parts + j % plan.lane_parts) * plan.n1_dev + j // plan.lane_parts
                for g in range(plan.n_groups):
                    out_ref[g, pl.ds(t * SUBS * stride + start, SUBS, stride=stride), :] = value

    @pl.when(step_id == 0)
    def _():
        open_ref[...] = total

    @pl.when(step_id > 0)
    def _():
        open_ref[...] = open_ref[...] + total


def own_kernel(plan, me_ref, tiles_ref, codes_ref, mask_ref, code_ref, kept_ref, open_ref):
    half = plan.row_dev // 2
    first = pl.multiple_of(me_ref[0] * half, half)
    total = jnp.zeros((SUBS, LANES), jnp.int32)
    for t in range(plan.row_dev // SUBS):
        for j in range(plan.pupil_dev // LANES):
            total = total + mask_ref[t * SUBS : (t + 1) * SUBS, j * LANES : (j + 1) * LANES]
    open_ref[...] = total
    for i in range(plan.pupil_dev // TILE_C):
        lanes = slice(i * TILE_C, (i + 1) * TILE_C)
        piston = jnp.int32(0)
        for k in range(plan.row_dev // TILE_R):
            piston = piston + jnp.where(first >= k * TILE_R, tiles_ref[k, i], 0)
        code_ref[:, lanes] = codes_ref[:, lanes] + piston
    kept_ref[...] = mask_ref[pl.ds(first, half), :]


def chip_field_kernel(plan, me_ref, *refs):
    n_other = plan.n_row - 1
    others, refs = (refs[:n_other], refs[n_other : 2 * n_other]), refs[2 * n_other :]
    near_tiles_ref, own_codes_ref, own_mask_ref, open_ref, near_codes_ref, near_mask_ref = refs[:6]
    outs, made_ref = refs[6:-1], refs[-1]
    core, chip, row = me_ref[0], me_ref[1], me_ref[2]
    half = plan.row_dev // 2
    first = pl.multiple_of(core * half, half)
    total = open_ref[...]
    for t in range(plan.row_dev // SUBS):
        for j in range(plan.pupil_dev // LANES):
            total = total + near_mask_ref[t * SUBS : (t + 1) * SUBS, j * LANES : (j + 1) * LANES]
    total = total.astype(jnp.float32)
    stride = 2 * plan.lane_parts * plan.n1_dev
    for owner in range(2):
        before = jnp.zeros((1, plan.pupil_dev // TILE_C), jnp.int32)
        for d, other in enumerate(others[owner]):
            before = before + jnp.where(row > d, jnp.sum(other[...], axis=0, keepdims=True), 0)
        if owner == 1:
            for k in range(plan.row_dev // TILE_R):
                before = before + jnp.where(first >= k * TILE_R, near_tiles_ref[k : k + 1], 0)
        codes, mask = ((own_codes_ref, own_mask_ref), (near_codes_ref, near_mask_ref))[owner]
        for t in range(half // SUBS):
            rows = pl.ds(t * SUBS, SUBS) if owner == 0 else pl.ds(pl.multiple_of(first + t * SUBS, SUBS), SUBS)
            for j in range(plan.pupil_dev // LANES):
                lanes = slice(j * LANES, (j + 1) * LANES)
                column = j * LANES // TILE_C
                piston = jnp.broadcast_to(before[:, column : column + 1], (SUBS, LANES))
                cos, sin, minus_cos, minus_sin = unit_phase((codes[rows, lanes] + piston) & (LEVELS - 1))
                amplitude = mask[rows, lanes].astype(jnp.float32)
                real = cos * jnp.where(minus_cos, -amplitude, amplitude)
                imag = sin * jnp.where(minus_sin, -amplitude, amplitude)
                for part, value in enumerate((real, imag)):
                    start = (part * plan.lane_parts + j % plan.lane_parts) * plan.n1_dev + j // plan.lane_parts
                    made_ref[owner, pl.ds(t * SUBS * stride + start, SUBS, stride=stride), :] = value
    own_rows = lax.rem(chip, plan.group // 2)
    for b, out in enumerate(outs):
        source = pl.multiple_of((own_rows ^ b % (plan.group // 2)) * plan.chunk, plan.chunk)
        for i in range(plan.chunk // plan.n1_dev):
            for side in range(2):
                block = made_ref[side ^ core, pl.ds(pl.multiple_of(source + i * plan.n1_dev, plan.n1_dev), plan.n1_dev), :]
                out[(2 * i + side) * plan.n1_dev : (2 * i + side + 1) * plan.n1_dev, :] = block
        out[2 * plan.chunk :, :] = total


def tables_kernel(plan, blocks, me_ref, outer_ref, inner_ref, twist_ref, w1_ref, w2_ref, turn_ref):
    me = me_ref[0]
    w1, w2 = [], []
    for s in range(2):
        rows = [outer_ref[s, (me >> 1) ^ b if blocks > 1 else 0] for b in range(blocks)]
        cos, sin = (jnp.concatenate([both[i] for both in rows]) for i in range(2))
        w1.append(jnp.concatenate([jnp.concatenate([cos, sin]), jnp.concatenate([-sin, cos])], axis=1))
        parts = []
        for b in range(plan.group):
            both = inner_ref[s, me ^ b]
            parts.append(both)
            parts.append(jnp.concatenate([-both[:, INNER:], both[:, :INNER]], axis=1))
        w2.append(jnp.concatenate(parts))
    w1_ref[...] = jnp.concatenate([w1[0], w1[0], w1[1]])
    w2_ref[...] = jnp.concatenate([w2[0], w2[1], w2[0]], axis=1)
    turn_ref[...] = twist_ref[...]


def chip_transform_kernel(plan, order, *refs):
    n_chips = plan.n_col // 2
    chunks = [refs[order.index(b)] for b in range(n_chips)]
    tables, outs, count_ref = refs[n_chips : n_chips + 3], refs[n_chips + 3 : -1], refs[-1]
    count = chunks[0][2 * plan.chunk :, :]
    for chunk in chunks[1:]:
        count = count + chunk[2 * plan.chunk :, :]
    count_ref[...] = count
    n1_chip = 2 * plan.n1_dev

    def part_of(r, part):
        pieces = []
        for lt in range(plan.lane_parts):
            at = ((r * 2 + part) * plan.lane_parts + lt) * n1_chip
            pieces.append(jnp.concatenate([chunk[at : at + n1_chip, :] for chunk in chunks]))
        return jnp.concatenate(pieces, axis=1)

    fields = [jnp.concatenate([part_of(r, 0), part_of(r, 1)]) for r in range(plan.rows)]
    transform_rows(plan, fields, tables, outs)


def transform_kernel(plan, info_ref, x_ref, *refs):
    chunk_row = plan.chunk // plan.rows
    info = info_ref[: plan.n_col]
    info = jnp.broadcast_to(info[:, None, :], (plan.n_col, plan.n1_dev, LANES)).reshape(plan.n1, LANES)
    tile = lax.broadcasted_iota(jnp.int32, info.shape, 0) % plan.n1_dev * INNER // TILE_C
    own = lax.broadcasted_iota(jnp.int32, info.shape, 1) == tile
    before = jnp.sum(jnp.where(own, info, 0.0), axis=1, keepdims=True).astype(jnp.int32)
    turn_cos, turn_sin, minus_cos, minus_sin = unit_phase(before)
    turn_cos = jnp.where(minus_cos, -turn_cos, turn_cos)
    turn_sin = jnp.where(minus_sin, -turn_sin, turn_sin)

    def field_of(r):
        halves = []
        for part in range(2):
            pieces = []
            for lt in range(plan.lane_parts):
                at = r * chunk_row + (part * plan.lane_parts + lt) * plan.n1_dev
                pieces.append(x_ref[:, at : at + plan.n1_dev, :].reshape(plan.n1, LANES))
            halves.append(jnp.concatenate(pieces, axis=1))
        real, imag = halves
        return jnp.concatenate([real * turn_cos - imag * turn_sin, real * turn_sin + imag * turn_cos], axis=0)

    transform_rows(plan, [field_of(r) for r in range(plan.rows)], refs[:3], refs[3:])


def transform_rows(plan, fields, tables, outs):
    w1_ref, w2_ref, turn_ref = tables
    size = 2 * plan.k2_dev
    x = jnp.concatenate(fields, axis=1)
    xh = x.astype(jnp.bfloat16)
    xl = (x - xh.astype(jnp.float32)).astype(jnp.bfloat16)
    y = lax.dot_general(
        jnp.concatenate([xh, xl, xh]), w1_ref[...], (((0,), (0,)), ((), ())), preferred_element_type=jnp.float32
    )
    tc, ts = [], []
    count = INNER // FINE
    fine_cos, fine_sin = turn_ref[2 * count : 2 * count + FINE], turn_ref[2 * count + FINE :]
    for a in range(count):
        cos, sin = turn_ref[a : a + 1], turn_ref[count + a : count + a + 1]
        tc.append(cos * fine_cos - sin * fine_sin)
        ts.append(sin * fine_cos + cos * fine_sin)
    tc, ts = jnp.concatenate(tc), jnp.concatenate(ts)
    fs = []
    for r in range(plan.rows):
        yr, yi = y[r * INNER : (r + 1) * INNER, : plan.k1], y[r * INNER : (r + 1) * INNER, plan.k1 :]
        fs.append(jnp.concatenate([yr * tc + yi * ts, yi * tc - yr * ts], axis=0))
    f = jnp.concatenate(fs, axis=1)
    fh = f.astype(jnp.bfloat16)
    fl = (f - fh.astype(jnp.float32)).astype(jnp.bfloat16)
    z = jnp.dot(w2_ref[...], jnp.concatenate([fh, fh, fl]), preferred_element_type=jnp.float32)
    for r in range(plan.rows):
        for b in range(plan.group):
            outs[b][r] = z[b * size : (b + 1) * size, r * plan.k1 : (r + 1) * plan.k1].reshape(2, plan.k2_dev, plan.k1)


def merge_kernel(plan, swap_bit, me_ref, *refs):
    chunks = [refs[(ORDER + (0,)).index(b)] for b in range(plan.group)]
    counts = refs[plan.group : plan.group + plan.n_row]
    out_ref, tile_ref, sems = refs[plan.group + plan.n_row :]
    total = counts[0][...]
    for other in counts[1:]:
        total = total + other[...]
    total = jnp.sum(jnp.sum(total, axis=0, keepdims=True), axis=1, keepdims=True)
    scale = jnp.sqrt(float(plan.rows_all) / total)
    inside = lax.rem(me_ref[0], plan.group)
    swapped = lax.rem(inside // swap_bit, 2) == 1
    take = min(plan.k2_dev, SUBS)
    stride = plan.k1_tiles * SUBS
    copies = []
    for slot in range(plan.group):
        part = slot % 2
        base = [b for b in range(plan.group) if b & swap_bit == 0][slot // 2]
        for r in range(plan.rows):
            for k2 in range(0, plan.k2_dev, take):
                for j in range(plan.k1_tiles):
                    lanes = slice(j * LANES, (j + 1) * LANES)
                    a = chunks[base][r, part, k2 : k2 + take, lanes] * scale
                    b = chunks[base + swap_bit][r, part, k2 : k2 + take, lanes] * scale
                    at = (k2 * plan.k1_tiles + j) * SUBS + r
                    tile_ref[slot, pl.ds(at, take, stride=stride), :] = jnp.where(swapped, b, a)
                    tile_ref[slot, pl.ds(at + plan.rows, take, stride=stride), :] = jnp.where(swapped, a, b)
        source = inside ^ base
        tile = source // 2 if swap_bit == 1 else source % 2 * 2 + source // 4
        copy = pltpu.make_async_copy(tile_ref.at[slot], out_ref.at[part, tile], sems.at[slot])
        copy.start()
        copies.append(copy)
    for copy in copies:
        copy.wait()


def along_rows(n_row, value):
    return [lax.ppermute(value, "row", [(i, (i + d) % n_row) for i in range(n_row)]) for d in range(1, n_row)]


def spectra_shapes(plan):
    return [jax.ShapeDtypeStruct((plan.rows, 2, plan.k2_dev, plan.k1), jnp.float32)] * plan.group


def ready_tables(plan, me, blocks):
    smem, vmem = pl.BlockSpec(memory_space=pltpu.SMEM), pl.BlockSpec(memory_space=pltpu.VMEM)
    return pl.pallas_call(
        partial(tables_kernel, plan, blocks),
        out_shape=[
            jax.ShapeDtypeStruct((6 * plan.n1, 2 * plan.k1), jnp.bfloat16),
            jax.ShapeDtypeStruct((2 * plan.group * plan.k2_dev, 6 * INNER), jnp.bfloat16),
            jax.ShapeDtypeStruct((2 * (INNER // FINE + FINE), plan.k1), jnp.float32),
        ],
        in_specs=[smem] + [vmem] * 3,
        out_specs=[vmem] * 3,
        compiler_params=pltpu.CompilerParams(vmem_limit_bytes=24 * 2**20),
        name="tables",
    )(me, outer_tables(plan, blocks), inner_tables(plan), twist_tables(plan))


def spectra_by_chip(plan, phase_codes, aperture, tile_offsets):
    n_col, n_row = plan.n_col, plan.n_row
    n_chips = n_col // 2
    half = plan.row_dev // 2
    row_index = lax.axis_index("row").astype(jnp.int32)
    col_index = lax.axis_index("col").astype(jnp.int32)
    smem, vmem = pl.BlockSpec(memory_space=pltpu.SMEM), pl.BlockSpec(memory_space=pltpu.VMEM)
    swap = [(q, q ^ 1) for q in range(n_col)]
    others = along_rows(n_row, tile_offsets)
    near_others = []
    for d in range(1, n_row):
        pairs = [(r * n_col + q, (r + d) % n_row * n_col + (q ^ 1)) for r in range(n_row) for q in range(n_col)]
        near_others.append(lax.ppermute(tile_offsets, ("row", "col"), pairs))
    near = [lax.ppermute(value, "col", swap) for value in (tile_offsets, phase_codes, aperture)]
    place = jnp.stack([col_index % 2, col_index // 2, row_index])
    own = pl.pallas_call(
        partial(own_kernel, plan),
        out_shape=[jax.ShapeDtypeStruct((half, plan.pupil_dev), jnp.int32)] * 2
        + [jax.ShapeDtypeStruct((SUBS, LANES), jnp.int32)],
        grid_spec=pltpu.PrefetchScalarGridSpec(
            num_scalar_prefetch=1,
            grid=(1,),
            in_specs=[
                smem,
                pl.BlockSpec((half, plan.pupil_dev), lambda i, p: (p[0], 0)),
                pl.BlockSpec((plan.row_dev, plan.pupil_dev), lambda i, p: (0, 0)),
            ],
            out_specs=[vmem] * 3,
        ),
        compiler_params=pltpu.CompilerParams(vmem_limit_bytes=16 * 2**20),
        name="own",
    )(place, *(pltpu.with_memory_space_constraint(a, pltpu.HBM) for a in (tile_offsets, phase_codes, aperture)))
    block = jax.ShapeDtypeStruct((2 * plan.chunk + SUBS, LANES), jnp.float32)
    rows = pl.pallas_call(
        partial(chip_field_kernel, plan),
        out_shape=[block] * n_chips,
        in_specs=[smem] + [vmem] * (2 * n_row + 4),
        out_specs=[vmem] * n_chips,
        scratch_shapes=[pltpu.VMEM((2, half * plan.chunk // plan.rows, LANES), jnp.float32)],
        compiler_params=pltpu.CompilerParams(vmem_limit_bytes=16 * 2**20),
        name="field",
    )(place, *others, *near_others, near[0], *own, near[1], near[2])
    order = CHIP_ORDER + (0,)
    received = [rows[0] if b == 0 else lax.ppermute(rows[b], "col", [(q, q ^ 2 * b) for q in range(n_col)]) for b in order]
    *made, opened = pl.pallas_call(
        partial(chip_transform_kernel, plan, order),
        out_shape=spectra_shapes(plan) + [jax.ShapeDtypeStruct((SUBS, LANES), jnp.float32)],
        in_specs=[vmem] * (n_chips + 3),
        out_specs=[vmem] * (plan.group + 1),
        compiler_params=pltpu.CompilerParams(vmem_limit_bytes=24 * 2**20),
        name="transform",
    )(*received, *ready_tables(plan, col_index.reshape(1), n_chips))
    return made, opened


def spectra_by_device(plan, phase_codes, aperture, tile_offsets):
    n_col, n_row = plan.n_col, plan.n_row
    row_index = lax.axis_index("row")
    col_index = lax.axis_index("col")
    me = col_index.astype(jnp.int32).reshape(1)
    smem = pl.BlockSpec(memory_space=pltpu.SMEM)
    vmem = pl.BlockSpec(memory_space=pltpu.VMEM)
    before = jnp.zeros((1, plan.pupil_dev // TILE_C), jnp.int32)
    for d, other in enumerate(along_rows(n_row, tile_offsets)):
        before = before + jnp.where(row_index > d, jnp.sum(other, axis=0, keepdims=True), 0)
    before = jnp.pad((before & (LEVELS - 1)).astype(jnp.float32), ((0, 0), (0, LANES - before.shape[1])))
    mine = jnp.arange(n_col, dtype=jnp.int32)[:, None] == col_index

    field_rows = plan.row_dev * 2 * plan.lane_parts * plan.n1_dev
    steps = plan.row_dev // TILE_R
    packed, opened = pl.pallas_call(
        partial(field_kernel, plan),
        out_shape=[
            jax.ShapeDtypeStruct((plan.n_groups, field_rows, LANES), jnp.float32),
            jax.ShapeDtypeStruct((SUBS, LANES), jnp.float32),
        ],
        grid=(steps,),
        in_specs=[
            smem,
            pl.BlockSpec((TILE_R, plan.pupil_dev), lambda t: (t, 0)),
            pl.BlockSpec((TILE_R, plan.pupil_dev), lambda t: (t, 0)),
        ],
        out_specs=[
            pl.BlockSpec((plan.n_groups, field_rows // steps, LANES), lambda t: (0, t, 0)),
            pl.BlockSpec((SUBS, LANES), lambda t: (0, 0)),
        ],
        name="field",
    )(tile_offsets, phase_codes, aperture)
    packed = packed.reshape(n_col, plan.chunk, LANES)
    received = lax.all_to_all(packed, "col", split_axis=0, concat_axis=0, tiled=True)

    info = jnp.concatenate([jnp.where(mine, before, 0.0), opened])
    for bit in range(n_col.bit_length() - 1):
        info = info + lax.ppermute(info, "col", [(q, q ^ 1 << bit) for q in range(n_col)])
    made = pl.pallas_call(
        partial(transform_kernel, plan),
        out_shape=spectra_shapes(plan),
        in_specs=[vmem] * 5,
        out_specs=[vmem] * plan.group,
        compiler_params=pltpu.CompilerParams(vmem_limit_bytes=24 * 2**20),
        name="transform",
    )(info, received, *ready_tables(plan, me, 1))
    return made, info[n_col:]


def per_device(phase_codes, aperture, tile_offsets):
    n_col = lax.axis_size("col")
    n_row = lax.axis_size("row")
    plan = Plan(*phase_codes.shape, n_col, n_row)
    by_chip = plan.n1_dev % SUBS == 0 and len(CHIP_ORDER) == n_col // 2 - 1
    spectra = spectra_by_chip if by_chip else spectra_by_device
    made, opened = spectra(plan, phase_codes, aperture, tile_offsets)
    chunks = [lax.ppermute(made[b], "col", [(q, q ^ b) for q in range(n_col)]) for b in ORDER] + [made[0]]
    opened, chunks[2] = lax.optimization_barrier((opened, chunks[2]))
    counts = [opened] + along_rows(n_row, opened)
    smem = pl.BlockSpec(memory_space=pltpu.SMEM)
    vmem = pl.BlockSpec(memory_space=pltpu.VMEM)
    tiles = plan.row_dev // SUBS
    out = pl.pallas_call(
        partial(merge_kernel, plan, 2 if by_chip else 1),
        out_shape=jax.ShapeDtypeStruct((2, tiles, plan.freq_tiles * SUBS, LANES), jnp.float32),
        in_specs=[smem] + [vmem] * (plan.group + n_row),
        out_specs=pl.BlockSpec(memory_space=pl.ANY),
        scratch_shapes=[
            pltpu.VMEM((plan.group, plan.freq_tiles * SUBS, LANES), jnp.float32),
            pltpu.SemaphoreType.DMA((plan.group,)),
        ],
        compiler_params=pltpu.CompilerParams(vmem_limit_bytes=24 * 2**20),
        name="merge",
    )(lax.axis_index("col").astype(jnp.int32).reshape(1), *chunks, *counts)
    out = out.reshape(2, tiles, plan.freq_tiles, SUBS, LANES).transpose(0, 1, 3, 2, 4)
    return out.reshape(2, plan.row_dev, plan.freq_tiles * LANES)


def solution(mesh):
    placed = (P("row", "col"), P("row", "col"), P("row", "col"))
    return jax.shard_map(
        per_device, mesh=mesh, in_specs=placed, out_specs=P(None, "row", "col"), check_vma=False
    )
```

```python
import math
from functools import partial

import jax
import jax.numpy as jnp
import ml_dtypes
import numpy as np
from jax import lax
from jax.experimental import pallas as pl
from jax.experimental.pallas import tpu as pltpu
from jax.sharding import PartitionSpec as P

LEVELS = 4096
TILE_R = 16
TILE_C = 512
LANES = 128
SUBS = 8
INNER = 256
PAD = 4
FINE = 16
CHIP_ORDER = (4, 1, 5, 2, 6, 3, 7)
ORDER = (6, 4, 2, 7, 5, 3, 1)
GROUP = 8


class Plan:
    def __init__(self, row_dev, pupil_dev, n_col, n_row):
        self.row_dev = row_dev
        self.pupil_dev = pupil_dev
        self.n_col = n_col
        self.n_row = n_row
        self.rows_all = row_dev * n_row
        self.group = min(GROUP, n_col)
        self.n_groups = n_col // self.group
        self.rows = row_dev // self.group
        self.n_pupil = pupil_dev * n_col
        self.n_pad = PAD * self.n_pupil
        self.n1 = self.n_pupil // INNER
        self.k1 = PAD * self.n1
        self.n1_dev = pupil_dev // INNER
        self.k2_group = INNER // self.n_groups
        self.k2_dev = INNER // n_col
        self.freq_tiles = PAD * pupil_dev // LANES
        self.k1_tiles = self.k1 // LANES
        self.lane_parts = INNER // LANES
        self.chunk = self.rows * 2 * self.lane_parts * self.n1_dev


def split_bf16(table):
    high = table.astype(ml_dtypes.bfloat16)
    low = (table - high.astype(np.float64)).astype(ml_dtypes.bfloat16)
    return np.stack([high, low])


def outer_tables(plan, blocks):
    angle = np.arange(plan.n1)[:, None] * np.arange(plan.k1)[None, :] % plan.k1
    angle = angle * (2.0 * np.pi / plan.k1)
    table = np.stack([np.cos(angle), np.sin(angle)]).reshape(2, blocks, plan.n1 // blocks, plan.k1)
    return split_bf16(table.transpose(1, 0, 2, 3))


def inner_tables(plan):
    angle = np.arange(INNER)[:, None] * np.arange(INNER // 2)[None, :] % INNER
    angle = angle * (2.0 * np.pi / INNER)
    table = np.concatenate([np.cos(angle), np.sin(angle)], axis=1)
    return split_bf16(table.reshape(plan.n_col, plan.k2_dev // 2, 2, INNER).transpose(0, 2, 1, 3))


def twist_tables(plan):
    made = []
    for cells in (np.arange(0, INNER, FINE), np.arange(FINE)):
        angle = cells[:, None] * np.arange(plan.k1)[None, :] * (2.0 * np.pi / plan.n_pad)
        made.extend([np.cos(angle), np.sin(angle)])
    return np.concatenate(made).astype(np.float32)


def unit_phase(code):
    quadrant = (code + LEVELS // 8) >> 10
    rest = (code - (quadrant << 10)).astype(jnp.float32) * (2.0 * math.pi / LEVELS)
    sq = rest * rest
    cos = 1.0 + sq * (-1.0 / 2 + sq * (1.0 / 24 + sq * (-1.0 / 720 + sq * (1.0 / 40320))))
    sin = rest * (1.0 + sq * (-1.0 / 6 + sq * (1.0 / 120 + sq * (-1.0 / 5040 + sq * (1.0 / 362880)))))
    swap = (quadrant & 1) == 1
    minus_cos = ((quadrant + 1) & 2) == 2
    minus_sin = (quadrant & 2) == 2
    return jnp.where(swap, sin, cos), jnp.where(swap, cos, sin), minus_cos, minus_sin


def field_kernel(plan, tiles_ref, codes_ref, mask_ref, out_ref, open_ref):
    step_id = pl.program_id(0)
    pistons = []
    for i in range(plan.pupil_dev // TILE_C):
        piston = jnp.int32(0)
        for k in range(plan.row_dev // TILE_R):
            piston = piston + jnp.where(step_id >= k, tiles_ref[k, i], 0)
        pistons.append(piston)
    stride = 2 * plan.lane_parts * plan.n1_dev
    total = jnp.zeros((SUBS, LANES), jnp.float32)
    for t in range(TILE_R // SUBS):
        for j in range(plan.pupil_dev // LANES):
            rows = slice(t * SUBS, (t + 1) * SUBS)
            lanes = slice(j * LANES, (j + 1) * LANES)
            code = (codes_ref[rows, lanes] + pistons[j * LANES // TILE_C]) & (LEVELS - 1)
            cos, sin, minus_cos, minus_sin = unit_phase(code)
            amplitude = mask_ref[rows, lanes].astype(jnp.float32)
            total = total + amplitude
            real = cos * jnp.where(minus_cos, -amplitude, amplitude)
            imag = sin * jnp.where(minus_sin, -amplitude, amplitude)
            for part, value in enumerate((real, imag)):
                start = (part * plan.lane_parts + j % plan.lane_parts) * plan.n1_dev + j // plan.lane_parts
                for g in range(plan.n_groups):
                    out_ref[g, pl.ds(t * SUBS * stride + start, SUBS, stride=stride), :] = value

    @pl.when(step_id == 0)
    def _():
        open_ref[...] = total

    @pl.when(step_id > 0)
    def _():
        open_ref[...] = open_ref[...] + total


def own_kernel(plan, me_ref, tiles_ref, codes_ref, mask_ref, code_ref, kept_ref, open_ref):
    half = plan.row_dev // 2
    first = pl.multiple_of(me_ref[0] * half, half)
    total = jnp.zeros((SUBS, LANES), jnp.int32)
    for t in range(plan.row_dev // SUBS):
        for j in range(plan.pupil_dev // LANES):
            total = total + mask_ref[t * SUBS : (t + 1) * SUBS, j * LANES : (j + 1) * LANES]
    open_ref[...] = total
    for i in range(plan.pupil_dev // TILE_C):
        lanes = slice(i * TILE_C, (i + 1) * TILE_C)
        piston = jnp.int32(0)
        for k in range(plan.row_dev // TILE_R):
            piston = piston + jnp.where(first >= k * TILE_R, tiles_ref[k, i], 0)
        code_ref[:, lanes] = codes_ref[:, lanes] + piston
    kept_ref[...] = mask_ref[pl.ds(first, half), :]


def chip_field_kernel(plan, me_ref, *refs):
    n_other = plan.n_row - 1
    others, refs = (refs[:n_other], refs[n_other : 2 * n_other]), refs[2 * n_other :]
    near_tiles_ref, own_codes_ref, own_mask_ref, open_ref, near_codes_ref, near_mask_ref = refs[:6]
    outs, made_ref = refs[6:-1], refs[-1]
    core, chip, row = me_ref[0], me_ref[1], me_ref[2]
    half = plan.row_dev // 2
    first = pl.multiple_of(core * half, half)
    total = open_ref[...]
    for t in range(plan.row_dev // SUBS):
        for j in range(plan.pupil_dev // LANES):
            total = total + near_mask_ref[t * SUBS : (t + 1) * SUBS, j * LANES : (j + 1) * LANES]
    total = total.astype(jnp.float32)
    stride = 2 * plan.lane_parts * plan.n1_dev
    for owner in range(2):
        before = jnp.zeros((1, plan.pupil_dev // TILE_C), jnp.int32)
        for d, other in enumerate(others[owner]):
            before = before + jnp.where(row > d, jnp.sum(other[...], axis=0, keepdims=True), 0)
        if owner == 1:
            for k in range(plan.row_dev // TILE_R):
                before = before + jnp.where(first >= k * TILE_R, near_tiles_ref[k : k + 1], 0)
        codes, mask = ((own_codes_ref, own_mask_ref), (near_codes_ref, near_mask_ref))[owner]
        for t in range(half // SUBS):
            rows = pl.ds(t * SUBS, SUBS) if owner == 0 else pl.ds(pl.multiple_of(first + t * SUBS, SUBS), SUBS)
            for j in range(plan.pupil_dev // LANES):
                lanes = slice(j * LANES, (j + 1) * LANES)
                column = j * LANES // TILE_C
                piston = jnp.broadcast_to(before[:, column : column + 1], (SUBS, LANES))
                cos, sin, minus_cos, minus_sin = unit_phase((codes[rows, lanes] + piston) & (LEVELS - 1))
                amplitude = mask[rows, lanes].astype(jnp.float32)
                real = cos * jnp.where(minus_cos, -amplitude, amplitude)
                imag = sin * jnp.where(minus_sin, -amplitude, amplitude)
                for part, value in enumerate((real, imag)):
                    start = (part * plan.lane_parts + j % plan.lane_parts) * plan.n1_dev + j // plan.lane_parts
                    made_ref[owner, pl.ds(t * SUBS * stride + start, SUBS, stride=stride), :] = value
    own_rows = lax.rem(chip, plan.group // 2)
    for b, out in enumerate(outs):
        source = pl.multiple_of((own_rows ^ b % (plan.group // 2)) * plan.chunk, plan.chunk)
        for i in range(plan.chunk // plan.n1_dev):
            for side in range(2):
                block = made_ref[side ^ core, pl.ds(pl.multiple_of(source + i * plan.n1_dev, plan.n1_dev), plan.n1_dev), :]
                out[(2 * i + side) * plan.n1_dev : (2 * i + side + 1) * plan.n1_dev, :] = block
        out[2 * plan.chunk :, :] = total


def tables_kernel(plan, blocks, me_ref, outer_ref, inner_ref, twist_ref, w1_ref, w2_ref, turn_ref):
    me = me_ref[0]
    w1, w2 = [], ([], [])
    for s in range(2):
        rows = [outer_ref[s, (me >> 1) ^ b if blocks > 1 else 0] for b in range(blocks)]
        cos, sin = (jnp.concatenate([both[i] for both in rows]) for i in range(2))
        w1.append(jnp.concatenate([jnp.concatenate([cos, sin]), jnp.concatenate([-sin, cos])], axis=1))
        for p in range(2):
            parts = []
            for b in range(plan.group):
                both = inner_ref[s, me ^ b, p].astype(jnp.float32)
                parts.append(both)
                parts.append(jnp.concatenate([-both[:, INNER // 2 :], both[:, : INNER // 2]], axis=1))
            w2[p].append(jnp.concatenate(parts).astype(jnp.bfloat16))
    w1_ref[...] = jnp.concatenate([w1[0], w1[0], w1[1]])
    for p in range(2):
        w2_ref[p] = jnp.concatenate([w2[p][0], w2[p][1]])
    turn_ref[...] = twist_ref[...]


def chip_transform_kernel(plan, order, *refs):
    n_chips = plan.n_col // 2
    chunks = [refs[order.index(b)] for b in range(n_chips)]
    tables, outs, count_ref = refs[n_chips : n_chips + 3], refs[n_chips + 3 : -1], refs[-1]
    count = chunks[0][2 * plan.chunk :, :]
    for chunk in chunks[1:]:
        count = count + chunk[2 * plan.chunk :, :]
    count_ref[...] = count
    n1_chip = 2 * plan.n1_dev

    def part_of(r, part):
        pieces = []
        for lt in range(plan.lane_parts):
            at = ((r * 2 + part) * plan.lane_parts + lt) * n1_chip
            pieces.append(jnp.concatenate([chunk[at : at + n1_chip, :] for chunk in chunks]))
        return jnp.concatenate(pieces, axis=1)

    fields = [jnp.concatenate([part_of(r, 0), part_of(r, 1)]) for r in range(plan.rows)]
    transform_rows(plan, fields, tables, outs)


def transform_kernel(plan, info_ref, x_ref, *refs):
    chunk_row = plan.chunk // plan.rows
    info = info_ref[: plan.n_col]
    info = jnp.broadcast_to(info[:, None, :], (plan.n_col, plan.n1_dev, LANES)).reshape(plan.n1, LANES)
    tile = lax.broadcasted_iota(jnp.int32, info.shape, 0) % plan.n1_dev * INNER // TILE_C
    own = lax.broadcasted_iota(jnp.int32, info.shape, 1) == tile
    before = jnp.sum(jnp.where(own, info, 0.0), axis=1, keepdims=True).astype(jnp.int32)
    turn_cos, turn_sin, minus_cos, minus_sin = unit_phase(before)
    turn_cos = jnp.where(minus_cos, -turn_cos, turn_cos)
    turn_sin = jnp.where(minus_sin, -turn_sin, turn_sin)

    def field_of(r):
        halves = []
        for part in range(2):
            pieces = []
            for lt in range(plan.lane_parts):
                at = r * chunk_row + (part * plan.lane_parts + lt) * plan.n1_dev
                pieces.append(x_ref[:, at : at + plan.n1_dev, :].reshape(plan.n1, LANES))
            halves.append(jnp.concatenate(pieces, axis=1))
        real, imag = halves
        return jnp.concatenate([real * turn_cos - imag * turn_sin, real * turn_sin + imag * turn_cos], axis=0)

    transform_rows(plan, [field_of(r) for r in range(plan.rows)], refs[:3], refs[3:])


def transform_rows(plan, fields, tables, outs):
    w1_ref, w2_ref, turn_ref = tables
    x = jnp.concatenate(fields, axis=1)
    xh = x.astype(jnp.bfloat16)
    xl = (x - xh.astype(jnp.float32)).astype(jnp.bfloat16)
    y = lax.dot_general(
        jnp.concatenate([xh, xl, xh]), w1_ref[...], (((0,), (0,)), ((), ())), preferred_element_type=jnp.float32
    )
    tc, ts = [], []
    count = INNER // FINE
    fine_cos, fine_sin = turn_ref[2 * count : 2 * count + FINE], turn_ref[2 * count + FINE :]
    for a in range(count):
        cos, sin = turn_ref[a : a + 1], turn_ref[count + a : count + a + 1]
        tc.append(cos * fine_cos - sin * fine_sin)
        ts.append(sin * fine_cos + cos * fine_sin)
    tc, ts = jnp.concatenate(tc), jnp.concatenate(ts)
    fs = ([], [])
    for r in range(plan.rows):
        yr, yi = y[r * INNER : (r + 1) * INNER, : plan.k1], y[r * INNER : (r + 1) * INNER, plan.k1 :]
        fr, fi = yr * tc + yi * ts, yi * tc - yr * ts
        for p in range(2):
            pair = [f[: INNER // 2] + f[INNER // 2 :] if p == 0 else f[: INNER // 2] - f[INNER // 2 :] for f in (fr, fi)]
            fs[p].append(jnp.concatenate(pair))
    half = plan.k2_dev // 2
    for p in range(2):
        f = jnp.concatenate(fs[p], axis=1)
        fh = f.astype(jnp.bfloat16)
        fl = (f - fh.astype(jnp.float32)).astype(jnp.bfloat16)
        size = plan.group * plan.k2_dev
        z = jnp.dot(w2_ref[p], fh, preferred_element_type=jnp.float32)
        z = z[:size] + z[size:] + jnp.dot(w2_ref[p, :size], fl, preferred_element_type=jnp.float32)
        for r in range(plan.rows):
            for b in range(plan.group):
                part = z[b * plan.k2_dev : (b + 1) * plan.k2_dev, r * plan.k1 : (r + 1) * plan.k1]
                outs[b][r, :, p * half : (p + 1) * half, :] = part.reshape(2, half, plan.k1)


def merge_kernel(plan, swap_bit, me_ref, *refs):
    chunks = [refs[(ORDER + (0,)).index(b)] for b in range(plan.group)]
    counts = refs[plan.group : plan.group + plan.n_row]
    out_ref, tile_ref, sems = refs[plan.group + plan.n_row :]
    total = counts[0][...]
    for other in counts[1:]:
        total = total + other[...]
    total = jnp.sum(jnp.sum(total, axis=0, keepdims=True), axis=1, keepdims=True)
    scale = jnp.sqrt(float(plan.rows_all) / total)
    inside = lax.rem(me_ref[0], plan.group)
    swapped = lax.rem(inside // swap_bit, 2) == 1
    half = plan.k2_dev // 2
    stride = 2 * plan.k1_tiles * SUBS
    copies = []
    for slot in range(plan.group):
        part = slot % 2
        base = [b for b in range(plan.group) if b & swap_bit == 0][slot // 2]
        for r in range(plan.rows):
            for p in range(2):
                for j in range(plan.k1_tiles):
                    rows, lanes = slice(p * half, (p + 1) * half), slice(j * LANES, (j + 1) * LANES)
                    a = chunks[base][r, part, rows, lanes] * scale
                    b = chunks[base + swap_bit][r, part, rows, lanes] * scale
                    at = (p * plan.k1_tiles + j) * SUBS + r
                    tile_ref[slot, pl.ds(at, half, stride=stride), :] = jnp.where(swapped, b, a)
                    tile_ref[slot, pl.ds(at + plan.rows, half, stride=stride), :] = jnp.where(swapped, a, b)
        source = inside ^ base
        tile = source // 2 if swap_bit == 1 else source % 2 * 2 + source // 4
        copy = pltpu.make_async_copy(tile_ref.at[slot], out_ref.at[part, tile], sems.at[slot])
        copy.start()
        copies.append(copy)
    for copy in copies:
        copy.wait()


def along_rows(n_row, value):
    return [lax.ppermute(value, "row", [(i, (i + d) % n_row) for i in range(n_row)]) for d in range(1, n_row)]


def spectra_shapes(plan):
    return [jax.ShapeDtypeStruct((plan.rows, 2, plan.k2_dev, plan.k1), jnp.float32)] * plan.group


def ready_tables(plan, me, blocks):
    smem, vmem = pl.BlockSpec(memory_space=pltpu.SMEM), pl.BlockSpec(memory_space=pltpu.VMEM)
    return pl.pallas_call(
        partial(tables_kernel, plan, blocks),
        out_shape=[
            jax.ShapeDtypeStruct((6 * plan.n1, 2 * plan.k1), jnp.bfloat16),
            jax.ShapeDtypeStruct((2, 2 * plan.group * plan.k2_dev, INNER), jnp.bfloat16),
            jax.ShapeDtypeStruct((2 * (INNER // FINE + FINE), plan.k1), jnp.float32),
        ],
        in_specs=[smem] + [vmem] * 3,
        out_specs=[vmem] * 3,
        compiler_params=pltpu.CompilerParams(vmem_limit_bytes=24 * 2**20),
        name="tables",
    )(me, outer_tables(plan, blocks), inner_tables(plan), twist_tables(plan))


def spectra_by_chip(plan, phase_codes, aperture, tile_offsets):
    n_col, n_row = plan.n_col, plan.n_row
    n_chips = n_col // 2
    half = plan.row_dev // 2
    row_index = lax.axis_index("row").astype(jnp.int32)
    col_index = lax.axis_index("col").astype(jnp.int32)
    smem, vmem = pl.BlockSpec(memory_space=pltpu.SMEM), pl.BlockSpec(memory_space=pltpu.VMEM)
    swap = [(q, q ^ 1) for q in range(n_col)]
    others = along_rows(n_row, tile_offsets)
    near_others = []
    for d in range(1, n_row):
        pairs = [(r * n_col + q, (r + d) % n_row * n_col + (q ^ 1)) for r in range(n_row) for q in range(n_col)]
        near_others.append(lax.ppermute(tile_offsets, ("row", "col"), pairs))
    near = [lax.ppermute(value, "col", swap) for value in (tile_offsets, phase_codes, aperture)]
    place = jnp.stack([col_index % 2, col_index // 2, row_index])
    own = pl.pallas_call(
        partial(own_kernel, plan),
        out_shape=[jax.ShapeDtypeStruct((half, plan.pupil_dev), jnp.int32)] * 2
        + [jax.ShapeDtypeStruct((SUBS, LANES), jnp.int32)],
        grid_spec=pltpu.PrefetchScalarGridSpec(
            num_scalar_prefetch=1,
            grid=(1,),
            in_specs=[
                smem,
                pl.BlockSpec((half, plan.pupil_dev), lambda i, p: (p[0], 0)),
                pl.BlockSpec((plan.row_dev, plan.pupil_dev), lambda i, p: (0, 0)),
            ],
            out_specs=[vmem] * 3,
        ),
        compiler_params=pltpu.CompilerParams(vmem_limit_bytes=16 * 2**20),
        name="own",
    )(place, *(pltpu.with_memory_space_constraint(a, pltpu.HBM) for a in (tile_offsets, phase_codes, aperture)))
    block = jax.ShapeDtypeStruct((2 * plan.chunk + SUBS, LANES), jnp.float32)
    rows = pl.pallas_call(
        partial(chip_field_kernel, plan),
        out_shape=[block] * n_chips,
        in_specs=[smem] + [vmem] * (2 * n_row + 4),
        out_specs=[vmem] * n_chips,
        scratch_shapes=[pltpu.VMEM((2, half * plan.chunk // plan.rows, LANES), jnp.float32)],
        compiler_params=pltpu.CompilerParams(vmem_limit_bytes=16 * 2**20),
        name="field",
    )(place, *others, *near_others, near[0], *own, near[1], near[2])
    order = CHIP_ORDER + (0,)
    received = [rows[0] if b == 0 else lax.ppermute(rows[b], "col", [(q, q ^ 2 * b) for q in range(n_col)]) for b in order]
    *made, opened = pl.pallas_call(
        partial(chip_transform_kernel, plan, order),
        out_shape=spectra_shapes(plan) + [jax.ShapeDtypeStruct((SUBS, LANES), jnp.float32)],
        in_specs=[vmem] * (n_chips + 3),
        out_specs=[vmem] * (plan.group + 1),
        compiler_params=pltpu.CompilerParams(vmem_limit_bytes=24 * 2**20),
        name="transform",
    )(*received, *ready_tables(plan, col_index.reshape(1), n_chips))
    return made, opened


def spectra_by_device(plan, phase_codes, aperture, tile_offsets):
    n_col, n_row = plan.n_col, plan.n_row
    row_index = lax.axis_index("row")
    col_index = lax.axis_index("col")
    me = col_index.astype(jnp.int32).reshape(1)
    smem = pl.BlockSpec(memory_space=pltpu.SMEM)
    vmem = pl.BlockSpec(memory_space=pltpu.VMEM)
    before = jnp.zeros((1, plan.pupil_dev // TILE_C), jnp.int32)
    for d, other in enumerate(along_rows(n_row, tile_offsets)):
        before = before + jnp.where(row_index > d, jnp.sum(other, axis=0, keepdims=True), 0)
    before = jnp.pad((before & (LEVELS - 1)).astype(jnp.float32), ((0, 0), (0, LANES - before.shape[1])))
    mine = jnp.arange(n_col, dtype=jnp.int32)[:, None] == col_index

    field_rows = plan.row_dev * 2 * plan.lane_parts * plan.n1_dev
    steps = plan.row_dev // TILE_R
    packed, opened = pl.pallas_call(
        partial(field_kernel, plan),
        out_shape=[
            jax.ShapeDtypeStruct((plan.n_groups, field_rows, LANES), jnp.float32),
            jax.ShapeDtypeStruct((SUBS, LANES), jnp.float32),
        ],
        grid=(steps,),
        in_specs=[
            smem,
            pl.BlockSpec((TILE_R, plan.pupil_dev), lambda t: (t, 0)),
            pl.BlockSpec((TILE_R, plan.pupil_dev), lambda t: (t, 0)),
        ],
        out_specs=[
            pl.BlockSpec((plan.n_groups, field_rows // steps, LANES), lambda t: (0, t, 0)),
            pl.BlockSpec((SUBS, LANES), lambda t: (0, 0)),
        ],
        name="field",
    )(tile_offsets, phase_codes, aperture)
    packed = packed.reshape(n_col, plan.chunk, LANES)
    received = lax.all_to_all(packed, "col", split_axis=0, concat_axis=0, tiled=True)

    info = jnp.concatenate([jnp.where(mine, before, 0.0), opened])
    for bit in range(n_col.bit_length() - 1):
        info = info + lax.ppermute(info, "col", [(q, q ^ 1 << bit) for q in range(n_col)])
    made = pl.pallas_call(
        partial(transform_kernel, plan),
        out_shape=spectra_shapes(plan),
        in_specs=[vmem] * 5,
        out_specs=[vmem] * plan.group,
        compiler_params=pltpu.CompilerParams(vmem_limit_bytes=24 * 2**20),
        name="transform",
    )(info, received, *ready_tables(plan, me, 1))
    return made, info[n_col:]


def per_device(phase_codes, aperture, tile_offsets):
    n_col = lax.axis_size("col")
    n_row = lax.axis_size("row")
    plan = Plan(*phase_codes.shape, n_col, n_row)
    by_chip = plan.n1_dev % SUBS == 0 and len(CHIP_ORDER) == n_col // 2 - 1
    spectra = spectra_by_chip if by_chip else spectra_by_device
    made, opened = spectra(plan, phase_codes, aperture, tile_offsets)
    chunks = [lax.ppermute(made[b], "col", [(q, q ^ b) for q in range(n_col)]) for b in ORDER] + [made[0]]
    opened, chunks[2] = lax.optimization_barrier((opened, chunks[2]))
    counts = [opened] + along_rows(n_row, opened)
    smem = pl.BlockSpec(memory_space=pltpu.SMEM)
    vmem = pl.BlockSpec(memory_space=pltpu.VMEM)
    tiles = plan.row_dev // SUBS
    out = pl.pallas_call(
        partial(merge_kernel, plan, 2 if by_chip else 1),
        out_shape=jax.ShapeDtypeStruct((2, tiles, plan.freq_tiles * SUBS, LANES), jnp.float32),
        in_specs=[smem] + [vmem] * (plan.group + n_row),
        out_specs=pl.BlockSpec(memory_space=pl.ANY),
        scratch_shapes=[
            pltpu.VMEM((plan.group, plan.freq_tiles * SUBS, LANES), jnp.float32),
            pltpu.SemaphoreType.DMA((plan.group,)),
        ],
        compiler_params=pltpu.CompilerParams(vmem_limit_bytes=24 * 2**20),
        name="merge",
    )(lax.axis_index("col").astype(jnp.int32).reshape(1), *chunks, *counts)
    out = out.reshape(2, tiles, plan.freq_tiles, SUBS, LANES).transpose(0, 1, 3, 2, 4)
    return out.reshape(2, plan.row_dev, plan.freq_tiles * LANES)


def solution(mesh):
    placed = (P("row", "col"), P("row", "col"), P("row", "col"))
    return jax.shard_map(
        per_device, mesh=mesh, in_specs=placed, out_specs=P(None, "row", "col"), check_vma=False
    )
```

```python
import math
from functools import partial

import jax
import jax.numpy as jnp
import ml_dtypes
import numpy as np
from jax import lax
from jax.experimental import pallas as pl
from jax.experimental.pallas import tpu as pltpu
from jax.sharding import PartitionSpec as P

LEVELS = 4096
TILE_R = 16
TILE_C = 512
LANES = 128
SUBS = 8
INNER = 256
PAD = 4
FINE = 16
CHIP_ORDER = (4, 1, 5, 2, 6, 3, 7)
ORDER = (6, 4, 2, 7, 5, 3, 1)
GROUP = 8


class Plan:
    def __init__(self, row_dev, pupil_dev, n_col, n_row):
        self.row_dev = row_dev
        self.pupil_dev = pupil_dev
        self.n_col = n_col
        self.n_row = n_row
        self.rows_all = row_dev * n_row
        self.group = min(GROUP, n_col)
        self.n_groups = n_col // self.group
        self.rows = row_dev // self.group
        self.n_pupil = pupil_dev * n_col
        self.n_pad = PAD * self.n_pupil
        self.n1 = self.n_pupil // INNER
        self.k1 = PAD * self.n1
        self.n1_dev = pupil_dev // INNER
        self.k2_group = INNER // self.n_groups
        self.k2_dev = INNER // n_col
        self.freq_tiles = PAD * pupil_dev // LANES
        self.k1_tiles = self.k1 // LANES
        self.lane_parts = INNER // LANES
        self.chunk = self.rows * 2 * self.lane_parts * self.n1_dev


def split_bf16(table):
    high = table.astype(ml_dtypes.bfloat16)
    low = (table - high.astype(np.float64)).astype(ml_dtypes.bfloat16)
    return np.stack([high, low])


def outer_tables(plan, blocks):
    k1 = plan.k1 // 2
    angle = np.arange(plan.n1)[:, None] * np.arange(k1)[None, :] % plan.k1
    angle = angle * (2.0 * np.pi / plan.k1)
    table = np.stack([np.cos(angle), np.sin(angle)]).reshape(2, blocks, plan.n1 // blocks // 2, 2, k1)
    return split_bf16(table.transpose(1, 3, 0, 2, 4))


def inner_tables(plan):
    angle = np.arange(INNER)[:, None] * np.arange(INNER // 2)[None, :] % INNER
    angle = angle * (2.0 * np.pi / INNER)
    table = np.concatenate([np.cos(angle), np.sin(angle)], axis=1)
    return split_bf16(table.reshape(plan.n_col, plan.k2_dev // 2, 2, INNER).transpose(0, 2, 1, 3))


def twist_tables(plan):
    made = []
    for cells in (np.arange(0, INNER, FINE), np.arange(FINE)):
        angle = cells[:, None] * np.arange(plan.k1)[None, :] * (2.0 * np.pi / plan.n_pad)
        made.extend([np.cos(angle), np.sin(angle)])
    return np.concatenate(made).astype(np.float32)


def unit_phase(code):
    quadrant = (code + LEVELS // 8) >> 10
    rest = (code - (quadrant << 10)).astype(jnp.float32) * (2.0 * math.pi / LEVELS)
    sq = rest * rest
    cos = 1.0 + sq * (-1.0 / 2 + sq * (1.0 / 24 + sq * (-1.0 / 720 + sq * (1.0 / 40320))))
    sin = rest * (1.0 + sq * (-1.0 / 6 + sq * (1.0 / 120 + sq * (-1.0 / 5040 + sq * (1.0 / 362880)))))
    swap = (quadrant & 1) == 1
    minus_cos = ((quadrant + 1) & 2) == 2
    minus_sin = (quadrant & 2) == 2
    return jnp.where(swap, sin, cos), jnp.where(swap, cos, sin), minus_cos, minus_sin


def field_kernel(plan, tiles_ref, codes_ref, mask_ref, out_ref, open_ref):
    step_id = pl.program_id(0)
    pistons = []
    for i in range(plan.pupil_dev // TILE_C):
        piston = jnp.int32(0)
        for k in range(plan.row_dev // TILE_R):
            piston = piston + jnp.where(step_id >= k, tiles_ref[k, i], 0)
        pistons.append(piston)
    stride = 2 * plan.lane_parts * plan.n1_dev
    total = jnp.zeros((SUBS, LANES), jnp.float32)
    for t in range(TILE_R // SUBS):
        for j in range(plan.pupil_dev // LANES):
            rows = slice(t * SUBS, (t + 1) * SUBS)
            lanes = slice(j * LANES, (j + 1) * LANES)
            code = (codes_ref[rows, lanes] + pistons[j * LANES // TILE_C]) & (LEVELS - 1)
            cos, sin, minus_cos, minus_sin = unit_phase(code)
            amplitude = mask_ref[rows, lanes].astype(jnp.float32)
            total = total + amplitude
            real = cos * jnp.where(minus_cos, -amplitude, amplitude)
            imag = sin * jnp.where(minus_sin, -amplitude, amplitude)
            for part, value in enumerate((real, imag)):
                start = (part * plan.lane_parts + j % plan.lane_parts) * plan.n1_dev + j // plan.lane_parts
                for g in range(plan.n_groups):
                    out_ref[g, pl.ds(t * SUBS * stride + start, SUBS, stride=stride), :] = value

    @pl.when(step_id == 0)
    def _():
        open_ref[...] = total

    @pl.when(step_id > 0)
    def _():
        open_ref[...] = open_ref[...] + total


def own_kernel(plan, me_ref, tiles_ref, codes_ref, mask_ref, code_ref, kept_ref, open_ref):
    half = plan.row_dev // 2
    first = pl.multiple_of(me_ref[0] * half, half)
    total = jnp.zeros((SUBS, LANES), jnp.int32)
    for t in range(plan.row_dev // SUBS):
        for j in range(plan.pupil_dev // LANES):
            total = total + mask_ref[t * SUBS : (t + 1) * SUBS, j * LANES : (j + 1) * LANES]
    open_ref[...] = total
    for i in range(plan.pupil_dev // TILE_C):
        lanes = slice(i * TILE_C, (i + 1) * TILE_C)
        piston = jnp.int32(0)
        for k in range(plan.row_dev // TILE_R):
            piston = piston + jnp.where(first >= k * TILE_R, tiles_ref[k, i], 0)
        code_ref[:, lanes] = codes_ref[:, lanes] + piston
    kept_ref[...] = mask_ref[pl.ds(first, half), :]


def chip_field_kernel(plan, me_ref, *refs):
    n_other = plan.n_row - 1
    others, refs = (refs[:n_other], refs[n_other : 2 * n_other]), refs[2 * n_other :]
    near_tiles_ref, own_codes_ref, own_mask_ref, open_ref, near_codes_ref, near_mask_ref = refs[:6]
    outs, made_ref = refs[6:-1], refs[-1]
    core, chip, row = me_ref[0], me_ref[1], me_ref[2]
    half = plan.row_dev // 2
    first = pl.multiple_of(core * half, half)
    total = open_ref[...]
    for t in range(plan.row_dev // SUBS):
        for j in range(plan.pupil_dev // LANES):
            total = total + near_mask_ref[t * SUBS : (t + 1) * SUBS, j * LANES : (j + 1) * LANES]
    total = total.astype(jnp.float32)
    stride = 2 * plan.lane_parts * plan.n1_dev
    for owner in range(2):
        before = jnp.zeros((1, plan.pupil_dev // TILE_C), jnp.int32)
        for d, other in enumerate(others[owner]):
            before = before + jnp.where(row > d, jnp.sum(other[...], axis=0, keepdims=True), 0)
        if owner == 1:
            for k in range(plan.row_dev // TILE_R):
                before = before + jnp.where(first >= k * TILE_R, near_tiles_ref[k : k + 1], 0)
        codes, mask = ((own_codes_ref, own_mask_ref), (near_codes_ref, near_mask_ref))[owner]
        for t in range(half // SUBS):
            rows = pl.ds(t * SUBS, SUBS) if owner == 0 else pl.ds(pl.multiple_of(first + t * SUBS, SUBS), SUBS)
            for j in range(plan.pupil_dev // LANES):
                lanes = slice(j * LANES, (j + 1) * LANES)
                column = j * LANES // TILE_C
                piston = jnp.broadcast_to(before[:, column : column + 1], (SUBS, LANES))
                cos, sin, minus_cos, minus_sin = unit_phase((codes[rows, lanes] + piston) & (LEVELS - 1))
                amplitude = mask[rows, lanes].astype(jnp.float32)
                real = cos * jnp.where(minus_cos, -amplitude, amplitude)
                imag = sin * jnp.where(minus_sin, -amplitude, amplitude)
                for part, value in enumerate((real, imag)):
                    start = (part * plan.lane_parts + j % plan.lane_parts) * plan.n1_dev + j // plan.lane_parts
                    made_ref[owner, pl.ds(t * SUBS * stride + start, SUBS, stride=stride), :] = value
    own_rows = lax.rem(chip, plan.group // 2)
    for b, out in enumerate(outs):
        source = pl.multiple_of((own_rows ^ b % (plan.group // 2)) * plan.chunk, plan.chunk)
        for i in range(plan.chunk // plan.n1_dev):
            for side in range(2):
                block = made_ref[side ^ core, pl.ds(pl.multiple_of(source + i * plan.n1_dev, plan.n1_dev), plan.n1_dev), :]
                out[(2 * i + side) * plan.n1_dev : (2 * i + side + 1) * plan.n1_dev, :] = block
        out[2 * plan.chunk :, :] = total


def tables_kernel(plan, blocks, me_ref, outer_ref, inner_ref, twist_ref, w1_ref, w2_ref, turn_ref):
    me = me_ref[0]
    w1, w2 = ([], []), ([], [])
    for s in range(2):
        rows = [outer_ref[s, (me >> 1) ^ b if blocks > 1 else 0].astype(jnp.float32) for b in range(blocks)]
        for p in range(2):
            cos, sin = (jnp.concatenate([both[p, i] for both in rows]) for i in range(2))
            both = jnp.concatenate([jnp.concatenate([cos, sin]), jnp.concatenate([-sin, cos])], axis=1)
            w1[p].append(both.astype(jnp.bfloat16))
        for p in range(2):
            parts = []
            for b in range(plan.group):
                both = inner_ref[s, me ^ b, p].astype(jnp.float32)
                parts.append(both)
                parts.append(jnp.concatenate([-both[:, INNER // 2 :], both[:, : INNER // 2]], axis=1))
            w2[p].append(jnp.concatenate(parts).astype(jnp.bfloat16))
    for p in range(2):
        w1_ref[p] = jnp.concatenate([w1[p][0], w1[p][0], w1[p][1]])
        w2_ref[p] = jnp.concatenate([w2[p][0], w2[p][1]])
    turn_ref[...] = twist_ref[...]


def chip_transform_kernel(plan, order, *refs):
    n_chips = plan.n_col // 2
    chunks = [refs[order.index(b)] for b in range(n_chips)]
    tables, outs, count_ref = refs[n_chips : n_chips + 3], refs[n_chips + 3 : -1], refs[-1]
    count = chunks[0][2 * plan.chunk :, :]
    for chunk in chunks[1:]:
        count = count + chunk[2 * plan.chunk :, :]
    count_ref[...] = count
    n1_chip = 2 * plan.n1_dev

    def part_of(r, part, p):
        pieces = []
        for lt in range(plan.lane_parts):
            at = ((r * 2 + part) * plan.lane_parts + lt) * n1_chip + p
            pieces.append(jnp.concatenate([chunk[pl.ds(at, n1_chip // 2, stride=2), :] for chunk in chunks]))
        return jnp.concatenate(pieces, axis=1)

    fields = []
    for p in range(2):
        fields.append([jnp.concatenate([part_of(r, 0, p), part_of(r, 1, p)]) for r in range(plan.rows)])
    transform_rows(plan, fields, tables, outs)


def transform_kernel(plan, info_ref, x_ref, *refs):
    chunk_row = plan.chunk // plan.rows
    n1_half, n1_dev = plan.n1 // 2, plan.n1_dev // 2
    info = info_ref[: plan.n_col]
    info = jnp.broadcast_to(info[:, None, :], (plan.n_col, n1_dev, LANES)).reshape(n1_half, LANES)
    tile = lax.broadcasted_iota(jnp.int32, info.shape, 0) % n1_dev * 2 * INNER // TILE_C
    own = lax.broadcasted_iota(jnp.int32, info.shape, 1) == tile
    before = jnp.sum(jnp.where(own, info, 0.0), axis=1, keepdims=True).astype(jnp.int32)
    turn_cos, turn_sin, minus_cos, minus_sin = unit_phase(before)
    turn_cos = jnp.where(minus_cos, -turn_cos, turn_cos)
    turn_sin = jnp.where(minus_sin, -turn_sin, turn_sin)

    def field_of(r, p):
        halves = []
        for part in range(2):
            pieces = []
            for lt in range(plan.lane_parts):
                at = r * chunk_row + (part * plan.lane_parts + lt) * plan.n1_dev + p
                cells = [x_ref[:, at + 2 * i : at + 2 * i + 1, :] for i in range(n1_dev)]
                pieces.append(jnp.concatenate(cells, axis=1).reshape(n1_half, LANES))
            halves.append(jnp.concatenate(pieces, axis=1))
        real, imag = halves
        return jnp.concatenate([real * turn_cos - imag * turn_sin, real * turn_sin + imag * turn_cos], axis=0)

    fields = [[field_of(r, p) for r in range(plan.rows)] for p in range(2)]
    transform_rows(plan, fields, refs[:3], refs[3:])


def transform_rows(plan, fields, tables, outs):
    w1_ref, w2_ref, turn_ref = tables
    ys = []
    for p in range(2):
        x = jnp.concatenate(fields[p], axis=1)
        xh = x.astype(jnp.bfloat16)
        xl = (x - xh.astype(jnp.float32)).astype(jnp.bfloat16)
        ys.append(
            lax.dot_general(
                jnp.concatenate([xh, xl, xh]), w1_ref[p], (((0,), (0,)), ((), ())), preferred_element_type=jnp.float32
            )
        )
    tc, ts = [], []
    count = INNER // FINE
    fine_cos, fine_sin = turn_ref[2 * count : 2 * count + FINE], turn_ref[2 * count + FINE :]
    for a in range(count):
        cos, sin = turn_ref[a : a + 1], turn_ref[count + a : count + a + 1]
        tc.append(cos * fine_cos - sin * fine_sin)
        ts.append(sin * fine_cos + cos * fine_sin)
    tc, ts = jnp.concatenate(tc), jnp.concatenate(ts)
    fs = ([], [])
    for r in range(plan.rows):
        even, odd = (y[r * INNER : (r + 1) * INNER] for y in ys)
        y = [even + odd, even - odd]
        yr, yi = (jnp.concatenate([one[:, i * plan.k1 // 2 : (i + 1) * plan.k1 // 2] for one in y], axis=1) for i in range(2))
        fr, fi = yr * tc + yi * ts, yi * tc - yr * ts
        for p in range(2):
            pair = [f[: INNER // 2] + f[INNER // 2 :] if p == 0 else f[: INNER // 2] - f[INNER // 2 :] for f in (fr, fi)]
            fs[p].append(jnp.concatenate(pair))
    half = plan.k2_dev // 2
    for p in range(2):
        f = jnp.concatenate(fs[p], axis=1)
        fh = f.astype(jnp.bfloat16)
        fl = (f - fh.astype(jnp.float32)).astype(jnp.bfloat16)
        size = plan.group * plan.k2_dev
        z = jnp.dot(w2_ref[p], fh, preferred_element_type=jnp.float32)
        z = z[:size] + z[size:] + jnp.dot(w2_ref[p, :size], fl, preferred_element_type=jnp.float32)
        for r in range(plan.rows):
            for b in range(plan.group):
                part = z[b * plan.k2_dev : (b + 1) * plan.k2_dev, r * plan.k1 : (r + 1) * plan.k1]
                outs[b][r, :, p * half : (p + 1) * half, :] = part.reshape(2, half, plan.k1)


def merge_kernel(plan, swap_bit, me_ref, *refs):
    chunks = [refs[(ORDER + (0,)).index(b)] for b in range(plan.group)]
    counts = refs[plan.group : plan.group + plan.n_row]
    out_ref, tile_ref, sems = refs[plan.group + plan.n_row :]
    total = counts[0][...]
    for other in counts[1:]:
        total = total + other[...]
    total = jnp.sum(jnp.sum(total, axis=0, keepdims=True), axis=1, keepdims=True)
    scale = jnp.sqrt(float(plan.rows_all) / total)
    inside = lax.rem(me_ref[0], plan.group)
    swapped = lax.rem(inside // swap_bit, 2) == 1
    half = plan.k2_dev // 2
    stride = 2 * plan.k1_tiles * SUBS
    copies = []
    for slot in range(plan.group):
        part = slot % 2
        base = [b for b in range(plan.group) if b & swap_bit == 0][slot // 2]
        for r in range(plan.rows):
            for p in range(2):
                for j in range(plan.k1_tiles):
                    rows, lanes = slice(p * half, (p + 1) * half), slice(j * LANES, (j + 1) * LANES)
                    a = chunks[base][r, part, rows, lanes] * scale
                    b = chunks[base + swap_bit][r, part, rows, lanes] * scale
                    at = (p * plan.k1_tiles + j) * SUBS + r
                    tile_ref[slot, pl.ds(at, half, stride=stride), :] = jnp.where(swapped, b, a)
                    tile_ref[slot, pl.ds(at + plan.rows, half, stride=stride), :] = jnp.where(swapped, a, b)
        source = inside ^ base
        tile = source // 2 if swap_bit == 1 else source % 2 * 2 + source // 4
        copy = pltpu.make_async_copy(tile_ref.at[slot], out_ref.at[part, tile], sems.at[slot])
        copy.start()
        copies.append(copy)
    for copy in copies:
        copy.wait()


def along_rows(n_row, value):
    return [lax.ppermute(value, "row", [(i, (i + d) % n_row) for i in range(n_row)]) for d in range(1, n_row)]


def spectra_shapes(plan):
    return [jax.ShapeDtypeStruct((plan.rows, 2, plan.k2_dev, plan.k1), jnp.float32)] * plan.group


def ready_tables(plan, me, blocks):
    smem, vmem = pl.BlockSpec(memory_space=pltpu.SMEM), pl.BlockSpec(memory_space=pltpu.VMEM)
    return pl.pallas_call(
        partial(tables_kernel, plan, blocks),
        out_shape=[
            jax.ShapeDtypeStruct((2, 3 * plan.n1, plan.k1), jnp.bfloat16),
            jax.ShapeDtypeStruct((2, 2 * plan.group * plan.k2_dev, INNER), jnp.bfloat16),
            jax.ShapeDtypeStruct((2 * (INNER // FINE + FINE), plan.k1), jnp.float32),
        ],
        in_specs=[smem] + [vmem] * 3,
        out_specs=[vmem] * 3,
        compiler_params=pltpu.CompilerParams(vmem_limit_bytes=24 * 2**20),
        name="tables",
    )(me, outer_tables(plan, blocks), inner_tables(plan), twist_tables(plan))


def spectra_by_chip(plan, phase_codes, aperture, tile_offsets):
    n_col, n_row = plan.n_col, plan.n_row
    n_chips = n_col // 2
    half = plan.row_dev // 2
    row_index = lax.axis_index("row").astype(jnp.int32)
    col_index = lax.axis_index("col").astype(jnp.int32)
    smem, vmem = pl.BlockSpec(memory_space=pltpu.SMEM), pl.BlockSpec(memory_space=pltpu.VMEM)
    swap = [(q, q ^ 1) for q in range(n_col)]
    others = along_rows(n_row, tile_offsets)
    near_others = []
    for d in range(1, n_row):
        pairs = [(r * n_col + q, (r + d) % n_row * n_col + (q ^ 1)) for r in range(n_row) for q in range(n_col)]
        near_others.append(lax.ppermute(tile_offsets, ("row", "col"), pairs))
    near = [lax.ppermute(value, "col", swap) for value in (tile_offsets, phase_codes, aperture)]
    place = jnp.stack([col_index % 2, col_index // 2, row_index])
    own = pl.pallas_call(
        partial(own_kernel, plan),
        out_shape=[jax.ShapeDtypeStruct((half, plan.pupil_dev), jnp.int32)] * 2
        + [jax.ShapeDtypeStruct((SUBS, LANES), jnp.int32)],
        grid_spec=pltpu.PrefetchScalarGridSpec(
            num_scalar_prefetch=1,
            grid=(1,),
            in_specs=[
                smem,
                pl.BlockSpec((half, plan.pupil_dev), lambda i, p: (p[0], 0)),
                pl.BlockSpec((plan.row_dev, plan.pupil_dev), lambda i, p: (0, 0)),
            ],
            out_specs=[vmem] * 3,
        ),
        compiler_params=pltpu.CompilerParams(vmem_limit_bytes=16 * 2**20),
        name="own",
    )(place, *(pltpu.with_memory_space_constraint(a, pltpu.HBM) for a in (tile_offsets, phase_codes, aperture)))
    block = jax.ShapeDtypeStruct((2 * plan.chunk + SUBS, LANES), jnp.float32)
    rows = pl.pallas_call(
        partial(chip_field_kernel, plan),
        out_shape=[block] * n_chips,
        in_specs=[smem] + [vmem] * (2 * n_row + 4),
        out_specs=[vmem] * n_chips,
        scratch_shapes=[pltpu.VMEM((2, half * plan.chunk // plan.rows, LANES), jnp.float32)],
        compiler_params=pltpu.CompilerParams(vmem_limit_bytes=16 * 2**20),
        name="field",
    )(place, *others, *near_others, near[0], *own, near[1], near[2])
    order = CHIP_ORDER + (0,)
    received = [rows[0] if b == 0 else lax.ppermute(rows[b], "col", [(q, q ^ 2 * b) for q in range(n_col)]) for b in order]
    *made, opened = pl.pallas_call(
        partial(chip_transform_kernel, plan, order),
        out_shape=spectra_shapes(plan) + [jax.ShapeDtypeStruct((SUBS, LANES), jnp.float32)],
        in_specs=[vmem] * (n_chips + 3),
        out_specs=[vmem] * (plan.group + 1),
        compiler_params=pltpu.CompilerParams(vmem_limit_bytes=24 * 2**20),
        name="transform",
    )(*received, *ready_tables(plan, col_index.reshape(1), n_chips))
    return made, opened


def spectra_by_device(plan, phase_codes, aperture, tile_offsets):
    n_col, n_row = plan.n_col, plan.n_row
    row_index = lax.axis_index("row")
    col_index = lax.axis_index("col")
    me = col_index.astype(jnp.int32).reshape(1)
    smem = pl.BlockSpec(memory_space=pltpu.SMEM)
    vmem = pl.BlockSpec(memory_space=pltpu.VMEM)
    before = jnp.zeros((1, plan.pupil_dev // TILE_C), jnp.int32)
    for d, other in enumerate(along_rows(n_row, tile_offsets)):
        before = before + jnp.where(row_index > d, jnp.sum(other, axis=0, keepdims=True), 0)
    before = jnp.pad((before & (LEVELS - 1)).astype(jnp.float32), ((0, 0), (0, LANES - before.shape[1])))
    mine = jnp.arange(n_col, dtype=jnp.int32)[:, None] == col_index

    field_rows = plan.row_dev * 2 * plan.lane_parts * plan.n1_dev
    steps = plan.row_dev // TILE_R
    packed, opened = pl.pallas_call(
        partial(field_kernel, plan),
        out_shape=[
            jax.ShapeDtypeStruct((plan.n_groups, field_rows, LANES), jnp.float32),
            jax.ShapeDtypeStruct((SUBS, LANES), jnp.float32),
        ],
        grid=(steps,),
        in_specs=[
            smem,
            pl.BlockSpec((TILE_R, plan.pupil_dev), lambda t: (t, 0)),
            pl.BlockSpec((TILE_R, plan.pupil_dev), lambda t: (t, 0)),
        ],
        out_specs=[
            pl.BlockSpec((plan.n_groups, field_rows // steps, LANES), lambda t: (0, t, 0)),
            pl.BlockSpec((SUBS, LANES), lambda t: (0, 0)),
        ],
        name="field",
    )(tile_offsets, phase_codes, aperture)
    packed = packed.reshape(n_col, plan.chunk, LANES)
    received = lax.all_to_all(packed, "col", split_axis=0, concat_axis=0, tiled=True)

    info = jnp.concatenate([jnp.where(mine, before, 0.0), opened])
    for bit in range(n_col.bit_length() - 1):
        info = info + lax.ppermute(info, "col", [(q, q ^ 1 << bit) for q in range(n_col)])
    made = pl.pallas_call(
        partial(transform_kernel, plan),
        out_shape=spectra_shapes(plan),
        in_specs=[vmem] * 5,
        out_specs=[vmem] * plan.group,
        compiler_params=pltpu.CompilerParams(vmem_limit_bytes=24 * 2**20),
        name="transform",
    )(info, received, *ready_tables(plan, me, 1))
    return made, info[n_col:]


def per_device(phase_codes, aperture, tile_offsets):
    n_col = lax.axis_size("col")
    n_row = lax.axis_size("row")
    plan = Plan(*phase_codes.shape, n_col, n_row)
    by_chip = plan.n1_dev % SUBS == 0 and len(CHIP_ORDER) == n_col // 2 - 1
    spectra = spectra_by_chip if by_chip else spectra_by_device
    made, opened = spectra(plan, phase_codes, aperture, tile_offsets)
    chunks = [lax.ppermute(made[b], "col", [(q, q ^ b) for q in range(n_col)]) for b in ORDER] + [made[0]]
    opened, chunks[2] = lax.optimization_barrier((opened, chunks[2]))
    counts = [opened] + along_rows(n_row, opened)
    smem = pl.BlockSpec(memory_space=pltpu.SMEM)
    vmem = pl.BlockSpec(memory_space=pltpu.VMEM)
    tiles = plan.row_dev // SUBS
    out = pl.pallas_call(
        partial(merge_kernel, plan, 2 if by_chip else 1),
        out_shape=jax.ShapeDtypeStruct((2, tiles, plan.freq_tiles * SUBS, LANES), jnp.float32),
        in_specs=[smem] + [vmem] * (plan.group + n_row),
        out_specs=pl.BlockSpec(memory_space=pl.ANY),
        scratch_shapes=[
            pltpu.VMEM((plan.group, plan.freq_tiles * SUBS, LANES), jnp.float32),
            pltpu.SemaphoreType.DMA((plan.group,)),
        ],
        compiler_params=pltpu.CompilerParams(vmem_limit_bytes=24 * 2**20),
        name="merge",
    )(lax.axis_index("col").astype(jnp.int32).reshape(1), *chunks, *counts)
    out = out.reshape(2, tiles, plan.freq_tiles, SUBS, LANES).transpose(0, 1, 3, 2, 4)
    return out.reshape(2, plan.row_dev, plan.freq_tiles * LANES)


def solution(mesh):
    placed = (P("row", "col"), P("row", "col"), P("row", "col"))
    return jax.shard_map(
        per_device, mesh=mesh, in_specs=placed, out_specs=P(None, "row", "col"), check_vma=False
    )
```

```python
import math
from functools import partial

import jax
import jax.numpy as jnp
import ml_dtypes
import numpy as np
from jax import lax
from jax.experimental import pallas as pl
from jax.experimental.pallas import tpu as pltpu
from jax.sharding import PartitionSpec as P

LEVELS = 4096
TILE_R = 16
TILE_C = 512
LANES = 128
SUBS = 8
INNER = 256
PAD = 4
FINE = 16
CHIP_ORDER = (4, 1, 5, 3, 6, 2, 7)
ORDER = (6, 4, 2, 7, 5, 3, 1)
GROUP = 8


class Plan:
    def __init__(self, row_dev, pupil_dev, n_col, n_row):
        self.row_dev = row_dev
        self.pupil_dev = pupil_dev
        self.n_col = n_col
        self.n_row = n_row
        self.rows_all = row_dev * n_row
        self.group = min(GROUP, n_col)
        self.n_groups = n_col // self.group
        self.rows = row_dev // self.group
        self.n_pupil = pupil_dev * n_col
        self.n_pad = PAD * self.n_pupil
        self.n1 = self.n_pupil // INNER
        self.k1 = PAD * self.n1
        self.n1_dev = pupil_dev // INNER
        self.k2_group = INNER // self.n_groups
        self.k2_dev = INNER // n_col
        self.freq_tiles = PAD * pupil_dev // LANES
        self.k1_tiles = self.k1 // LANES
        self.lane_parts = INNER // LANES
        self.chunk = self.rows * 2 * self.lane_parts * self.n1_dev


def split_bf16(table):
    high = table.astype(ml_dtypes.bfloat16)
    low = (table - high.astype(np.float64)).astype(ml_dtypes.bfloat16)
    return np.stack([high, low])


def outer_tables(plan, blocks):
    k1 = plan.k1 // 2
    angle = np.arange(plan.n1)[:, None] * np.arange(k1)[None, :] % plan.k1
    angle = angle * (2.0 * np.pi / plan.k1)
    table = np.stack([np.cos(angle), np.sin(angle)]).reshape(2, blocks, plan.n1 // blocks // 2, 2, k1)
    return split_bf16(table.transpose(1, 3, 0, 2, 4))


def inner_tables(plan):
    angle = np.arange(INNER)[:, None] * np.arange(INNER // 2)[None, :] % INNER
    angle = angle * (2.0 * np.pi / INNER)
    table = np.concatenate([np.cos(angle), np.sin(angle)], axis=1)
    return split_bf16(table.reshape(plan.n_col, plan.k2_dev // 2, 2, INNER).transpose(0, 2, 1, 3))


def twist_tables(plan):
    made = []
    for cells in (np.arange(0, INNER, FINE), np.arange(FINE)):
        angle = cells[:, None] * np.arange(plan.k1)[None, :] * (2.0 * np.pi / plan.n_pad)
        made.extend([np.cos(angle), np.sin(angle)])
    return np.concatenate(made).astype(np.float32)


def unit_phase(code):
    quadrant = (code + LEVELS // 8) >> 10
    rest = (code - (quadrant << 10)).astype(jnp.float32) * (2.0 * math.pi / LEVELS)
    sq = rest * rest
    cos = 1.0 + sq * (-1.0 / 2 + sq * (1.0 / 24 + sq * (-1.0 / 720 + sq * (1.0 / 40320))))
    sin = rest * (1.0 + sq * (-1.0 / 6 + sq * (1.0 / 120 + sq * (-1.0 / 5040 + sq * (1.0 / 362880)))))
    swap = (quadrant & 1) == 1
    minus_cos = ((quadrant + 1) & 2) == 2
    minus_sin = (quadrant & 2) == 2
    return jnp.where(swap, sin, cos), jnp.where(swap, cos, sin), minus_cos, minus_sin


def field_kernel(plan, tiles_ref, codes_ref, mask_ref, out_ref, open_ref):
    step_id = pl.program_id(0)
    pistons = []
    for i in range(plan.pupil_dev // TILE_C):
        piston = jnp.int32(0)
        for k in range(plan.row_dev // TILE_R):
            piston = piston + jnp.where(step_id >= k, tiles_ref[k, i], 0)
        pistons.append(piston)
    stride = 2 * plan.lane_parts * plan.n1_dev
    total = jnp.zeros((SUBS, LANES), jnp.float32)
    for t in range(TILE_R // SUBS):
        for j in range(plan.pupil_dev // LANES):
            rows = slice(t * SUBS, (t + 1) * SUBS)
            lanes = slice(j * LANES, (j + 1) * LANES)
            code = (codes_ref[rows, lanes] + pistons[j * LANES // TILE_C]) & (LEVELS - 1)
            cos, sin, minus_cos, minus_sin = unit_phase(code)
            amplitude = mask_ref[rows, lanes].astype(jnp.float32)
            total = total + amplitude
            real = cos * jnp.where(minus_cos, -amplitude, amplitude)
            imag = sin * jnp.where(minus_sin, -amplitude, amplitude)
            for part, value in enumerate((real, imag)):
                start = (part * plan.lane_parts + j % plan.lane_parts) * plan.n1_dev + j // plan.lane_parts
                for g in range(plan.n_groups):
                    out_ref[g, pl.ds(t * SUBS * stride + start, SUBS, stride=stride), :] = value

    @pl.when(step_id == 0)
    def _():
        open_ref[...] = total

    @pl.when(step_id > 0)
    def _():
        open_ref[...] = open_ref[...] + total


def own_kernel(plan, me_ref, tiles_ref, codes_ref, mask_ref, code_ref, kept_ref, open_ref):
    half = plan.row_dev // 2
    first = pl.multiple_of(me_ref[0] * half, half)
    total = jnp.zeros((SUBS, LANES), jnp.int32)
    for t in range(plan.row_dev // SUBS):
        for j in range(plan.pupil_dev // LANES):
            total = total + mask_ref[t * SUBS : (t + 1) * SUBS, j * LANES : (j + 1) * LANES]
    open_ref[...] = total
    for i in range(plan.pupil_dev // TILE_C):
        lanes = slice(i * TILE_C, (i + 1) * TILE_C)
        piston = jnp.int32(0)
        for k in range(plan.row_dev // TILE_R):
            piston = piston + jnp.where(first >= k * TILE_R, tiles_ref[k, i], 0)
        code_ref[:, lanes] = codes_ref[:, lanes] + piston
    kept_ref[...] = mask_ref[pl.ds(first, half), :]


def chip_field_kernel(plan, me_ref, *refs):
    n_other = plan.n_row - 1
    others, refs = (refs[:n_other], refs[n_other : 2 * n_other]), refs[2 * n_other :]
    near_tiles_ref, own_codes_ref, own_mask_ref, open_ref, near_codes_ref, near_mask_ref = refs[:6]
    outs, made_ref = refs[6:-1], refs[-1]
    core, chip, row = me_ref[0], me_ref[1], me_ref[2]
    half = plan.row_dev // 2
    first = pl.multiple_of(core * half, half)
    total = open_ref[...]
    for t in range(plan.row_dev // SUBS):
        for j in range(plan.pupil_dev // LANES):
            total = total + near_mask_ref[t * SUBS : (t + 1) * SUBS, j * LANES : (j + 1) * LANES]
    total = total.astype(jnp.float32)
    stride = 2 * plan.lane_parts * plan.n1_dev
    for owner in range(2):
        before = jnp.zeros((1, plan.pupil_dev // TILE_C), jnp.int32)
        for d, other in enumerate(others[owner]):
            before = before + jnp.where(row > d, jnp.sum(other[...], axis=0, keepdims=True), 0)
        if owner == 1:
            for k in range(plan.row_dev // TILE_R):
                before = before + jnp.where(first >= k * TILE_R, near_tiles_ref[k : k + 1], 0)
        codes, mask = ((own_codes_ref, own_mask_ref), (near_codes_ref, near_mask_ref))[owner]
        for t in range(half // SUBS):
            rows = pl.ds(t * SUBS, SUBS) if owner == 0 else pl.ds(pl.multiple_of(first + t * SUBS, SUBS), SUBS)
            for j in range(plan.pupil_dev // LANES):
                lanes = slice(j * LANES, (j + 1) * LANES)
                column = j * LANES // TILE_C
                piston = jnp.broadcast_to(before[:, column : column + 1], (SUBS, LANES))
                cos, sin, minus_cos, minus_sin = unit_phase((codes[rows, lanes] + piston) & (LEVELS - 1))
                amplitude = mask[rows, lanes].astype(jnp.float32)
                real = cos * jnp.where(minus_cos, -amplitude, amplitude)
                imag = sin * jnp.where(minus_sin, -amplitude, amplitude)
                for part, value in enumerate((real, imag)):
                    start = (part * plan.lane_parts + j % plan.lane_parts) * plan.n1_dev + j // plan.lane_parts
                    made_ref[owner, pl.ds(t * SUBS * stride + start, SUBS, stride=stride), :] = value
    own_rows = lax.rem(chip, plan.group // 2)
    for b, out in enumerate(outs):
        source = pl.multiple_of((own_rows ^ b % (plan.group // 2)) * plan.chunk, plan.chunk)
        for i in range(plan.chunk // plan.n1_dev):
            for side in range(2):
                block = made_ref[side ^ core, pl.ds(pl.multiple_of(source + i * plan.n1_dev, plan.n1_dev), plan.n1_dev), :]
                out[(2 * i + side) * plan.n1_dev : (2 * i + side + 1) * plan.n1_dev, :] = block
        out[2 * plan.chunk :, :] = total


def tables_kernel(plan, blocks, me_ref, outer_ref, inner_ref, twist_ref, w1_ref, w2_ref, turn_ref):
    me = me_ref[0]
    w1, w2 = ([], []), ([], [])
    for s in range(2):
        rows = [outer_ref[s, (me >> 1) ^ b if blocks > 1 else 0].astype(jnp.float32) for b in range(blocks)]
        for p in range(2):
            cos, sin = (jnp.concatenate([both[p, i] for both in rows]) for i in range(2))
            both = jnp.concatenate([jnp.concatenate([cos, sin]), jnp.concatenate([-sin, cos])], axis=1)
            w1[p].append(both.astype(jnp.bfloat16))
        for p in range(2):
            parts = []
            for b in range(plan.group):
                both = inner_ref[s, me ^ b, p].astype(jnp.float32)
                parts.append(both)
                parts.append(jnp.concatenate([-both[:, INNER // 2 :], both[:, : INNER // 2]], axis=1))
            w2[p].append(jnp.concatenate(parts).astype(jnp.bfloat16))
    for p in range(2):
        w1_ref[p] = jnp.concatenate([w1[p][0], w1[p][0], w1[p][1]])
        w2_ref[p] = jnp.concatenate([w2[p][0], w2[p][1]])
    turn_ref[...] = twist_ref[...]


def chip_transform_kernel(plan, order, *refs):
    n_chips = plan.n_col // 2
    chunks = [refs[order.index(b)] for b in range(n_chips)]
    tables, outs, count_ref = refs[n_chips : n_chips + 3], refs[n_chips + 3 : -1], refs[-1]
    count = chunks[0][2 * plan.chunk :, :]
    for chunk in chunks[1:]:
        count = count + chunk[2 * plan.chunk :, :]
    count_ref[...] = count
    n1_chip = 2 * plan.n1_dev

    def part_of(r, part, p):
        pieces = []
        for lt in range(plan.lane_parts):
            at = ((r * 2 + part) * plan.lane_parts + lt) * n1_chip + p
            pieces.append(jnp.concatenate([chunk[pl.ds(at, n1_chip // 2, stride=2), :] for chunk in chunks]))
        return jnp.concatenate(pieces, axis=1)

    fields = []
    for p in range(2):
        fields.append([jnp.concatenate([part_of(r, 0, p), part_of(r, 1, p)]) for r in range(plan.rows)])
    transform_rows(plan, fields, tables, outs)


def transform_kernel(plan, info_ref, x_ref, *refs):
    chunk_row = plan.chunk // plan.rows
    n1_half, n1_dev = plan.n1 // 2, plan.n1_dev // 2
    info = info_ref[: plan.n_col]
    info = jnp.broadcast_to(info[:, None, :], (plan.n_col, n1_dev, LANES)).reshape(n1_half, LANES)
    tile = lax.broadcasted_iota(jnp.int32, info.shape, 0) % n1_dev * 2 * INNER // TILE_C
    own = lax.broadcasted_iota(jnp.int32, info.shape, 1) == tile
    before = jnp.sum(jnp.where(own, info, 0.0), axis=1, keepdims=True).astype(jnp.int32)
    turn_cos, turn_sin, minus_cos, minus_sin = unit_phase(before)
    turn_cos = jnp.where(minus_cos, -turn_cos, turn_cos)
    turn_sin = jnp.where(minus_sin, -turn_sin, turn_sin)

    def field_of(r, p):
        halves = []
        for part in range(2):
            pieces = []
            for lt in range(plan.lane_parts):
                at = r * chunk_row + (part * plan.lane_parts + lt) * plan.n1_dev + p
                cells = [x_ref[:, at + 2 * i : at + 2 * i + 1, :] for i in range(n1_dev)]
                pieces.append(jnp.concatenate(cells, axis=1).reshape(n1_half, LANES))
            halves.append(jnp.concatenate(pieces, axis=1))
        real, imag = halves
        return jnp.concatenate([real * turn_cos - imag * turn_sin, real * turn_sin + imag * turn_cos], axis=0)

    fields = [[field_of(r, p) for r in range(plan.rows)] for p in range(2)]
    transform_rows(plan, fields, refs[:3], refs[3:])


def transform_rows(plan, fields, tables, outs):
    w1_ref, w2_ref, turn_ref = tables
    ys = []
    for p in range(2):
        x = jnp.concatenate(fields[p], axis=1)
        xh = x.astype(jnp.bfloat16)
        xl = (x - xh.astype(jnp.float32)).astype(jnp.bfloat16)
        ys.append(
            lax.dot_general(
                jnp.concatenate([xh, xl, xh]), w1_ref[p], (((0,), (0,)), ((), ())), preferred_element_type=jnp.float32
            )
        )
    tc, ts = [], []
    count = INNER // FINE
    fine_cos, fine_sin = turn_ref[2 * count : 2 * count + FINE], turn_ref[2 * count + FINE :]
    for a in range(count):
        cos, sin = turn_ref[a : a + 1], turn_ref[count + a : count + a + 1]
        tc.append(cos * fine_cos - sin * fine_sin)
        ts.append(sin * fine_cos + cos * fine_sin)
    tc, ts = jnp.concatenate(tc), jnp.concatenate(ts)
    fs = ([], [])
    for r in range(plan.rows):
        even, odd = (y[r * INNER : (r + 1) * INNER] for y in ys)
        y = [even + odd, even - odd]
        yr, yi = (jnp.concatenate([one[:, i * plan.k1 // 2 : (i + 1) * plan.k1 // 2] for one in y], axis=1) for i in range(2))
        fr, fi = yr * tc + yi * ts, yi * tc - yr * ts
        for p in range(2):
            pair = [f[: INNER // 2] + f[INNER // 2 :] if p == 0 else f[: INNER // 2] - f[INNER // 2 :] for f in (fr, fi)]
            fs[p].append(jnp.concatenate(pair))
    half = plan.k2_dev // 2
    for p in range(2):
        f = jnp.concatenate(fs[p], axis=1)
        fh = f.astype(jnp.bfloat16)
        fl = (f - fh.astype(jnp.float32)).astype(jnp.bfloat16)
        size = plan.group * plan.k2_dev
        z = jnp.dot(w2_ref[p], fh, preferred_element_type=jnp.float32)
        z = z[:size] + z[size:] + jnp.dot(w2_ref[p, :size], fl, preferred_element_type=jnp.float32)
        for r in range(plan.rows):
            for b in range(plan.group):
                part = z[b * plan.k2_dev : (b + 1) * plan.k2_dev, r * plan.k1 : (r + 1) * plan.k1]
                outs[b][r, :, p * half : (p + 1) * half, :] = part.reshape(2, half, plan.k1)


def merge_kernel(plan, swap_bit, me_ref, *refs):
    chunks = [refs[(ORDER + (0,)).index(b)] for b in range(plan.group)]
    counts = refs[plan.group : plan.group + plan.n_row]
    out_ref, tile_ref, sems = refs[plan.group + plan.n_row :]
    total = counts[0][...]
    for other in counts[1:]:
        total = total + other[...]
    total = jnp.sum(jnp.sum(total, axis=0, keepdims=True), axis=1, keepdims=True)
    scale = jnp.sqrt(float(plan.rows_all) / total)
    inside = lax.rem(me_ref[0], plan.group)
    swapped = lax.rem(inside // swap_bit, 2) == 1
    half = plan.k2_dev // 2
    stride = 2 * plan.k1_tiles * SUBS
    copies = []
    for slot in range(plan.group):
        part = slot % 2
        base = [b for b in range(plan.group) if b & swap_bit == 0][slot // 2]
        for r in range(plan.rows):
            for p in range(2):
                for j in range(plan.k1_tiles):
                    rows, lanes = slice(p * half, (p + 1) * half), slice(j * LANES, (j + 1) * LANES)
                    a = chunks[base][r, part, rows, lanes] * scale
                    b = chunks[base + swap_bit][r, part, rows, lanes] * scale
                    at = (p * plan.k1_tiles + j) * SUBS + r
                    tile_ref[slot, pl.ds(at, half, stride=stride), :] = jnp.where(swapped, b, a)
                    tile_ref[slot, pl.ds(at + plan.rows, half, stride=stride), :] = jnp.where(swapped, a, b)
        source = inside ^ base
        tile = source // 2 if swap_bit == 1 else source % 2 * 2 + source // 4
        whole = tile_ref.at[slot, pl.ds(0, plan.freq_tiles * SUBS), :]
        copy = pltpu.make_async_copy(whole, out_ref.at[part, tile], sems.at[slot])
        copy.start()
        copies.append(copy)
    for copy in copies:
        copy.wait()


def along_rows(n_row, value):
    return [lax.ppermute(value, "row", [(i, (i + d) % n_row) for i in range(n_row)]) for d in range(1, n_row)]


def spectra_shapes(plan):
    return [jax.ShapeDtypeStruct((plan.rows, 2, plan.k2_dev, plan.k1), jnp.float32)] * plan.group


def ready_tables(plan, me, blocks):
    smem, vmem = pl.BlockSpec(memory_space=pltpu.SMEM), pl.BlockSpec(memory_space=pltpu.VMEM)
    return pl.pallas_call(
        partial(tables_kernel, plan, blocks),
        out_shape=[
            jax.ShapeDtypeStruct((2, 3 * plan.n1, plan.k1), jnp.bfloat16),
            jax.ShapeDtypeStruct((2, 2 * plan.group * plan.k2_dev, INNER), jnp.bfloat16),
            jax.ShapeDtypeStruct((2 * (INNER // FINE + FINE), plan.k1), jnp.float32),
        ],
        in_specs=[smem] + [vmem] * 3,
        out_specs=[vmem] * 3,
        compiler_params=pltpu.CompilerParams(vmem_limit_bytes=24 * 2**20),
        name="tables",
    )(me, outer_tables(plan, blocks), inner_tables(plan), twist_tables(plan))


def spectra_by_chip(plan, phase_codes, aperture, tile_offsets):
    n_col, n_row = plan.n_col, plan.n_row
    n_chips = n_col // 2
    half = plan.row_dev // 2
    row_index = lax.axis_index("row").astype(jnp.int32)
    col_index = lax.axis_index("col").astype(jnp.int32)
    smem, vmem = pl.BlockSpec(memory_space=pltpu.SMEM), pl.BlockSpec(memory_space=pltpu.VMEM)
    swap = [(q, q ^ 1) for q in range(n_col)]
    others = along_rows(n_row, tile_offsets)
    near_others = []
    for d in range(1, n_row):
        pairs = [(r * n_col + q, (r + d) % n_row * n_col + (q ^ 1)) for r in range(n_row) for q in range(n_col)]
        near_others.append(lax.ppermute(tile_offsets, ("row", "col"), pairs))
    near = [lax.ppermute(value, "col", swap) for value in (tile_offsets, phase_codes, aperture)]
    place = jnp.stack([col_index % 2, col_index // 2, row_index])
    own = pl.pallas_call(
        partial(own_kernel, plan),
        out_shape=[jax.ShapeDtypeStruct((half, plan.pupil_dev), jnp.int32)] * 2
        + [jax.ShapeDtypeStruct((SUBS, LANES), jnp.int32)],
        grid_spec=pltpu.PrefetchScalarGridSpec(
            num_scalar_prefetch=1,
            grid=(1,),
            in_specs=[
                smem,
                pl.BlockSpec((half, plan.pupil_dev), lambda i, p: (p[0], 0)),
                pl.BlockSpec((plan.row_dev, plan.pupil_dev), lambda i, p: (0, 0)),
            ],
            out_specs=[vmem] * 3,
        ),
        compiler_params=pltpu.CompilerParams(vmem_limit_bytes=16 * 2**20),
        name="own",
    )(place, *(pltpu.with_memory_space_constraint(a, pltpu.HBM) for a in (tile_offsets, phase_codes, aperture)))
    block = jax.ShapeDtypeStruct((2 * plan.chunk + SUBS, LANES), jnp.float32)
    rows = pl.pallas_call(
        partial(chip_field_kernel, plan),
        out_shape=[block] * n_chips,
        in_specs=[smem] + [vmem] * (2 * n_row + 4),
        out_specs=[vmem] * n_chips,
        scratch_shapes=[pltpu.VMEM((2, (half + 1) * plan.chunk // plan.rows, LANES), jnp.float32)],
        compiler_params=pltpu.CompilerParams(vmem_limit_bytes=16 * 2**20),
        name="field",
    )(place, *others, *near_others, near[0], *own, near[1], near[2])
    order = CHIP_ORDER + (0,)
    received = [rows[0] if b == 0 else lax.ppermute(rows[b], "col", [(q, q ^ 2 * b) for q in range(n_col)]) for b in order]
    *made, opened = pl.pallas_call(
        partial(chip_transform_kernel, plan, order),
        out_shape=spectra_shapes(plan) + [jax.ShapeDtypeStruct((SUBS, LANES), jnp.float32)],
        in_specs=[vmem] * (n_chips + 3),
        out_specs=[vmem] * (plan.group + 1),
        compiler_params=pltpu.CompilerParams(vmem_limit_bytes=24 * 2**20),
        name="transform",
    )(*received, *ready_tables(plan, col_index.reshape(1), n_chips))
    return made, opened


def spectra_by_device(plan, phase_codes, aperture, tile_offsets):
    n_col, n_row = plan.n_col, plan.n_row
    row_index = lax.axis_index("row")
    col_index = lax.axis_index("col")
    me = col_index.astype(jnp.int32).reshape(1)
    smem = pl.BlockSpec(memory_space=pltpu.SMEM)
    vmem = pl.BlockSpec(memory_space=pltpu.VMEM)
    before = jnp.zeros((1, plan.pupil_dev // TILE_C), jnp.int32)
    for d, other in enumerate(along_rows(n_row, tile_offsets)):
        before = before + jnp.where(row_index > d, jnp.sum(other, axis=0, keepdims=True), 0)
    before = jnp.pad((before & (LEVELS - 1)).astype(jnp.float32), ((0, 0), (0, LANES - before.shape[1])))
    mine = jnp.arange(n_col, dtype=jnp.int32)[:, None] == col_index

    field_rows = plan.row_dev * 2 * plan.lane_parts * plan.n1_dev
    steps = plan.row_dev // TILE_R
    packed, opened = pl.pallas_call(
        partial(field_kernel, plan),
        out_shape=[
            jax.ShapeDtypeStruct((plan.n_groups, field_rows, LANES), jnp.float32),
            jax.ShapeDtypeStruct((SUBS, LANES), jnp.float32),
        ],
        grid=(steps,),
        in_specs=[
            smem,
            pl.BlockSpec((TILE_R, plan.pupil_dev), lambda t: (t, 0)),
            pl.BlockSpec((TILE_R, plan.pupil_dev), lambda t: (t, 0)),
        ],
        out_specs=[
            pl.BlockSpec((plan.n_groups, field_rows // steps, LANES), lambda t: (0, t, 0)),
            pl.BlockSpec((SUBS, LANES), lambda t: (0, 0)),
        ],
        name="field",
    )(tile_offsets, phase_codes, aperture)
    packed = packed.reshape(n_col, plan.chunk, LANES)
    received = lax.all_to_all(packed, "col", split_axis=0, concat_axis=0, tiled=True)

    info = jnp.concatenate([jnp.where(mine, before, 0.0), opened])
    for bit in range(n_col.bit_length() - 1):
        info = info + lax.ppermute(info, "col", [(q, q ^ 1 << bit) for q in range(n_col)])
    made = pl.pallas_call(
        partial(transform_kernel, plan),
        out_shape=spectra_shapes(plan),
        in_specs=[vmem] * 5,
        out_specs=[vmem] * plan.group,
        compiler_params=pltpu.CompilerParams(vmem_limit_bytes=24 * 2**20),
        name="transform",
    )(info, received, *ready_tables(plan, me, 1))
    return made, info[n_col:]


def per_device(phase_codes, aperture, tile_offsets):
    n_col = lax.axis_size("col")
    n_row = lax.axis_size("row")
    plan = Plan(*phase_codes.shape, n_col, n_row)
    by_chip = plan.n1_dev % SUBS == 0 and len(CHIP_ORDER) == n_col // 2 - 1
    spectra = spectra_by_chip if by_chip else spectra_by_device
    made, opened = spectra(plan, phase_codes, aperture, tile_offsets)
    chunks = [lax.ppermute(made[b], "col", [(q, q ^ b) for q in range(n_col)]) for b in ORDER] + [made[0]]
    opened, chunks[2] = lax.optimization_barrier((opened, chunks[2]))
    counts = [opened] + along_rows(n_row, opened)
    smem = pl.BlockSpec(memory_space=pltpu.SMEM)
    vmem = pl.BlockSpec(memory_space=pltpu.VMEM)
    tiles = plan.row_dev // SUBS
    out = pl.pallas_call(
        partial(merge_kernel, plan, 2 if by_chip else 1),
        out_shape=jax.ShapeDtypeStruct((2, tiles, plan.freq_tiles * SUBS, LANES), jnp.float32),
        in_specs=[smem] + [vmem] * (plan.group + n_row),
        out_specs=pl.BlockSpec(memory_space=pl.ANY),
        scratch_shapes=[
            pltpu.VMEM((plan.group, (plan.freq_tiles + 2 * plan.k1_tiles) * SUBS, LANES), jnp.float32),
            pltpu.SemaphoreType.DMA((plan.group,)),
        ],
        compiler_params=pltpu.CompilerParams(vmem_limit_bytes=24 * 2**20),
        name="merge",
    )(lax.axis_index("col").astype(jnp.int32).reshape(1), *chunks, *counts)
    out = out.reshape(2, tiles, plan.freq_tiles, SUBS, LANES).transpose(0, 1, 3, 2, 4)
    return out.reshape(2, plan.row_dev, plan.freq_tiles * LANES)


def solution(mesh):
    placed = (P("row", "col"), P("row", "col"), P("row", "col"))
    return jax.shard_map(
        per_device, mesh=mesh, in_specs=placed, out_specs=P(None, "row", "col"), check_vma=False
    )
```

```python
import math
from functools import partial

import jax
import jax.numpy as jnp
import ml_dtypes
import numpy as np
from jax import lax
from jax.experimental import pallas as pl
from jax.experimental.pallas import tpu as pltpu
from jax.sharding import PartitionSpec as P

LEVELS = 4096
TILE_R = 16
TILE_C = 512
LANES = 128
SUBS = 8
INNER = 256
PAD = 4
FINE = 16
CHIP_ORDER = (4, 1, 5, 3, 6, 2, 7)
ORDER = (6, 4, 2, 7, 5, 3, 1)
GROUP = 8


class Plan:
    def __init__(self, row_dev, pupil_dev, n_col, n_row):
        self.row_dev = row_dev
        self.pupil_dev = pupil_dev
        self.n_col = n_col
        self.n_row = n_row
        self.rows_all = row_dev * n_row
        self.group = min(GROUP, n_col)
        self.n_groups = n_col // self.group
        self.rows = row_dev // self.group
        self.n_pupil = pupil_dev * n_col
        self.n_pad = PAD * self.n_pupil
        self.n1 = self.n_pupil // INNER
        self.k1 = PAD * self.n1
        self.n1_dev = pupil_dev // INNER
        self.k2_group = INNER // self.n_groups
        self.k2_dev = INNER // n_col
        self.freq_tiles = PAD * pupil_dev // LANES
        self.k1_tiles = self.k1 // LANES
        self.lane_parts = INNER // LANES
        self.chunk = self.rows * 2 * self.lane_parts * self.n1_dev


def split_bf16(table):
    high = table.astype(ml_dtypes.bfloat16)
    low = (table - high.astype(np.float64)).astype(ml_dtypes.bfloat16)
    return np.stack([high, low])


def outer_tables(plan, blocks):
    k1 = plan.k1 // 2
    angle = np.arange(plan.n1)[:, None] * np.arange(k1)[None, :] % plan.k1
    angle = angle * (2.0 * np.pi / plan.k1)
    table = np.stack([np.cos(angle), np.sin(angle)]).reshape(2, blocks, plan.n1 // blocks // 2, 2, k1)
    return split_bf16(table.transpose(1, 3, 0, 2, 4))


def inner_tables(plan):
    angle = np.arange(INNER)[:, None] * np.arange(INNER // 2)[None, :] % INNER
    angle = angle * (2.0 * np.pi / INNER)
    table = np.concatenate([np.cos(angle), np.sin(angle)], axis=1)
    return split_bf16(table.reshape(plan.n_col, plan.k2_dev // 2, 2, INNER).transpose(0, 2, 1, 3))


def twist_tables(plan):
    made = []
    for cells in (np.arange(0, INNER, FINE), np.arange(FINE)):
        angle = cells[:, None] * np.arange(plan.k1)[None, :] * (2.0 * np.pi / plan.n_pad)
        made.extend([np.cos(angle), np.sin(angle)])
    return np.concatenate(made).astype(np.float32)


def unit_phase(code):
    quadrant = (code + LEVELS // 8) >> 10
    rest = (code - (quadrant << 10)).astype(jnp.float32) * (2.0 * math.pi / LEVELS)
    sq = rest * rest
    cos = 1.0 + sq * (-1.0 / 2 + sq * (1.0 / 24 + sq * (-1.0 / 720 + sq * (1.0 / 40320))))
    sin = rest * (1.0 + sq * (-1.0 / 6 + sq * (1.0 / 120 + sq * (-1.0 / 5040 + sq * (1.0 / 362880)))))
    swap = (quadrant & 1) == 1
    minus_cos = ((quadrant + 1) & 2) == 2
    minus_sin = (quadrant & 2) == 2
    return jnp.where(swap, sin, cos), jnp.where(swap, cos, sin), minus_cos, minus_sin


def field_kernel(plan, tiles_ref, codes_ref, mask_ref, out_ref, open_ref):
    step_id = pl.program_id(0)
    pistons = []
    for i in range(plan.pupil_dev // TILE_C):
        piston = jnp.int32(0)
        for k in range(plan.row_dev // TILE_R):
            piston = piston + jnp.where(step_id >= k, tiles_ref[k, i], 0)
        pistons.append(piston)
    stride = 2 * plan.lane_parts * plan.n1_dev
    total = jnp.zeros((SUBS, LANES), jnp.float32)
    for t in range(TILE_R // SUBS):
        for j in range(plan.pupil_dev // LANES):
            rows = slice(t * SUBS, (t + 1) * SUBS)
            lanes = slice(j * LANES, (j + 1) * LANES)
            code = (codes_ref[rows, lanes] + pistons[j * LANES // TILE_C]) & (LEVELS - 1)
            cos, sin, minus_cos, minus_sin = unit_phase(code)
            amplitude = mask_ref[rows, lanes].astype(jnp.float32)
            total = total + amplitude
            real = cos * jnp.where(minus_cos, -amplitude, amplitude)
            imag = sin * jnp.where(minus_sin, -amplitude, amplitude)
            for part, value in enumerate((real, imag)):
                start = (part * plan.lane_parts + j % plan.lane_parts) * plan.n1_dev + j // plan.lane_parts
                for g in range(plan.n_groups):
                    out_ref[g, pl.ds(t * SUBS * stride + start, SUBS, stride=stride), :] = value

    @pl.when(step_id == 0)
    def _():
        open_ref[...] = total

    @pl.when(step_id > 0)
    def _():
        open_ref[...] = open_ref[...] + total


def own_kernel(plan, me_ref, tiles_ref, codes_ref, mask_ref, real_ref, imag_ref, open_ref):
    half = plan.row_dev // 2
    first = pl.multiple_of(me_ref[0] * half, half)
    total = jnp.zeros((SUBS, LANES), jnp.int32)
    for t in range(plan.row_dev // SUBS):
        for j in range(plan.pupil_dev // LANES):
            total = total + mask_ref[t * SUBS : (t + 1) * SUBS, j * LANES : (j + 1) * LANES]
    open_ref[...] = total
    for i in range(plan.pupil_dev // TILE_C):
        lanes = slice(i * TILE_C, (i + 1) * TILE_C)
        piston = jnp.int32(0)
        for k in range(plan.row_dev // TILE_R):
            piston = piston + jnp.where(first >= k * TILE_R, tiles_ref[k, i], 0)
        for t in range(half // SUBS):
            rows = slice(t * SUBS, (t + 1) * SUBS)
            cos, sin, minus_cos, minus_sin = unit_phase((codes_ref[rows, lanes] + piston) & (LEVELS - 1))
            amplitude = mask_ref[pl.ds(pl.multiple_of(first + t * SUBS, SUBS), SUBS), lanes].astype(jnp.float32)
            real_ref[rows, lanes] = cos * jnp.where(minus_cos, -amplitude, amplitude)
            imag_ref[rows, lanes] = sin * jnp.where(minus_sin, -amplitude, amplitude)


def chip_field_kernel(plan, me_ref, *refs):
    n_other = plan.n_row - 1
    others, refs = (refs[:n_other], refs[n_other : 2 * n_other]), refs[2 * n_other :]
    near_tiles_ref, own_real_ref, own_imag_ref, open_ref, near_codes_ref, near_mask_ref = refs[:6]
    outs, made_ref = refs[6:-1], refs[-1]
    core, chip, row = me_ref[0], me_ref[1], me_ref[2]
    half = plan.row_dev // 2
    first = pl.multiple_of(core * half, half)
    total = open_ref[...]
    for t in range(plan.row_dev // SUBS):
        for j in range(plan.pupil_dev // LANES):
            total = total + near_mask_ref[t * SUBS : (t + 1) * SUBS, j * LANES : (j + 1) * LANES]
    total = total.astype(jnp.float32)
    stride = 2 * plan.lane_parts * plan.n1_dev
    for owner in range(2):
        before = jnp.zeros((1, plan.pupil_dev // TILE_C), jnp.int32)
        for d, other in enumerate(others[owner]):
            before = before + jnp.where(row > d, jnp.sum(other[...], axis=0, keepdims=True), 0)
        if owner == 1:
            for k in range(plan.row_dev // TILE_R):
                before = before + jnp.where(first >= k * TILE_R, near_tiles_ref[k : k + 1], 0)
        pistons = [jnp.broadcast_to(before[:, i : i + 1], (SUBS, LANES)) for i in range(before.shape[1])]
        turns = []
        if owner == 0:
            for piston in pistons:
                cos, sin, minus_cos, minus_sin = unit_phase(piston & (LEVELS - 1))
                turns.append((jnp.where(minus_cos, -cos, cos), jnp.where(minus_sin, -sin, sin)))
        for t in range(half // SUBS):
            rows = pl.ds(t * SUBS, SUBS) if owner == 0 else pl.ds(pl.multiple_of(first + t * SUBS, SUBS), SUBS)
            for j in range(plan.pupil_dev // LANES):
                lanes = slice(j * LANES, (j + 1) * LANES)
                column = j * LANES // TILE_C
                if owner == 0:
                    turn_cos, turn_sin = turns[column]
                    own_real, own_imag = own_real_ref[rows, lanes], own_imag_ref[rows, lanes]
                    real = own_real * turn_cos - own_imag * turn_sin
                    imag = own_real * turn_sin + own_imag * turn_cos
                else:
                    cos, sin, minus_cos, minus_sin = unit_phase((near_codes_ref[rows, lanes] + pistons[column]) & (LEVELS - 1))
                    amplitude = near_mask_ref[rows, lanes].astype(jnp.float32)
                    real = cos * jnp.where(minus_cos, -amplitude, amplitude)
                    imag = sin * jnp.where(minus_sin, -amplitude, amplitude)
                for part, value in enumerate((real, imag)):
                    start = (part * plan.lane_parts + j % plan.lane_parts) * plan.n1_dev + j // plan.lane_parts
                    made_ref[owner, pl.ds(t * SUBS * stride + start, SUBS, stride=stride), :] = value
    own_rows = lax.rem(chip, plan.group // 2)
    for b, out in enumerate(outs):
        source = pl.multiple_of((own_rows ^ b % (plan.group // 2)) * plan.chunk, plan.chunk)
        for i in range(plan.chunk // plan.n1_dev):
            for side in range(2):
                block = made_ref[side ^ core, pl.ds(pl.multiple_of(source + i * plan.n1_dev, plan.n1_dev), plan.n1_dev), :]
                out[(2 * i + side) * plan.n1_dev : (2 * i + side + 1) * plan.n1_dev, :] = block
        out[2 * plan.chunk :, :] = total


def tables_kernel(plan, blocks, me_ref, outer_ref, inner_ref, twist_ref, w1_ref, w2_ref, turn_ref):
    me = me_ref[0]
    w1, w2 = ([], []), ([], [])
    for s in range(2):
        rows = [outer_ref[s, (me >> 1) ^ b if blocks > 1 else 0].astype(jnp.float32) for b in range(blocks)]
        for p in range(2):
            cos, sin = (jnp.concatenate([both[p, i] for both in rows]) for i in range(2))
            both = jnp.concatenate([jnp.concatenate([cos, sin]), jnp.concatenate([-sin, cos])], axis=1)
            w1[p].append(both.astype(jnp.bfloat16))
        for p in range(2):
            parts = []
            for b in range(plan.group):
                both = inner_ref[s, me ^ b, p].astype(jnp.float32)
                parts.append(both)
                parts.append(jnp.concatenate([-both[:, INNER // 2 :], both[:, : INNER // 2]], axis=1))
            w2[p].append(jnp.concatenate(parts).astype(jnp.bfloat16))
    for p in range(2):
        w1_ref[p] = jnp.concatenate([w1[p][0], w1[p][0], w1[p][1]])
        w2_ref[p] = jnp.concatenate([w2[p][0], w2[p][1]])
    turn_ref[...] = twist_ref[...]


def chip_transform_kernel(plan, order, *refs):
    n_chips = plan.n_col // 2
    chunks = [refs[order.index(b)] for b in range(n_chips)]
    tables, outs, count_ref = refs[n_chips : n_chips + 3], refs[n_chips + 3 : -1], refs[-1]
    count = chunks[0][2 * plan.chunk :, :]
    for chunk in chunks[1:]:
        count = count + chunk[2 * plan.chunk :, :]
    count_ref[...] = count
    n1_chip = 2 * plan.n1_dev

    def part_of(r, part, p):
        pieces = []
        for lt in range(plan.lane_parts):
            at = ((r * 2 + part) * plan.lane_parts + lt) * n1_chip + p
            pieces.append(jnp.concatenate([chunk[pl.ds(at, n1_chip // 2, stride=2), :] for chunk in chunks]))
        return jnp.concatenate(pieces, axis=1)

    fields = []
    for p in range(2):
        fields.append([jnp.concatenate([part_of(r, 0, p), part_of(r, 1, p)]) for r in range(plan.rows)])
    transform_rows(plan, fields, tables, outs)


def transform_kernel(plan, info_ref, x_ref, *refs):
    chunk_row = plan.chunk // plan.rows
    n1_half, n1_dev = plan.n1 // 2, plan.n1_dev // 2
    info = info_ref[: plan.n_col]
    info = jnp.broadcast_to(info[:, None, :], (plan.n_col, n1_dev, LANES)).reshape(n1_half, LANES)
    tile = lax.broadcasted_iota(jnp.int32, info.shape, 0) % n1_dev * 2 * INNER // TILE_C
    own = lax.broadcasted_iota(jnp.int32, info.shape, 1) == tile
    before = jnp.sum(jnp.where(own, info, 0.0), axis=1, keepdims=True).astype(jnp.int32)
    turn_cos, turn_sin, minus_cos, minus_sin = unit_phase(before)
    turn_cos = jnp.where(minus_cos, -turn_cos, turn_cos)
    turn_sin = jnp.where(minus_sin, -turn_sin, turn_sin)

    def field_of(r, p):
        halves = []
        for part in range(2):
            pieces = []
            for lt in range(plan.lane_parts):
                at = r * chunk_row + (part * plan.lane_parts + lt) * plan.n1_dev + p
                cells = [x_ref[:, at + 2 * i : at + 2 * i + 1, :] for i in range(n1_dev)]
                pieces.append(jnp.concatenate(cells, axis=1).reshape(n1_half, LANES))
            halves.append(jnp.concatenate(pieces, axis=1))
        real, imag = halves
        return jnp.concatenate([real * turn_cos - imag * turn_sin, real * turn_sin + imag * turn_cos], axis=0)

    fields = [[field_of(r, p) for r in range(plan.rows)] for p in range(2)]
    transform_rows(plan, fields, refs[:3], refs[3:])


def transform_rows(plan, fields, tables, outs):
    w1_ref, w2_ref, turn_ref = tables
    ys = []
    for p in range(2):
        x = jnp.concatenate(fields[p], axis=1)
        xh = x.astype(jnp.bfloat16)
        xl = (x - xh.astype(jnp.float32)).astype(jnp.bfloat16)
        ys.append(
            lax.dot_general(
                jnp.concatenate([xh, xl, xh]), w1_ref[p], (((0,), (0,)), ((), ())), preferred_element_type=jnp.float32
            )
        )
    tc, ts = [], []
    count = INNER // FINE
    fine_cos, fine_sin = turn_ref[2 * count : 2 * count + FINE], turn_ref[2 * count + FINE :]
    for a in range(count):
        cos, sin = turn_ref[a : a + 1], turn_ref[count + a : count + a + 1]
        tc.append(cos * fine_cos - sin * fine_sin)
        ts.append(sin * fine_cos + cos * fine_sin)
    tc, ts = jnp.concatenate(tc), jnp.concatenate(ts)
    fs = ([], [])
    for r in range(plan.rows):
        even, odd = (y[r * INNER : (r + 1) * INNER] for y in ys)
        y = [even + odd, even - odd]
        yr, yi = (jnp.concatenate([one[:, i * plan.k1 // 2 : (i + 1) * plan.k1 // 2] for one in y], axis=1) for i in range(2))
        fr, fi = yr * tc + yi * ts, yi * tc - yr * ts
        for p in range(2):
            pair = [f[: INNER // 2] + f[INNER // 2 :] if p == 0 else f[: INNER // 2] - f[INNER // 2 :] for f in (fr, fi)]
            fs[p].append(jnp.concatenate(pair))
    half = plan.k2_dev // 2
    for p in range(2):
        f = jnp.concatenate(fs[p], axis=1)
        fh = f.astype(jnp.bfloat16)
        fl = (f - fh.astype(jnp.float32)).astype(jnp.bfloat16)
        size = plan.group * plan.k2_dev
        z = jnp.dot(w2_ref[p], fh, preferred_element_type=jnp.float32)
        z = z[:size] + z[size:] + jnp.dot(w2_ref[p, :size], fl, preferred_element_type=jnp.float32)
        for r in range(plan.rows):
            for b in range(plan.group):
                part = z[b * plan.k2_dev : (b + 1) * plan.k2_dev, r * plan.k1 : (r + 1) * plan.k1]
                outs[b][r, :, p * half : (p + 1) * half, :] = part.reshape(2, half, plan.k1)


def merge_kernel(plan, swap_bit, me_ref, *refs):
    chunks = [refs[(ORDER + (0,)).index(b)] for b in range(plan.group)]
    counts = refs[plan.group : plan.group + plan.n_row]
    out_ref, tile_ref, sems = refs[plan.group + plan.n_row :]
    total = counts[0][...]
    for other in counts[1:]:
        total = total + other[...]
    total = jnp.sum(jnp.sum(total, axis=0, keepdims=True), axis=1, keepdims=True)
    scale = jnp.sqrt(float(plan.rows_all) / total)
    inside = lax.rem(me_ref[0], plan.group)
    swapped = lax.rem(inside // swap_bit, 2) == 1
    half = plan.k2_dev // 2
    stride = 2 * plan.k1_tiles * SUBS
    copies = []
    for slot in range(plan.group):
        part = slot % 2
        base = [b for b in range(plan.group) if b & swap_bit == 0][slot // 2]
        for r in range(plan.rows):
            for p in range(2):
                for j in range(plan.k1_tiles):
                    rows, lanes = slice(p * half, (p + 1) * half), slice(j * LANES, (j + 1) * LANES)
                    a = chunks[base][r, part, rows, lanes] * scale
                    b = chunks[base + swap_bit][r, part, rows, lanes] * scale
                    at = (p * plan.k1_tiles + j) * SUBS + r
                    tile_ref[slot, pl.ds(at, half, stride=stride), :] = jnp.where(swapped, b, a)
                    tile_ref[slot, pl.ds(at + plan.rows, half, stride=stride), :] = jnp.where(swapped, a, b)
        source = inside ^ base
        tile = source // 2 if swap_bit == 1 else source % 2 * 2 + source // 4
        whole = tile_ref.at[slot, pl.ds(0, plan.freq_tiles * SUBS), :]
        copy = pltpu.make_async_copy(whole, out_ref.at[part, tile], sems.at[slot])
        copy.start()
        copies.append(copy)
    for copy in copies:
        copy.wait()


def along_rows(n_row, value):
    return [lax.ppermute(value, "row", [(i, (i + d) % n_row) for i in range(n_row)]) for d in range(1, n_row)]


def spectra_shapes(plan):
    return [jax.ShapeDtypeStruct((plan.rows, 2, plan.k2_dev, plan.k1), jnp.float32)] * plan.group


def ready_tables(plan, me, blocks):
    smem, vmem = pl.BlockSpec(memory_space=pltpu.SMEM), pl.BlockSpec(memory_space=pltpu.VMEM)
    return pl.pallas_call(
        partial(tables_kernel, plan, blocks),
        out_shape=[
            jax.ShapeDtypeStruct((2, 3 * plan.n1, plan.k1), jnp.bfloat16),
            jax.ShapeDtypeStruct((2, 2 * plan.group * plan.k2_dev, INNER), jnp.bfloat16),
            jax.ShapeDtypeStruct((2 * (INNER // FINE + FINE), plan.k1), jnp.float32),
        ],
        in_specs=[smem] + [vmem] * 3,
        out_specs=[vmem] * 3,
        compiler_params=pltpu.CompilerParams(vmem_limit_bytes=24 * 2**20),
        name="tables",
    )(me, outer_tables(plan, blocks), inner_tables(plan), twist_tables(plan))


def spectra_by_chip(plan, phase_codes, aperture, tile_offsets):
    n_col, n_row = plan.n_col, plan.n_row
    n_chips = n_col // 2
    half = plan.row_dev // 2
    row_index = lax.axis_index("row").astype(jnp.int32)
    col_index = lax.axis_index("col").astype(jnp.int32)
    smem, vmem = pl.BlockSpec(memory_space=pltpu.SMEM), pl.BlockSpec(memory_space=pltpu.VMEM)
    swap = [(q, q ^ 1) for q in range(n_col)]
    others = along_rows(n_row, tile_offsets)
    near_others = []
    for d in range(1, n_row):
        pairs = [(r * n_col + q, (r + d) % n_row * n_col + (q ^ 1)) for r in range(n_row) for q in range(n_col)]
        near_others.append(lax.ppermute(tile_offsets, ("row", "col"), pairs))
    near = [lax.ppermute(value, "col", swap) for value in (tile_offsets, phase_codes, aperture)]
    place = jnp.stack([col_index % 2, col_index // 2, row_index])
    own = pl.pallas_call(
        partial(own_kernel, plan),
        out_shape=[jax.ShapeDtypeStruct((half, plan.pupil_dev), jnp.float32)] * 2
        + [jax.ShapeDtypeStruct((SUBS, LANES), jnp.int32)],
        grid_spec=pltpu.PrefetchScalarGridSpec(
            num_scalar_prefetch=1,
            grid=(1,),
            in_specs=[
                smem,
                pl.BlockSpec((half, plan.pupil_dev), lambda i, p: (p[0], 0)),
                pl.BlockSpec((plan.row_dev, plan.pupil_dev), lambda i, p: (0, 0)),
            ],
            out_specs=[vmem] * 3,
        ),
        compiler_params=pltpu.CompilerParams(vmem_limit_bytes=16 * 2**20),
        name="own",
    )(place, *(pltpu.with_memory_space_constraint(a, pltpu.HBM) for a in (tile_offsets, phase_codes, aperture)))
    block = jax.ShapeDtypeStruct((2 * plan.chunk + SUBS, LANES), jnp.float32)
    rows = pl.pallas_call(
        partial(chip_field_kernel, plan),
        out_shape=[block] * n_chips,
        in_specs=[smem] + [vmem] * (2 * n_row + 4),
        out_specs=[vmem] * n_chips,
        scratch_shapes=[pltpu.VMEM((2, (half + 1) * plan.chunk // plan.rows, LANES), jnp.float32)],
        compiler_params=pltpu.CompilerParams(vmem_limit_bytes=16 * 2**20),
        name="field",
    )(place, *others, *near_others, near[0], *own, near[1], near[2])
    order = CHIP_ORDER + (0,)
    received = [rows[0] if b == 0 else lax.ppermute(rows[b], "col", [(q, q ^ 2 * b) for q in range(n_col)]) for b in order]
    *made, opened = pl.pallas_call(
        partial(chip_transform_kernel, plan, order),
        out_shape=spectra_shapes(plan) + [jax.ShapeDtypeStruct((SUBS, LANES), jnp.float32)],
        in_specs=[vmem] * (n_chips + 3),
        out_specs=[vmem] * (plan.group + 1),
        compiler_params=pltpu.CompilerParams(vmem_limit_bytes=24 * 2**20),
        name="transform",
    )(*received, *ready_tables(plan, col_index.reshape(1), n_chips))
    return made, opened


def spectra_by_device(plan, phase_codes, aperture, tile_offsets):
    n_col, n_row = plan.n_col, plan.n_row
    row_index = lax.axis_index("row")
    col_index = lax.axis_index("col")
    me = col_index.astype(jnp.int32).reshape(1)
    smem = pl.BlockSpec(memory_space=pltpu.SMEM)
    vmem = pl.BlockSpec(memory_space=pltpu.VMEM)
    before = jnp.zeros((1, plan.pupil_dev // TILE_C), jnp.int32)
    for d, other in enumerate(along_rows(n_row, tile_offsets)):
        before = before + jnp.where(row_index > d, jnp.sum(other, axis=0, keepdims=True), 0)
    before = jnp.pad((before & (LEVELS - 1)).astype(jnp.float32), ((0, 0), (0, LANES - before.shape[1])))
    mine = jnp.arange(n_col, dtype=jnp.int32)[:, None] == col_index

    field_rows = plan.row_dev * 2 * plan.lane_parts * plan.n1_dev
    steps = plan.row_dev // TILE_R
    packed, opened = pl.pallas_call(
        partial(field_kernel, plan),
        out_shape=[
            jax.ShapeDtypeStruct((plan.n_groups, field_rows, LANES), jnp.float32),
            jax.ShapeDtypeStruct((SUBS, LANES), jnp.float32),
        ],
        grid=(steps,),
        in_specs=[
            smem,
            pl.BlockSpec((TILE_R, plan.pupil_dev), lambda t: (t, 0)),
            pl.BlockSpec((TILE_R, plan.pupil_dev), lambda t: (t, 0)),
        ],
        out_specs=[
            pl.BlockSpec((plan.n_groups, field_rows // steps, LANES), lambda t: (0, t, 0)),
            pl.BlockSpec((SUBS, LANES), lambda t: (0, 0)),
        ],
        name="field",
    )(tile_offsets, phase_codes, aperture)
    packed = packed.reshape(n_col, plan.chunk, LANES)
    received = lax.all_to_all(packed, "col", split_axis=0, concat_axis=0, tiled=True)

    info = jnp.concatenate([jnp.where(mine, before, 0.0), opened])
    for bit in range(n_col.bit_length() - 1):
        info = info + lax.ppermute(info, "col", [(q, q ^ 1 << bit) for q in range(n_col)])
    made = pl.pallas_call(
        partial(transform_kernel, plan),
        out_shape=spectra_shapes(plan),
        in_specs=[vmem] * 5,
        out_specs=[vmem] * plan.group,
        compiler_params=pltpu.CompilerParams(vmem_limit_bytes=24 * 2**20),
        name="transform",
    )(info, received, *ready_tables(plan, me, 1))
    return made, info[n_col:]


def per_device(phase_codes, aperture, tile_offsets):
    n_col = lax.axis_size("col")
    n_row = lax.axis_size("row")
    plan = Plan(*phase_codes.shape, n_col, n_row)
    by_chip = plan.n1_dev % SUBS == 0 and len(CHIP_ORDER) == n_col // 2 - 1
    spectra = spectra_by_chip if by_chip else spectra_by_device
    made, opened = spectra(plan, phase_codes, aperture, tile_offsets)
    chunks = [lax.ppermute(made[b], "col", [(q, q ^ b) for q in range(n_col)]) for b in ORDER] + [made[0]]
    opened, chunks[2] = lax.optimization_barrier((opened, chunks[2]))
    counts = [opened] + along_rows(n_row, opened)
    smem = pl.BlockSpec(memory_space=pltpu.SMEM)
    vmem = pl.BlockSpec(memory_space=pltpu.VMEM)
    tiles = plan.row_dev // SUBS
    out = pl.pallas_call(
        partial(merge_kernel, plan, 2 if by_chip else 1),
        out_shape=jax.ShapeDtypeStruct((2, tiles, plan.freq_tiles * SUBS, LANES), jnp.float32),
        in_specs=[smem] + [vmem] * (plan.group + n_row),
        out_specs=pl.BlockSpec(memory_space=pl.ANY),
        scratch_shapes=[
            pltpu.VMEM((plan.group, (plan.freq_tiles + 2 * plan.k1_tiles) * SUBS, LANES), jnp.float32),
            pltpu.SemaphoreType.DMA((plan.group,)),
        ],
        compiler_params=pltpu.CompilerParams(vmem_limit_bytes=24 * 2**20),
        name="merge",
    )(lax.axis_index("col").astype(jnp.int32).reshape(1), *chunks, *counts)
    out = out.reshape(2, tiles, plan.freq_tiles, SUBS, LANES).transpose(0, 1, 3, 2, 4)
    return out.reshape(2, plan.row_dev, plan.freq_tiles * LANES)


def solution(mesh):
    placed = (P("row", "col"), P("row", "col"), P("row", "col"))
    return jax.shard_map(
        per_device, mesh=mesh, in_specs=placed, out_specs=P(None, "row", "col"), check_vma=False
    )
```

```python
import math
from functools import partial

import jax
import jax.numpy as jnp
import ml_dtypes
import numpy as np
from jax import lax
from jax.experimental import pallas as pl
from jax.experimental.pallas import tpu as pltpu
from jax.sharding import PartitionSpec as P

LEVELS = 4096
TILE_R = 16
TILE_C = 512
LANES = 128
SUBS = 8
INNER = 256
PAD = 4
FINE = 16
CHIP_ORDER = (4, 1, 6, 2, 5, 3, 7)
ORDER = (6, 4, 2, 7, 5, 3, 1)
GROUP = 8


class Plan:
    def __init__(self, row_dev, pupil_dev, n_col, n_row):
        self.row_dev = row_dev
        self.pupil_dev = pupil_dev
        self.n_col = n_col
        self.n_row = n_row
        self.rows_all = row_dev * n_row
        self.group = min(GROUP, n_col)
        self.n_groups = n_col // self.group
        self.rows = row_dev // self.group
        self.n_pupil = pupil_dev * n_col
        self.n_pad = PAD * self.n_pupil
        self.n1 = self.n_pupil // INNER
        self.k1 = PAD * self.n1
        self.n1_dev = pupil_dev // INNER
        self.k2_group = INNER // self.n_groups
        self.k2_dev = INNER // n_col
        self.freq_tiles = PAD * pupil_dev // LANES
        self.k1_tiles = self.k1 // LANES
        self.lane_parts = INNER // LANES
        self.chunk = self.rows * 2 * self.lane_parts * self.n1_dev


def split_bf16(table):
    high = table.astype(ml_dtypes.bfloat16)
    low = (table - high.astype(np.float64)).astype(ml_dtypes.bfloat16)
    return np.stack([high, low])


def outer_tables(plan, blocks):
    k1 = plan.k1 // 2
    angle = np.arange(plan.n1)[:, None] * np.arange(k1)[None, :] % plan.k1
    angle = angle * (2.0 * np.pi / plan.k1)
    table = np.stack([np.cos(angle), np.sin(angle)]).reshape(2, blocks, plan.n1 // blocks // 2, 2, k1)
    return split_bf16(table.transpose(1, 3, 0, 2, 4))


def inner_tables(plan):
    angle = np.arange(INNER)[:, None] * np.arange(INNER // 2)[None, :] % INNER
    angle = angle * (2.0 * np.pi / INNER)
    table = np.concatenate([np.cos(angle), np.sin(angle)], axis=1)
    return split_bf16(table.reshape(plan.n_col, plan.k2_dev // 2, 2, INNER).transpose(0, 2, 1, 3))


def twist_tables(plan):
    made = []
    for cells in (np.arange(0, INNER, FINE), np.arange(FINE)):
        angle = cells[:, None] * np.arange(plan.k1)[None, :] * (2.0 * np.pi / plan.n_pad)
        made.extend([np.cos(angle), np.sin(angle)])
    return np.concatenate(made).astype(np.float32)


def unit_phase(code):
    quadrant = (code + LEVELS // 8) >> 10
    rest = (code - (quadrant << 10)).astype(jnp.float32) * (2.0 * math.pi / LEVELS)
    sq = rest * rest
    cos = 1.0 + sq * (-1.0 / 2 + sq * (1.0 / 24 + sq * (-1.0 / 720 + sq * (1.0 / 40320))))
    sin = rest * (1.0 + sq * (-1.0 / 6 + sq * (1.0 / 120 + sq * (-1.0 / 5040 + sq * (1.0 / 362880)))))
    swap = (quadrant & 1) == 1
    minus_cos = ((quadrant + 1) & 2) == 2
    minus_sin = (quadrant & 2) == 2
    return jnp.where(swap, sin, cos), jnp.where(swap, cos, sin), minus_cos, minus_sin


def field_kernel(plan, tiles_ref, codes_ref, mask_ref, out_ref, open_ref):
    step_id = pl.program_id(0)
    pistons = []
    for i in range(plan.pupil_dev // TILE_C):
        piston = jnp.int32(0)
        for k in range(plan.row_dev // TILE_R):
            piston = piston + jnp.where(step_id >= k, tiles_ref[k, i], 0)
        pistons.append(piston)
    stride = 2 * plan.lane_parts * plan.n1_dev
    total = jnp.zeros((SUBS, LANES), jnp.float32)
    for t in range(TILE_R // SUBS):
        for j in range(plan.pupil_dev // LANES):
            rows = slice(t * SUBS, (t + 1) * SUBS)
            lanes = slice(j * LANES, (j + 1) * LANES)
            code = (codes_ref[rows, lanes] + pistons[j * LANES // TILE_C]) & (LEVELS - 1)
            cos, sin, minus_cos, minus_sin = unit_phase(code)
            amplitude = mask_ref[rows, lanes].astype(jnp.float32)
            total = total + amplitude
            real = cos * jnp.where(minus_cos, -amplitude, amplitude)
            imag = sin * jnp.where(minus_sin, -amplitude, amplitude)
            for part, value in enumerate((real, imag)):
                start = (part * plan.lane_parts + j % plan.lane_parts) * plan.n1_dev + j // plan.lane_parts
                for g in range(plan.n_groups):
                    out_ref[g, pl.ds(t * SUBS * stride + start, SUBS, stride=stride), :] = value

    @pl.when(step_id == 0)
    def _():
        open_ref[...] = total

    @pl.when(step_id > 0)
    def _():
        open_ref[...] = open_ref[...] + total


def own_kernel(plan, me_ref, tiles_ref, codes_ref, mask_ref, real_ref, imag_ref, open_ref):
    half = plan.row_dev // 2
    first = pl.multiple_of(me_ref[0] * half, half)
    total = jnp.zeros((SUBS, LANES), jnp.int32)
    for t in range(plan.row_dev // SUBS):
        for j in range(plan.pupil_dev // LANES):
            total = total + mask_ref[t * SUBS : (t + 1) * SUBS, j * LANES : (j + 1) * LANES]
    open_ref[...] = total
    for i in range(plan.pupil_dev // TILE_C):
        lanes = slice(i * TILE_C, (i + 1) * TILE_C)
        piston = jnp.int32(0)
        for k in range(plan.row_dev // TILE_R):
            piston = piston + jnp.where(first >= k * TILE_R, tiles_ref[k, i], 0)
        for t in range(half // SUBS):
            rows = slice(t * SUBS, (t + 1) * SUBS)
            cos, sin, minus_cos, minus_sin = unit_phase((codes_ref[rows, lanes] + piston) & (LEVELS - 1))
            amplitude = mask_ref[pl.ds(pl.multiple_of(first + t * SUBS, SUBS), SUBS), lanes].astype(jnp.float32)
            real_ref[rows, lanes] = cos * jnp.where(minus_cos, -amplitude, amplitude)
            imag_ref[rows, lanes] = sin * jnp.where(minus_sin, -amplitude, amplitude)


def chip_field_kernel(plan, me_ref, *refs):
    n_other = plan.n_row - 1
    others, refs = (refs[:n_other], refs[n_other : 2 * n_other]), refs[2 * n_other :]
    near_tiles_ref, own_real_ref, own_imag_ref, open_ref, near_codes_ref, near_mask_ref = refs[:6]
    outs, made_ref = refs[6:-1], refs[-1]
    core, chip, row = me_ref[0], me_ref[1], me_ref[2]
    half = plan.row_dev // 2
    first = pl.multiple_of(core * half, half)
    total = open_ref[...]
    for t in range(plan.row_dev // SUBS):
        for j in range(plan.pupil_dev // LANES):
            total = total + near_mask_ref[t * SUBS : (t + 1) * SUBS, j * LANES : (j + 1) * LANES]
    total = total.astype(jnp.float32)
    stride = 2 * plan.lane_parts * plan.n1_dev
    for owner in range(2):
        before = jnp.zeros((1, plan.pupil_dev // TILE_C), jnp.int32)
        for d, other in enumerate(others[owner]):
            before = before + jnp.where(row > d, jnp.sum(other[...], axis=0, keepdims=True), 0)
        if owner == 1:
            for k in range(plan.row_dev // TILE_R):
                before = before + jnp.where(first >= k * TILE_R, near_tiles_ref[k : k + 1], 0)
        pistons = [jnp.broadcast_to(before[:, i : i + 1], (SUBS, LANES)) for i in range(before.shape[1])]
        turns = []
        if owner == 0:
            for piston in pistons:
                cos, sin, minus_cos, minus_sin = unit_phase(piston & (LEVELS - 1))
                turns.append((jnp.where(minus_cos, -cos, cos), jnp.where(minus_sin, -sin, sin)))
        for t in range(half // SUBS):
            rows = pl.ds(t * SUBS, SUBS) if owner == 0 else pl.ds(pl.multiple_of(first + t * SUBS, SUBS), SUBS)
            for j in range(plan.pupil_dev // LANES):
                lanes = slice(j * LANES, (j + 1) * LANES)
                column = j * LANES // TILE_C
                if owner == 0:
                    turn_cos, turn_sin = turns[column]
                    own_real, own_imag = own_real_ref[rows, lanes], own_imag_ref[rows, lanes]
                    real = own_real * turn_cos - own_imag * turn_sin
                    imag = own_real * turn_sin + own_imag * turn_cos
                else:
                    cos, sin, minus_cos, minus_sin = unit_phase((near_codes_ref[rows, lanes] + pistons[column]) & (LEVELS - 1))
                    amplitude = near_mask_ref[rows, lanes].astype(jnp.float32)
                    real = cos * jnp.where(minus_cos, -amplitude, amplitude)
                    imag = sin * jnp.where(minus_sin, -amplitude, amplitude)
                for part, value in enumerate((real, imag)):
                    start = (part * plan.lane_parts + j % plan.lane_parts) * plan.n1_dev + j // plan.lane_parts
                    made_ref[owner, pl.ds(t * SUBS * stride + start, SUBS, stride=stride), :] = value
    own_rows = lax.rem(chip, plan.group // 2)
    for b, out in enumerate(outs):
        source = pl.multiple_of((own_rows ^ b % (plan.group // 2)) * plan.chunk, plan.chunk)
        for i in range(plan.chunk // plan.n1_dev):
            for side in range(2):
                block = made_ref[side ^ core, pl.ds(pl.multiple_of(source + i * plan.n1_dev, plan.n1_dev), plan.n1_dev), :]
                out[(2 * i + side) * plan.n1_dev : (2 * i + side + 1) * plan.n1_dev, :] = block
        out[2 * plan.chunk :, :] = total


def tables_kernel(plan, blocks, me_ref, outer_ref, inner_ref, twist_ref, w1_ref, w2_ref, turn_ref):
    me = me_ref[0]
    w1, w2 = ([], []), ([], [])
    for s in range(2):
        rows = [outer_ref[s, (me >> 1) ^ b if blocks > 1 else 0].astype(jnp.float32) for b in range(blocks)]
        for p in range(2):
            cos, sin = (jnp.concatenate([both[p, i] for both in rows]) for i in range(2))
            both = jnp.concatenate([jnp.concatenate([cos, sin]), jnp.concatenate([-sin, cos])], axis=1)
            w1[p].append(both.astype(jnp.bfloat16))
        for p in range(2):
            parts = []
            for b in range(plan.group):
                both = inner_ref[s, me ^ b, p].astype(jnp.float32)
                parts.append(both)
                parts.append(jnp.concatenate([-both[:, INNER // 2 :], both[:, : INNER // 2]], axis=1))
            w2[p].append(jnp.concatenate(parts).astype(jnp.bfloat16))
    for p in range(2):
        w1_ref[p] = jnp.concatenate([w1[p][0], w1[p][0], w1[p][1]])
        w2_ref[p] = jnp.concatenate([w2[p][0], w2[p][1]])
    turn_ref[...] = twist_ref[...]


def chip_transform_kernel(plan, order, *refs):
    n_chips = plan.n_col // 2
    chunks = [refs[order.index(b)] for b in range(n_chips)]
    tables, outs, count_ref = refs[n_chips : n_chips + 3], refs[n_chips + 3 : -1], refs[-1]
    count = chunks[0][2 * plan.chunk :, :]
    for chunk in chunks[1:]:
        count = count + chunk[2 * plan.chunk :, :]
    count_ref[...] = count
    n1_chip = 2 * plan.n1_dev

    def part_of(r, part, p):
        pieces = []
        for lt in range(plan.lane_parts):
            at = ((r * 2 + part) * plan.lane_parts + lt) * n1_chip + p
            pieces.append(jnp.concatenate([chunk[pl.ds(at, n1_chip // 2, stride=2), :] for chunk in chunks]))
        return jnp.concatenate(pieces, axis=1)

    fields = []
    for p in range(2):
        fields.append([jnp.concatenate([part_of(r, 0, p), part_of(r, 1, p)]) for r in range(plan.rows)])
    transform_rows(plan, fields, tables, outs)


def transform_kernel(plan, info_ref, x_ref, *refs):
    chunk_row = plan.chunk // plan.rows
    n1_half, n1_dev = plan.n1 // 2, plan.n1_dev // 2
    info = info_ref[: plan.n_col]
    info = jnp.broadcast_to(info[:, None, :], (plan.n_col, n1_dev, LANES)).reshape(n1_half, LANES)
    tile = lax.broadcasted_iota(jnp.int32, info.shape, 0) % n1_dev * 2 * INNER // TILE_C
    own = lax.broadcasted_iota(jnp.int32, info.shape, 1) == tile
    before = jnp.sum(jnp.where(own, info, 0.0), axis=1, keepdims=True).astype(jnp.int32)
    turn_cos, turn_sin, minus_cos, minus_sin = unit_phase(before)
    turn_cos = jnp.where(minus_cos, -turn_cos, turn_cos)
    turn_sin = jnp.where(minus_sin, -turn_sin, turn_sin)

    def field_of(r, p):
        halves = []
        for part in range(2):
            pieces = []
            for lt in range(plan.lane_parts):
                at = r * chunk_row + (part * plan.lane_parts + lt) * plan.n1_dev + p
                cells = [x_ref[:, at + 2 * i : at + 2 * i + 1, :] for i in range(n1_dev)]
                pieces.append(jnp.concatenate(cells, axis=1).reshape(n1_half, LANES))
            halves.append(jnp.concatenate(pieces, axis=1))
        real, imag = halves
        return jnp.concatenate([real * turn_cos - imag * turn_sin, real * turn_sin + imag * turn_cos], axis=0)

    fields = [[field_of(r, p) for r in range(plan.rows)] for p in range(2)]
    transform_rows(plan, fields, refs[:3], refs[3:])


def transform_rows(plan, fields, tables, outs):
    w1_ref, w2_ref, turn_ref = tables
    ys = []
    for p in range(2):
        x = jnp.concatenate(fields[p], axis=1)
        xh = x.astype(jnp.bfloat16)
        xl = (x - xh.astype(jnp.float32)).astype(jnp.bfloat16)
        ys.append(
            lax.dot_general(
                jnp.concatenate([xh, xl, xh]), w1_ref[p], (((0,), (0,)), ((), ())), preferred_element_type=jnp.float32
            )
        )
    tc, ts = [], []
    count = INNER // FINE
    fine_cos, fine_sin = turn_ref[2 * count : 2 * count + FINE], turn_ref[2 * count + FINE :]
    for a in range(count):
        cos, sin = turn_ref[a : a + 1], turn_ref[count + a : count + a + 1]
        tc.append(cos * fine_cos - sin * fine_sin)
        ts.append(sin * fine_cos + cos * fine_sin)
    tc, ts = jnp.concatenate(tc), jnp.concatenate(ts)
    fs = ([], [])
    for r in range(plan.rows):
        even, odd = (y[r * INNER : (r + 1) * INNER] for y in ys)
        y = [even + odd, even - odd]
        yr, yi = (jnp.concatenate([one[:, i * plan.k1 // 2 : (i + 1) * plan.k1 // 2] for one in y], axis=1) for i in range(2))
        fr, fi = yr * tc + yi * ts, yi * tc - yr * ts
        for p in range(2):
            pair = [f[: INNER // 2] + f[INNER // 2 :] if p == 0 else f[: INNER // 2] - f[INNER // 2 :] for f in (fr, fi)]
            fs[p].append(jnp.concatenate(pair))
    half = plan.k2_dev // 2
    for p in range(2):
        f = jnp.concatenate(fs[p], axis=1)
        fh = f.astype(jnp.bfloat16)
        fl = (f - fh.astype(jnp.float32)).astype(jnp.bfloat16)
        size = plan.group * plan.k2_dev
        z = jnp.dot(w2_ref[p], fh, preferred_element_type=jnp.float32)
        z = z[:size] + z[size:] + jnp.dot(w2_ref[p, :size], fl, preferred_element_type=jnp.float32)
        for r in range(plan.rows):
            for b in range(plan.group):
                part = z[b * plan.k2_dev : (b + 1) * plan.k2_dev, r * plan.k1 : (r + 1) * plan.k1]
                outs[b][r, :, p * half : (p + 1) * half, :] = part.reshape(2, half, plan.k1)


def merge_kernel(plan, swap_bit, me_ref, *refs):
    chunks = [refs[(ORDER + (0,)).index(b)] for b in range(plan.group)]
    counts = refs[plan.group : plan.group + plan.n_row]
    out_ref, tile_ref, sems = refs[plan.group + plan.n_row :]
    total = counts[0][...]
    for other in counts[1:]:
        total = total + other[...]
    total = jnp.sum(jnp.sum(total, axis=0, keepdims=True), axis=1, keepdims=True)
    scale = jnp.sqrt(float(plan.rows_all) / total)
    inside = lax.rem(me_ref[0], plan.group)
    swapped = lax.rem(inside // swap_bit, 2) == 1
    half = plan.k2_dev // 2
    stride = 2 * plan.k1_tiles * SUBS
    copies = []
    for slot in range(plan.group):
        part = slot % 2
        base = [b for b in range(plan.group) if b & swap_bit == 0][slot // 2]
        for r in range(plan.rows):
            for p in range(2):
                for j in range(plan.k1_tiles):
                    rows, lanes = slice(p * half, (p + 1) * half), slice(j * LANES, (j + 1) * LANES)
                    a = chunks[base][r, part, rows, lanes] * scale
                    b = chunks[base + swap_bit][r, part, rows, lanes] * scale
                    at = (p * plan.k1_tiles + j) * SUBS + r
                    tile_ref[slot, pl.ds(at, half, stride=stride), :] = jnp.where(swapped, b, a)
                    tile_ref[slot, pl.ds(at + plan.rows, half, stride=stride), :] = jnp.where(swapped, a, b)
        source = inside ^ base
        tile = source // 2 if swap_bit == 1 else source % 2 * 2 + source // 4
        whole = tile_ref.at[slot, pl.ds(0, plan.freq_tiles * SUBS), :]
        copy = pltpu.make_async_copy(whole, out_ref.at[part, tile], sems.at[slot])
        copy.start()
        copies.append(copy)
    for copy in copies:
        copy.wait()


def along_rows(n_row, value):
    return [lax.ppermute(value, "row", [(i, (i + d) % n_row) for i in range(n_row)]) for d in range(1, n_row)]


def spectra_shapes(plan):
    return [jax.ShapeDtypeStruct((plan.rows, 2, plan.k2_dev, plan.k1), jnp.float32)] * plan.group


def ready_tables(plan, me, blocks):
    smem, vmem = pl.BlockSpec(memory_space=pltpu.SMEM), pl.BlockSpec(memory_space=pltpu.VMEM)
    return pl.pallas_call(
        partial(tables_kernel, plan, blocks),
        out_shape=[
            jax.ShapeDtypeStruct((2, 3 * plan.n1, plan.k1), jnp.bfloat16),
            jax.ShapeDtypeStruct((2, 2 * plan.group * plan.k2_dev, INNER), jnp.bfloat16),
            jax.ShapeDtypeStruct((2 * (INNER // FINE + FINE), plan.k1), jnp.float32),
        ],
        in_specs=[smem] + [vmem] * 3,
        out_specs=[vmem] * 3,
        compiler_params=pltpu.CompilerParams(vmem_limit_bytes=24 * 2**20),
        name="tables",
    )(me, outer_tables(plan, blocks), inner_tables(plan), twist_tables(plan))


def spectra_by_chip(plan, phase_codes, aperture, tile_offsets):
    n_col, n_row = plan.n_col, plan.n_row
    n_chips = n_col // 2
    half = plan.row_dev // 2
    row_index = lax.axis_index("row").astype(jnp.int32)
    col_index = lax.axis_index("col").astype(jnp.int32)
    smem, vmem = pl.BlockSpec(memory_space=pltpu.SMEM), pl.BlockSpec(memory_space=pltpu.VMEM)
    swap = [(q, q ^ 1) for q in range(n_col)]
    others = along_rows(n_row, tile_offsets)
    near_others = []
    for d in range(1, n_row):
        pairs = [(r * n_col + q, (r + d) % n_row * n_col + (q ^ 1)) for r in range(n_row) for q in range(n_col)]
        near_others.append(lax.ppermute(tile_offsets, ("row", "col"), pairs))
    near = [lax.ppermute(value, "col", swap) for value in (tile_offsets, phase_codes, aperture)]
    place = jnp.stack([col_index % 2, col_index // 2, row_index])
    own = pl.pallas_call(
        partial(own_kernel, plan),
        out_shape=[jax.ShapeDtypeStruct((half, plan.pupil_dev), jnp.float32)] * 2
        + [jax.ShapeDtypeStruct((SUBS, LANES), jnp.int32)],
        grid_spec=pltpu.PrefetchScalarGridSpec(
            num_scalar_prefetch=1,
            grid=(1,),
            in_specs=[
                smem,
                pl.BlockSpec((half, plan.pupil_dev), lambda i, p: (p[0], 0)),
                pl.BlockSpec((plan.row_dev, plan.pupil_dev), lambda i, p: (0, 0)),
            ],
            out_specs=[vmem] * 3,
        ),
        compiler_params=pltpu.CompilerParams(vmem_limit_bytes=16 * 2**20),
        name="own",
    )(place, *(pltpu.with_memory_space_constraint(a, pltpu.HBM) for a in (tile_offsets, phase_codes, aperture)))
    block = jax.ShapeDtypeStruct((2 * plan.chunk + SUBS, LANES), jnp.float32)
    rows = pl.pallas_call(
        partial(chip_field_kernel, plan),
        out_shape=[block] * n_chips,
        in_specs=[smem] + [vmem] * (2 * n_row + 4),
        out_specs=[vmem] * n_chips,
        scratch_shapes=[pltpu.VMEM((2, (half + 1) * plan.chunk // plan.rows, LANES), jnp.float32)],
        compiler_params=pltpu.CompilerParams(vmem_limit_bytes=16 * 2**20),
        name="field",
    )(place, *others, *near_others, near[0], *own, near[1], near[2])
    order = CHIP_ORDER + (0,)
    received = [rows[0] if b == 0 else lax.ppermute(rows[b], "col", [(q, q ^ 2 * b) for q in range(n_col)]) for b in order]
    *made, opened = pl.pallas_call(
        partial(chip_transform_kernel, plan, order),
        out_shape=spectra_shapes(plan) + [jax.ShapeDtypeStruct((SUBS, LANES), jnp.float32)],
        in_specs=[vmem] * (n_chips + 3),
        out_specs=[vmem] * (plan.group + 1),
        compiler_params=pltpu.CompilerParams(vmem_limit_bytes=24 * 2**20),
        name="transform",
    )(*received, *ready_tables(plan, col_index.reshape(1), n_chips))
    return made, opened


def spectra_by_device(plan, phase_codes, aperture, tile_offsets):
    n_col, n_row = plan.n_col, plan.n_row
    row_index = lax.axis_index("row")
    col_index = lax.axis_index("col")
    me = col_index.astype(jnp.int32).reshape(1)
    smem = pl.BlockSpec(memory_space=pltpu.SMEM)
    vmem = pl.BlockSpec(memory_space=pltpu.VMEM)
    before = jnp.zeros((1, plan.pupil_dev // TILE_C), jnp.int32)
    for d, other in enumerate(along_rows(n_row, tile_offsets)):
        before = before + jnp.where(row_index > d, jnp.sum(other, axis=0, keepdims=True), 0)
    before = jnp.pad((before & (LEVELS - 1)).astype(jnp.float32), ((0, 0), (0, LANES - before.shape[1])))
    mine = jnp.arange(n_col, dtype=jnp.int32)[:, None] == col_index

    field_rows = plan.row_dev * 2 * plan.lane_parts * plan.n1_dev
    steps = plan.row_dev // TILE_R
    packed, opened = pl.pallas_call(
        partial(field_kernel, plan),
        out_shape=[
            jax.ShapeDtypeStruct((plan.n_groups, field_rows, LANES), jnp.float32),
            jax.ShapeDtypeStruct((SUBS, LANES), jnp.float32),
        ],
        grid=(steps,),
        in_specs=[
            smem,
            pl.BlockSpec((TILE_R, plan.pupil_dev), lambda t: (t, 0)),
            pl.BlockSpec((TILE_R, plan.pupil_dev), lambda t: (t, 0)),
        ],
        out_specs=[
            pl.BlockSpec((plan.n_groups, field_rows // steps, LANES), lambda t: (0, t, 0)),
            pl.BlockSpec((SUBS, LANES), lambda t: (0, 0)),
        ],
        name="field",
    )(tile_offsets, phase_codes, aperture)
    packed = packed.reshape(n_col, plan.chunk, LANES)
    received = lax.all_to_all(packed, "col", split_axis=0, concat_axis=0, tiled=True)

    info = jnp.concatenate([jnp.where(mine, before, 0.0), opened])
    for bit in range(n_col.bit_length() - 1):
        info = info + lax.ppermute(info, "col", [(q, q ^ 1 << bit) for q in range(n_col)])
    made = pl.pallas_call(
        partial(transform_kernel, plan),
        out_shape=spectra_shapes(plan),
        in_specs=[vmem] * 5,
        out_specs=[vmem] * plan.group,
        compiler_params=pltpu.CompilerParams(vmem_limit_bytes=24 * 2**20),
        name="transform",
    )(info, received, *ready_tables(plan, me, 1))
    return made, info[n_col:]


def per_device(phase_codes, aperture, tile_offsets):
    n_col = lax.axis_size("col")
    n_row = lax.axis_size("row")
    plan = Plan(*phase_codes.shape, n_col, n_row)
    by_chip = plan.n1_dev % SUBS == 0 and len(CHIP_ORDER) == n_col // 2 - 1
    spectra = spectra_by_chip if by_chip else spectra_by_device
    made, opened = spectra(plan, phase_codes, aperture, tile_offsets)
    chunks = [lax.ppermute(made[b], "col", [(q, q ^ b) for q in range(n_col)]) for b in ORDER] + [made[0]]
    opened, chunks[2] = lax.optimization_barrier((opened, chunks[2]))
    counts = [opened] + along_rows(n_row, opened)
    smem = pl.BlockSpec(memory_space=pltpu.SMEM)
    vmem = pl.BlockSpec(memory_space=pltpu.VMEM)
    tiles = plan.row_dev // SUBS
    out = pl.pallas_call(
        partial(merge_kernel, plan, 2 if by_chip else 1),
        out_shape=jax.ShapeDtypeStruct((2, tiles, plan.freq_tiles * SUBS, LANES), jnp.float32),
        in_specs=[smem] + [vmem] * (plan.group + n_row),
        out_specs=pl.BlockSpec(memory_space=pl.ANY),
        scratch_shapes=[
            pltpu.VMEM((plan.group, (plan.freq_tiles + 2 * plan.k1_tiles) * SUBS, LANES), jnp.float32),
            pltpu.SemaphoreType.DMA((plan.group,)),
        ],
        compiler_params=pltpu.CompilerParams(vmem_limit_bytes=24 * 2**20),
        name="merge",
    )(lax.axis_index("col").astype(jnp.int32).reshape(1), *chunks, *counts)
    out = out.reshape(2, tiles, plan.freq_tiles, SUBS, LANES).transpose(0, 1, 3, 2, 4)
    return out.reshape(2, plan.row_dev, plan.freq_tiles * LANES)


def solution(mesh):
    placed = (P("row", "col"), P("row", "col"), P("row", "col"))
    return jax.shard_map(
        per_device, mesh=mesh, in_specs=placed, out_specs=P(None, "row", "col"), check_vma=False
    )
```
